256 devices in a mesh: task: 8 (over y_lo, x), row: 32 (over z, y_hi, core).
Axes of the slice: x: 4, y: 4 (y_hi: 2, y_lo: 2; y = y_hi * 2 + y_lo), z: 8, core: 2. Of those that a mesh axis runs over, the one named last changes fastest.
Arguments:
- delta: bfloat16 [8, 14336, 4096], P('task', 'row'), may hold values from -23 to 23
- sketch: bfloat16 [8, 4096, 320], P('task'), may hold values from -6 to 6
- base: bfloat16 [14336, 4096], P('row', 'task'), may hold values from -6 to 6
Outputs:
- merged: bfloat16 [14336, 4096], P('row', 'task')
The draws below stay inside these ranges and needn't reach their ends.
All inputs are finite; a program needn't handle non-finite values.
Results may differ from the reference program's by a relative error of at most 0.0052.
Values may be sent and summed in bfloat16 or wider, within the bound.
A program may use at most 128 MiB of HBM per device.

```python
import math
import jax
import jax.numpy as jnp
from jax import lax

D = 4096
FF = 14336
R = 320
ITERS = 2
TASKS = 8


def draw_delta(key, part):
    key = jax.random.fold_in(key, 3)
    scale_key = jax.random.fold_in(key, 11)
    value_key = jax.random.fold_in(key, 12)
    log_scale = jax.random.uniform(scale_key, (1, FF, 1), jnp.float32, 0.0, math.log(1000.0))
    row_scale = jnp.exp(log_scale) * 0.003717
    values = jnp.clip(jax.random.normal(value_key, (TASKS, FF, D), jnp.float32), -6.0, 6.0)
    return (values * row_scale).astype(jnp.bfloat16)


def level_of(stream_key, dims, split, least, top_value):
    gain = 1.0
    for dim, parts in split:
        draws = jax.random.uniform(jax.random.fold_in(jax.random.fold_in(stream_key, 6), dim), (parts,), jnp.float32, least / len(split), top_value / len(split))
        gain = gain * jnp.repeat(jnp.exp(draws), dims[dim] // parts).reshape((-1,) + (1,) * (len(dims) - 1 - dim))
    return gain


def bell_draw(rng, shape, deviation, bound, split=(), held_as=jnp.bfloat16):
    values = jax.random.normal(rng, shape, jnp.float32) * deviation
    if len(split) > 0:
        values = level_of(rng, shape, split, -0.22, 0.18) * values
    return jnp.clip(values, min=-bound, max=bound).astype(held_as)


def setup_inputs(seed: int = 0) -> dict:
    keys = jax.random.split(jax.random.key(seed), 4)
    delta = draw_delta(jax.random.fold_in(keys[3], 71), 0)
    sketch = bell_draw(keys[1], (TASKS, D, R), 1.0, 6.0, ((0, 8),))
    base = bell_draw(keys[2], (FF, D), 0.5, 6.0, ((0, 32), (1, 8)))
    return {"delta": delta, "sketch": sketch, "base": base}


highest = lax.Precision.HIGHEST

def task_basis(pair):
    delta_one, sketch_one = pair
    sketched = jnp.dot(delta_one.astype(jnp.float32), sketch_one.astype(jnp.float32), preferred_element_type=jnp.float32)
    square = jnp.dot(sketched.T, sketched, precision=highest)
    factor = jnp.linalg.cholesky(square)
    return lax.linalg.triangular_solve(factor, sketched, left_side=False, lower=True, transpose_a=True)

def project_task(pair):
    weight_one, delta_one = pair
    return jnp.dot(weight_one.T.astype(jnp.float32), delta_one.astype(jnp.float32), preferred_element_type=jnp.float32).astype(jnp.bfloat16)

def reference(delta, sketch, base):
    bases = lax.map(task_basis, (delta, sketch))
    stacked = jnp.transpose(bases, (1, 0, 2)).reshape(FF, TASKS * R) / math.sqrt(TASKS)
    for sweep in range(ITERS):
        joint_gram = jnp.dot(stacked.T, stacked, precision=highest)
        stacked = 1.5 * stacked - 0.5 * jnp.dot(stacked, joint_gram, precision=highest)
    weights = stacked.astype(jnp.bfloat16)
    task_weights = jnp.transpose(weights.reshape(FF, TASKS, R), (1, 0, 2))
    coefficients = lax.map(project_task, (task_weights, delta)).reshape(TASKS * R, D)
    update = jnp.dot(weights.astype(jnp.float32), coefficients.astype(jnp.float32), preferred_element_type=jnp.float32)
    return (base.astype(jnp.float32) + update).astype(jnp.bfloat16)
```

```python
import functools
import math

import jax
import jax.numpy as jnp
from jax import lax
from jax.experimental import pallas as pl
from jax.experimental.pallas import tpu as pltpu
from jax.sharding import PartitionSpec as P

highest = lax.Precision.HIGHEST
MESH = pl.DeviceIdType.MESH
VMEM = pl.BlockSpec(memory_space=pltpu.VMEM)
DMA = pltpu.SemaphoreType.DMA
f32 = jnp.float32
bf16 = jnp.bfloat16
CB = 64


def params(cid):
    return pltpu.CompilerParams(
        collective_id=cid, has_side_effects=True, vmem_limit_bytes=48 * 1024 * 1024
    )


def place(chips):
    row = lax.axis_index("row")
    chip, core = row // 2, row % 2
    return chip, core, chip * 2 + (1 - core)


def around(me, step, count):
    return (me + step) % count


def remote(src, dst, ssem, rsem, where):
    return pltpu.make_async_remote_copy(
        src_ref=src, dst_ref=dst, send_sem=ssem, recv_sem=rsem,
        device_id=where, device_id_type=MESH,
    )


def loop(lo, hi, body):
    def step(i, carry):
        body(i)
        return carry

    lax.fori_loop(lo, hi, step, 0)


def greet(chips, tasks, rows):
    barrier = pltpu.get_barrier_semaphore()
    total = 0
    if rows:
        chip, core, sib = place(chips)
        pl.semaphore_signal(barrier, inc=1, device_id={"row": sib}, device_id_type=MESH)
        loop(1, chips, lambda d: pl.semaphore_signal(
            barrier, inc=1, device_id={"row": around(chip, d, chips) * 2 + core},
            device_id_type=MESH))
        total += chips
    if tasks:
        me = lax.axis_index("task")
        loop(1, tasks, lambda d: pl.semaphore_signal(
            barrier, inc=1, device_id={"task": around(me, d, tasks)}, device_id_type=MESH))
        total += tasks - 1
    pl.semaphore_wait(barrier, total)


def to_chips(chips, src, dst, ssem, rsem):
    chip, core, _ = place(chips)

    def body(d):
        other = around(chip, d, chips)
        remote(src(other), dst(d), ssem.at[d], rsem.at[d], {"row": other * 2 + core}).start()

    loop(1, chips, body)


def wait_chips(chips, src, dst, ssem, rsem):
    chip, core, _ = place(chips)

    def body(d):
        other = around(chip, d, chips)
        copy = remote(src(other), dst(d), ssem.at[d], rsem.at[d], {"row": other * 2 + core})
        copy.wait()

    loop(1, chips, body)


def reduce_rows(chips, mine, sib_buf, half, slots, sems, parts_half, part_slot):
    raise NotImplementedError


def square_kernel(chips, in_ref, out_ref, sib_buf, half, slots, core_s, core_r, a_s, a_r, b_s, b_r):
    chip, core, sib = place(chips)
    greet(chips, 0, True)
    swap = remote(in_ref.at[1 - core], sib_buf, core_s.at[0], core_r.at[0], {"row": sib})
    swap.start()
    swap.wait()
    half[...] = in_ref[core] + sib_buf[...]
    src, dst = (lambda c: half.at[c]), (lambda d: slots.at[d])
    to_chips(chips, src, dst, a_s, a_r)
    wait_chips(chips, src, dst, a_s, a_r)
    total = lax.fori_loop(1, chips, lambda d, t: t + slots[d], half[chip])
    out_ref[core, chip] = total
    src = lambda c: out_ref.at[core, chip]
    to_chips(chips, src, lambda d: out_ref.at[core, chip], b_s, b_r)
    wait_chips(chips, src, lambda d: out_ref.at[core, around(chip, chips - d, chips)], b_s, b_r)
    swap = remote(out_ref.at[core], out_ref.at[core], core_s.at[1], core_r.at[1], {"row": sib})
    swap.start()
    swap.wait_send()
    remote(out_ref.at[core], out_ref.at[1 - core], core_s.at[1], core_r.at[1], {"row": sib}).wait_recv()


def all_reduce_square(packed, chips):
    rows, lanes = packed.shape
    part = rows // (2 * chips)
    shaped = packed.reshape(2, chips, part, lanes)
    out = pl.pallas_call(
        functools.partial(square_kernel, chips),
        out_shape=jax.ShapeDtypeStruct(shaped.shape, f32),
        in_specs=[VMEM],
        out_specs=VMEM,
        scratch_shapes=[pltpu.VMEM((chips, part, lanes), f32)] * 3
        + [DMA((2,)), DMA((2,))] + [DMA((chips,))] * 4,
        compiler_params=params(1),
        name="square_sum",
    )(shaped)
    return out.reshape(rows, lanes)


def dot_nt(a, b):
    return lax.dot_general(a, b, (((1,), (1,)), ((), ())), precision=highest,
                           preferred_element_type=f32)


def dot_nn(a, b):
    return lax.dot_general(a, b, (((1,), (0,)), ((), ())), precision=highest,
                           preferred_element_type=f32)


def chol_kernel(blocks, a_ref, z_ref, cols, fac, inv):
    row_id = lax.broadcasted_iota(jnp.int32, (CB, 2 * CB), 0)
    lane_id = lax.broadcasted_iota(jnp.int32, (CB, 2 * CB), 1)
    eye = (lane_id == row_id + CB).astype(f32)
    inv[...] = jnp.zeros_like(inv)
    cols[...] = a_ref[...]
    for k in range(blocks):
        at = k * CB
        both = jnp.concatenate([cols[k, at:at + CB, :], jnp.zeros((CB, CB), f32)], axis=1) + eye
        for j in range(CB):
            scale = lax.rsqrt(both[j:j + 1, j:j + 1])
            line = both[j:j + 1, :] * scale
            down = both[:, j:j + 1] * scale
            below = both - down * line
            both = jnp.where(row_id > j, below, jnp.where(row_id == j, line, both))
        zkk = both[:, CB:]
        if k + 1 < blocks:
            panel = dot_nt(cols[k, at + CB:, :], zkk)
            fac[k, at + CB:, :] = panel
            for j in range(k + 1, blocks):
                off = (j - k - 1) * CB
                cols[j, j * CB:, :] = cols[j, j * CB:, :] - dot_nt(
                    panel[off:, :], panel[off:off + CB, :])
        for c in range(k):
            acc = dot_nn(fac[c, at:at + CB, :], inv[c, c * CB:(c + 1) * CB, :])
            for m in range(c + 1, k):
                acc = acc + dot_nn(fac[m, at:at + CB, :], inv[c, m * CB:(m + 1) * CB, :])
            inv[c, at:at + CB, :] = -dot_nn(zkk, acc)
        inv[k, at:at + CB, :] = zkk
    z_ref[...] = inv[...]


def inverse_factor(square):
    n = square.shape[0]
    blocks = n // CB
    a = jnp.transpose(square.reshape(n, blocks, CB), (1, 0, 2))
    z = pl.pallas_call(
        functools.partial(chol_kernel, blocks),
        out_shape=jax.ShapeDtypeStruct((blocks, n, CB), f32),
        in_specs=[VMEM],
        out_specs=VMEM,
        scratch_shapes=[pltpu.VMEM((blocks, n, CB), f32)] * 3,
        compiler_params=pltpu.CompilerParams(vmem_limit_bytes=32 * 1024 * 1024),
        name="inverse_factor",
    )(a)
    return jnp.transpose(z, (1, 0, 2)).reshape(n, n)


def start_tasks(tasks, src, dst, ssem, rsem):
    me = lax.axis_index("task")

    def body(d):
        other = around(me, d, tasks)
        remote(src(other), dst(me), ssem.at[d], rsem.at[d], {"task": other}).start()

    loop(1, tasks, body)


def wait_tasks(tasks, src, dst, ssem, rsem):
    me = lax.axis_index("task")

    def body(d):
        other = around(me, d, tasks)
        back = around(me, tasks - d, tasks)
        remote(src(other), dst(back), ssem.at[d], rsem.at[d], {"task": other}).wait()

    loop(1, tasks, body)


def gather_kernel(tasks, in_ref, out_ref, a_s, a_r):
    me = lax.axis_index("task")
    greet(0, tasks, False)
    src, dst = (lambda c: in_ref), (lambda c: out_ref.at[c])
    start_tasks(tasks, src, dst, a_s, a_r)
    out_ref[me] = in_ref[...]
    wait_tasks(tasks, src, dst, a_s, a_r)


def gather_tasks(block, tasks):
    return pl.pallas_call(
        functools.partial(gather_kernel, tasks),
        out_shape=jax.ShapeDtypeStruct((tasks,) + block.shape, block.dtype),
        in_specs=[VMEM],
        out_specs=VMEM,
        scratch_shapes=[DMA((tasks,)), DMA((tasks,))],
        compiler_params=params(2),
        name="basis_gather",
    )(block)


def poly_kernel(chips, tasks, in_ref, out_ref, sib_buf, half, slots, column, slab, slab2, slab3,
                core_s, core_r, a_s, a_r, b_s, b_r, c_s, c_r, t1_s, t1_r, t2_s, t2_r, t3_s, t3_r):
    chip, core, sib = place(chips)
    me = lax.axis_index("task")
    greet(chips, tasks, True)
    swap = remote(in_ref.at[:, 1 - core], sib_buf, core_s.at[0], core_r.at[0], {"row": sib})
    swap.start()
    swap.wait()
    half[...] = (in_ref[:, core].astype(f32) + sib_buf[...].astype(f32)).astype(bf16)
    src, dst = (lambda c: half.at[c]), (lambda d: slots.at[d])
    to_chips(chips, src, dst, a_s, a_r)
    wait_chips(chips, src, dst, a_s, a_r)
    gram = lax.fori_loop(
        1, chips, lambda d, t: t + slots[d].astype(f32), half[chip].astype(f32))
    mine = gram.astype(bf16)
    slab[me] = mine
    column[chip, core] = mine
    tsrc = lambda c: slab.at[me]
    start_tasks(tasks, tsrc, lambda c: slab.at[c], t1_s, t1_r)
    rsrc = lambda c: column.at[chip, core]
    to_chips(chips, rsrc, lambda d: column.at[chip, core], b_s, b_r)
    wait_chips(chips, rsrc, lambda d: column.at[around(chip, chips - d, chips), core], b_s, b_r)
    swap = remote(column.at[:, core], column.at[:, core], core_s.at[1], core_r.at[1], {"row": sib})
    swap.start()
    wait_tasks(tasks, tsrc, lambda c: slab.at[c], t1_s, t1_r)
    swap.wait_send()
    remote(column.at[:, core], column.at[:, 1 - core], core_s.at[1], core_r.at[1],
           {"row": sib}).wait_recv()

    depth, width = slab.shape[1:]
    per = width // depth // 2

    def times(left):
        def body(s, total):
            block = column[pl.ds(s * per, per)].reshape(width, width)
            return total + jnp.dot(left[s], block, preferred_element_type=f32)
        return lax.fori_loop(0, tasks, body, jnp.zeros((depth, width), f32))

    two = times(slab)
    slab2[me] = two.astype(bf16)
    src2 = lambda c: slab2.at[me]
    start_tasks(tasks, src2, lambda c: slab2.at[c], t2_s, t2_r)
    wait_tasks(tasks, src2, lambda c: slab2.at[c], t2_s, t2_r)
    three = times(slab2)
    slab3[me] = three.astype(bf16)
    src3 = lambda c: slab3.at[me]
    start_tasks(tasks, src3, lambda c: slab3.at[c], t3_s, t3_r)
    wait_tasks(tasks, src3, lambda c: slab3.at[c], t3_s, t3_r)
    four = times(slab3)
    poly = -2.4375 * gram + 1.6875 * two - 0.5625 * three + 0.0625 * four
    out_ref[chip, core] = poly.astype(bf16)
    osrc = lambda c: out_ref.at[chip, core]
    to_chips(chips, osrc, lambda d: out_ref.at[chip, core], c_s, c_r)
    wait_chips(chips, osrc, lambda d: out_ref.at[around(chip, chips - d, chips), core], c_s, c_r)
    swap = remote(out_ref.at[:, core], out_ref.at[:, core], core_s.at[2], core_r.at[2], {"row": sib})
    swap.start()
    swap.wait_send()
    remote(out_ref.at[:, core], out_ref.at[:, 1 - core], core_s.at[2], core_r.at[2],
           {"row": sib}).wait_recv()


def polynomial(partial, chips, tasks):
    total, width = partial.shape
    depth = total // (2 * chips)
    shaped = partial.reshape(chips, 2, depth, width)
    out = pl.pallas_call(
        functools.partial(poly_kernel, chips, tasks),
        out_shape=jax.ShapeDtypeStruct(shaped.shape, bf16),
        in_specs=[VMEM],
        out_specs=VMEM,
        scratch_shapes=[pltpu.VMEM((chips, depth, width), bf16)] * 3
        + [pltpu.VMEM(shaped.shape, bf16)]
        + [pltpu.VMEM((tasks, depth, width), bf16)] * 3
        + [DMA((3,)), DMA((3,))] + [DMA((chips,))] * 6 + [DMA((tasks,))] * 6,
        compiler_params=params(3),
        name="polynomial",
    )(shaped)
    return out.reshape(total, width)


def coef_kernel(chips, tasks, in_ref, w_ref, out_ref, wall_ref, sib_buf, half, slots, mine, block,
                core_s, core_r, a_s, a_r, b_s, b_r, t1_s, t1_r, w_s, w_r):
    chip, core, sib = place(chips)
    me = lax.axis_index("task")
    greet(chips, tasks, True)
    swap = remote(in_ref.at[:, :, 1 - core], sib_buf, core_s.at[0], core_r.at[0], {"row": sib})
    swap.start()
    wsrc, wdst = (lambda c: w_ref), (lambda c: wall_ref.at[c])
    start_tasks(tasks, wsrc, wdst, w_s, w_r)
    wall_ref[me] = w_ref[...]
    swap.wait()

    def add(u):
        half[u] = (in_ref[u, :, core].astype(f32) + sib_buf[u].astype(f32)).astype(bf16)

    loop(0, tasks, add)
    src, dst = (lambda c: half.at[:, c]), (lambda d: slots.at[d])
    to_chips(chips, src, dst, a_s, a_r)
    wait_chips(chips, src, dst, a_s, a_r)
    total = lax.fori_loop(
        1, chips, lambda d, t: t + slots[d].astype(f32), half[:, chip].astype(f32))
    mine[...] = total.astype(bf16)
    block[me] = mine[me]
    tsrc, tdst = (lambda c: mine.at[c]), (lambda c: block.at[c])
    start_tasks(tasks, tsrc, tdst, t1_s, t1_r)
    wait_tasks(tasks, tsrc, tdst, t1_s, t1_r)
    out_ref[:, chip, core] = block[...]
    rsrc = lambda c: block
    to_chips(chips, rsrc, lambda d: out_ref.at[:, chip, core], b_s, b_r)
    wait_chips(chips, rsrc, lambda d: out_ref.at[:, around(chip, chips - d, chips), core], b_s, b_r)
    swap = remote(out_ref.at[:, :, core], out_ref.at[:, :, core], core_s.at[1], core_r.at[1],
                  {"row": sib})
    swap.start()
    wait_tasks(tasks, wsrc, wdst, w_s, w_r)
    swap.wait_send()
    remote(out_ref.at[:, :, core], out_ref.at[:, :, 1 - core], core_s.at[1], core_r.at[1],
           {"row": sib}).wait_recv()


def coefficients_and_weights(partial, weights, chips, tasks):
    features, width = partial.shape
    depth = features // (tasks * chips * 2)
    shaped = partial.reshape(tasks, chips, 2, depth, width)
    out, wall = pl.pallas_call(
        functools.partial(coef_kernel, chips, tasks),
        out_shape=(jax.ShapeDtypeStruct(shaped.shape, bf16),
                   jax.ShapeDtypeStruct((tasks,) + weights.shape, bf16)),
        in_specs=[VMEM, VMEM],
        out_specs=(VMEM, VMEM),
        scratch_shapes=[pltpu.VMEM((tasks, chips, depth, width), bf16)] * 2
        + [pltpu.VMEM((chips, tasks, depth, width), bf16)]
        + [pltpu.VMEM((tasks, depth, width), bf16)] * 2
        + [DMA((2,)), DMA((2,))] + [DMA((chips,))] * 4 + [DMA((tasks,))] * 4,
        compiler_params=params(4),
        name="coefficients",
    )(shaped, weights)
    return out.reshape(tasks, features // tasks, width), wall


def pack(square):
    n = square.shape[0]
    parts = []
    for at in range(0, n, 128):
        piece = square[at:, at:min(at + 128, n)]
        parts.append(jnp.pad(piece, ((0, 0), (0, 128 - piece.shape[1]))))
    return jnp.concatenate(parts, axis=0)


def unpack(packed, n):
    parts, top = [], 0
    for at in range(0, n, 128):
        piece = packed[top:top + n - at, :min(128, n - at)]
        parts.append(jnp.pad(piece, ((at, 0), (0, 0))))
        top += n - at
    return jnp.concatenate(parts, axis=1)


def local(delta, sketch, base):
    tasks = lax.axis_size("task")
    chips = lax.axis_size("row") // 2
    delta_rows, task_sketch = delta[0], sketch[0]
    width = task_sketch.shape[1]
    sketched = jnp.dot(delta_rows, task_sketch, preferred_element_type=f32)
    packed = pack(jnp.dot(sketched.T, sketched, precision=highest))
    unit = 16 * chips
    packed = jnp.pad(packed, ((0, -packed.shape[0] % unit), (0, 0)))
    square = unpack(all_reduce_square(packed, chips), width)
    inverse = inverse_factor(square)
    own = lax.dot_general(
        sketched, inverse, (((1,), (1,)), ((), ())), precision=highest
    ) * (1.0 / math.sqrt(tasks))
    stack = gather_tasks(own.astype(bf16), tasks)
    gram = lax.dot_general(
        stack, own.astype(bf16), (((1,), (0,)), ((), ())), preferred_element_type=f32
    ).reshape(tasks * width, width).astype(bf16)
    poly = polynomial(gram, chips, tasks).reshape(tasks, width, width)
    weights = (
        2.25 * own
        + lax.dot_general(stack, poly, (((0, 2), (0, 1)), ((), ())), preferred_element_type=f32)
    ).astype(bf16)
    partial = lax.dot_general(
        delta_rows, weights, (((0,), (0,)), ((), ())), preferred_element_type=f32
    ).astype(bf16)
    coefs, stack2 = coefficients_and_weights(partial, weights, chips, tasks)
    update = lax.dot_general(
        stack2, coefs, (((0, 2), (0, 2)), ((), ())), preferred_element_type=f32
    )
    return (base.astype(f32) + update).astype(bf16)


def solution(mesh):
    return jax.shard_map(
        local,
        mesh=mesh,
        in_specs=(P("task", "row", None), P("task", None, None), P("row", "task")),
        out_specs=P("row", "task"),
        check_vma=False,
    )
```

```python
import functools
import math

import jax
import jax.numpy as jnp
from jax import lax
from jax.experimental import pallas as pl
from jax.experimental.pallas import tpu as pltpu
from jax.sharding import PartitionSpec as P

highest = lax.Precision.HIGHEST
MESH = pl.DeviceIdType.MESH
VMEM = pl.BlockSpec(memory_space=pltpu.VMEM)
DMA = pltpu.SemaphoreType.DMA
f32 = jnp.float32
bf16 = jnp.bfloat16
CB = 64


def params(cid):
    return pltpu.CompilerParams(
        collective_id=cid, has_side_effects=True, vmem_limit_bytes=48 * 1024 * 1024
    )


def place(chips):
    row = lax.axis_index("row")
    chip, core = row // 2, row % 2
    return chip, core, chip * 2 + (1 - core)


def around(me, step, count):
    return (me + step) % count


def remote(src, dst, ssem, rsem, where):
    return pltpu.make_async_remote_copy(
        src_ref=src, dst_ref=dst, send_sem=ssem, recv_sem=rsem,
        device_id=where, device_id_type=MESH,
    )


def loop(lo, hi, body):
    def step(i, carry):
        body(i)
        return carry

    lax.fori_loop(lo, hi, step, 0)


def greet(chips, tasks, rows):
    barrier = pltpu.get_barrier_semaphore()
    total = 0
    if rows:
        chip, core, sib = place(chips)
        pl.semaphore_signal(barrier, inc=1, device_id={"row": sib}, device_id_type=MESH)
        loop(1, chips, lambda d: pl.semaphore_signal(
            barrier, inc=1, device_id={"row": around(chip, d, chips) * 2 + core},
            device_id_type=MESH))
        total += chips
    if tasks:
        me = lax.axis_index("task")
        loop(1, tasks, lambda d: pl.semaphore_signal(
            barrier, inc=1, device_id={"task": around(me, d, tasks)}, device_id_type=MESH))
        total += tasks - 1
    pl.semaphore_wait(barrier, total)


def to_chips(chips, src, dst, ssem, rsem):
    chip, core, _ = place(chips)

    def body(d):
        other = around(chip, d, chips)
        remote(src(other), dst(d), ssem.at[d], rsem.at[d], {"row": other * 2 + core}).start()

    loop(1, chips, body)


def wait_chips(chips, src, dst, ssem, rsem):
    chip, core, _ = place(chips)

    def body(d):
        other = around(chip, d, chips)
        copy = remote(src(other), dst(d), ssem.at[d], rsem.at[d], {"row": other * 2 + core})
        copy.wait()

    loop(1, chips, body)


def tiles(depth, width):
    full = width // 128
    top = -(-depth // 32) * 16 if width % 128 else 0
    return full, top, full * depth + top


def pack_rows(value):
    depth, width = value.shape
    full, top, _ = tiles(depth, width)
    parts = [value[:, i * 128:(i + 1) * 128] for i in range(full)]
    if top:
        tail = value[:, full * 128:]
        low = jnp.concatenate(
            [tail[top:], jnp.zeros((2 * top - depth, 64), value.dtype)], axis=0
        ) if 2 * top > depth else tail[top:]
        parts.append(jnp.concatenate([tail[:top], low], axis=1))
    return jnp.concatenate(parts, axis=0)


def unpack_rows(packed, depth, width):
    full, top, _ = tiles(depth, width)
    parts = [packed[i * depth:(i + 1) * depth] for i in range(full)]
    if top:
        tail = packed[full * depth:full * depth + top]
        parts.append(jnp.concatenate([tail[:, :64], tail[:depth - top, 64:]], axis=0))
    return jnp.concatenate(parts, axis=1)


def unpack_to(dst, packed, depth, width):
    full, top, _ = tiles(depth, width)
    for i in range(full):
        dst[:, i * 128:(i + 1) * 128] = packed[i * depth:(i + 1) * depth]
    if top:
        tail = packed[full * depth:full * depth + top]
        dst[:top, full * 128:] = tail[:, :64]
        dst[top:, full * 128:] = tail[:depth - top, 64:]


def greet_near(chips, tasks):
    barrier = pltpu.get_barrier_semaphore()
    chip, core, sib = place(chips)
    zs, z, y = chips // 2, chip // 2, chip % 2
    for there in (sib, line(zs, z + 1, y, core), line(zs, z - 1, y, core), line(zs, z, 1 - y, core)):
        pl.semaphore_signal(barrier, inc=1, device_id={"row": there}, device_id_type=MESH)
    me = lax.axis_index("task")
    loop(1, tasks, lambda d: pl.semaphore_signal(
        barrier, inc=1, device_id={"task": around(me, d, tasks)}, device_id_type=MESH))
    pl.semaphore_wait(barrier, 4 + tasks - 1)


def line(zs, z, y, core):
    return (((z + zs) % zs) * 2 + y) * 2 + core


def streams(zs, y):
    far, near = zs // 2, zs // 2 - 1
    return [(2, 1, near, 1 - y), (3, -1, far, 1 - y), (0, 1, far, y), (1, -1, near, y)]


def ring_reduce(chips, half, slots, other, other_in, ssem, rsem, ysem):
    chip, core, _ = place(chips)
    zs, z, y = chips // 2, chip // 2, chip % 2
    hops = zs // 2
    sent = []

    def term(zz, yy):
        return half[((zz + zs) % zs) * 2 + yy]

    def send(stream, step, src):
        k, way = stream[0], stream[1]
        n = k * hops + step - 1
        copy = remote(src, slots.at[n], ssem.at[n], rsem.at[n], {"row": line(zs, z + way, y, core)})
        copy.start()
        sent.append(copy)

    def arrive(stream, step):
        n = stream[0] * hops + step - 1
        remote(slots.at[n], slots.at[n], ssem.at[n], rsem.at[n], {"row": line(zs, z, y, core)}).wait_recv()
        return n

    for st in streams(zs, y):
        if st[2]:
            dest = ((z + st[1] * st[2] + zs) % zs) * 2 + st[3]
            send(st, 1, half.at[dest])
    for step in range(1, hops + 1):
        for st in streams(zs, y):
            if step <= st[2]:
                n = arrive(st, step)
                if step < st[2]:
                    dest = z + st[1] * (st[2] - step)
                    slots[n] = (slots[n].astype(f32) + term(dest, st[3]).astype(f32)).astype(bf16)
                    send(st, step + 1, slots.at[n])

    def final(plane, pair):
        total = term(z, plane).astype(f32)
        for k, n in pair:
            if n:
                total = total + slots[k * hops + n - 1].astype(f32)
        return total

    other[...] = final(1 - y, [(2, hops - 1), (3, hops)]).astype(bf16)
    swap = remote(other, other_in, ysem.at[0], ysem.at[1], {"row": line(zs, z, 1 - y, core)})
    swap.start()
    own = final(y, [(0, hops), (1, hops - 1)])
    swap.wait()
    for copy in sent:
        copy.wait_send()
    return own + other_in[...].astype(f32)


def ring_gather(chips, at, ssem, rsem, ysem):
    chip, core, _ = place(chips)
    zs, z, y = chips // 2, chip // 2, chip % 2
    hops = zs // 2
    sent = []

    def spot(zz, yy):
        return at(((zz + zs) % zs) * 2 + yy)

    def send(stream, step):
        k, way, _, yy = stream
        n = k * hops + step - 1
        block = spot(z - way * (step - 1), yy)
        copy = remote(block, block, ssem.at[n], rsem.at[n], {"row": line(zs, z + way, y, core)})
        copy.start()
        sent.append(copy)

    def arrive(stream, step):
        k, way, _, yy = stream
        n = k * hops + step - 1
        block = spot(z - way * step, yy)
        remote(block, block, ssem.at[n], rsem.at[n], {"row": line(zs, z, y, core)}).wait_recv()

    across = {"row": line(zs, z, 1 - y, core)}
    swap = remote(spot(z, y), spot(z, y), ysem.at[2], ysem.at[3], across)
    swap.start()
    order = streams(zs, y)[2:] + streams(zs, y)[:2]
    for st in order[:2]:
        if st[2]:
            send(st, 1)
    remote(spot(z, 1 - y), spot(z, 1 - y), ysem.at[2], ysem.at[3], across).wait_recv()
    for st in order[2:]:
        if st[2]:
            send(st, 1)
    for step in range(1, hops + 1):
        for st in order:
            if step <= st[2]:
                arrive(st, step)
                if step < st[2]:
                    send(st, step + 1)
    swap.wait_send()
    for copy in sent:
        copy.wait_send()


def square_kernel(chips, in_ref, out_ref, sib_buf, half, slots, core_s, core_r, a_s, a_r, b_s, b_r):
    chip, core, sib = place(chips)
    greet(chips, 0, True)
    swap = remote(in_ref.at[1 - core], sib_buf, core_s.at[0], core_r.at[0], {"row": sib})
    swap.start()
    swap.wait()
    half[...] = in_ref[core] + sib_buf[...]
    src, dst = (lambda c: half.at[c]), (lambda d: slots.at[d])
    to_chips(chips, src, dst, a_s, a_r)
    wait_chips(chips, src, dst, a_s, a_r)
    total = lax.fori_loop(1, chips, lambda d, t: t + slots[d], half[chip])
    out_ref[core, chip] = total
    src = lambda c: out_ref.at[core, chip]
    to_chips(chips, src, lambda d: out_ref.at[core, chip], b_s, b_r)
    wait_chips(chips, src, lambda d: out_ref.at[core, around(chip, chips - d, chips)], b_s, b_r)
    swap = remote(out_ref.at[core], out_ref.at[core], core_s.at[1], core_r.at[1], {"row": sib})
    swap.start()
    swap.wait_send()
    remote(out_ref.at[core], out_ref.at[1 - core], core_s.at[1], core_r.at[1], {"row": sib}).wait_recv()


def all_reduce_square(packed, chips):
    rows, lanes = packed.shape
    part = rows // (2 * chips)
    shaped = packed.reshape(2, chips, part, lanes)
    out = pl.pallas_call(
        functools.partial(square_kernel, chips),
        out_shape=jax.ShapeDtypeStruct(shaped.shape, f32),
        in_specs=[VMEM],
        out_specs=VMEM,
        scratch_shapes=[pltpu.VMEM((chips, part, lanes), f32)] * 3
        + [DMA((2,)), DMA((2,))] + [DMA((chips,))] * 4,
        compiler_params=params(1),
        name="square_sum",
    )(shaped)
    return out.reshape(rows, lanes)


def dot_nt(a, b):
    return lax.dot_general(a, b, (((1,), (1,)), ((), ())), precision=highest,
                           preferred_element_type=f32)


def dot_nn(a, b):
    return lax.dot_general(a, b, (((1,), (0,)), ((), ())), precision=highest,
                           preferred_element_type=f32)


def chol_kernel(blocks, a_ref, z_ref, cols, fac, inv):
    row_id = lax.broadcasted_iota(jnp.int32, (CB, 2 * CB), 0)
    lane_id = lax.broadcasted_iota(jnp.int32, (CB, 2 * CB), 1)
    eye = (lane_id == row_id + CB).astype(f32)
    inv[...] = jnp.zeros_like(inv)
    cols[...] = a_ref[...]
    for k in range(blocks):
        at = k * CB
        both = jnp.concatenate([cols[k, at:at + CB, :], jnp.zeros((CB, CB), f32)], axis=1) + eye
        for j in range(CB):
            scale = lax.rsqrt(both[j:j + 1, j:j + 1])
            line = both[j:j + 1, :] * scale
            down = both[:, j:j + 1] * scale
            below = both - down * line
            both = jnp.where(row_id > j, below, jnp.where(row_id == j, line, both))
        zkk = both[:, CB:]
        if k + 1 < blocks:
            panel = dot_nt(cols[k, at + CB:, :], zkk)
            fac[k, at + CB:, :] = panel
            for j in range(k + 1, blocks):
                off = (j - k - 1) * CB
                cols[j, j * CB:, :] = cols[j, j * CB:, :] - dot_nt(
                    panel[off:, :], panel[off:off + CB, :])
        for c in range(k):
            acc = dot_nn(fac[c, at:at + CB, :], inv[c, c * CB:(c + 1) * CB, :])
            for m in range(c + 1, k):
                acc = acc + dot_nn(fac[m, at:at + CB, :], inv[c, m * CB:(m + 1) * CB, :])
            inv[c, at:at + CB, :] = -dot_nn(zkk, acc)
        inv[k, at:at + CB, :] = zkk
    z_ref[...] = inv[...]


def inverse_factor(square):
    n = square.shape[0]
    blocks = n // CB
    a = jnp.transpose(square.reshape(n, blocks, CB), (1, 0, 2))
    z = pl.pallas_call(
        functools.partial(chol_kernel, blocks),
        out_shape=jax.ShapeDtypeStruct((blocks, n, CB), f32),
        in_specs=[VMEM],
        out_specs=VMEM,
        scratch_shapes=[pltpu.VMEM((blocks, n, CB), f32)] * 3,
        compiler_params=pltpu.CompilerParams(vmem_limit_bytes=32 * 1024 * 1024),
        name="inverse_factor",
    )(a)
    return jnp.transpose(z, (1, 0, 2)).reshape(n, n)


def start_tasks(tasks, src, dst, ssem, rsem):
    me = lax.axis_index("task")

    def body(d):
        other = around(me, d, tasks)
        remote(src(other), dst(me), ssem.at[d], rsem.at[d], {"task": other}).start()

    loop(1, tasks, body)


def wait_tasks(tasks, src, dst, ssem, rsem):
    me = lax.axis_index("task")

    def body(d):
        other = around(me, d, tasks)
        back = around(me, tasks - d, tasks)
        remote(src(other), dst(back), ssem.at[d], rsem.at[d], {"task": other}).wait()

    loop(1, tasks, body)


def spread(tasks, at, ssem, rsem):
    me = lax.axis_index("task")
    xs = tasks // 2
    x, y = me % xs, me // xs
    sent = []

    def send(n, block, to):
        copy = remote(block, block, ssem.at[n], rsem.at[n], {"task": to})
        copy.start()
        sent.append(copy)

    def arrive(n, block):
        remote(block, block, ssem.at[n], rsem.at[n], {"task": me}).wait_recv()

    def name(xx, yy):
        return yy * xs + xx % xs

    own = at(me)
    send(0, own, name(x, 1 - y))
    for d in range(1, xs):
        send(d, own, name(x + d, y))
    yield
    twin = at(name(x, 1 - y))
    arrive(0, twin)
    yield name(x, 1 - y)
    across = [d for d in range(1, xs) if d == xs // 2]
    along = [d for d in range(1, xs) if d != xs // 2]
    for d in along:
        send(xs + d, twin, name(x + d, y))
    for d in across:
        block = at(name(x + xs - d, y))
        arrive(d, block)
        send(xs + d, block, name(x, 1 - y))
        yield name(x + xs - d, y)
    for d in along:
        block = name(x + xs - d, y)
        arrive(d, at(block))
        yield block
    for d in along + across:
        block = name(x + xs - d, 1 - y)
        arrive(xs + d, at(block))
        yield block
    for copy in sent:
        copy.wait_send()


def gather_kernel(tasks, in_ref, out_ref, packed, a_s, a_r):
    me = lax.axis_index("task")
    depth, width = in_ref.shape
    greet(0, tasks, False)
    packed[me] = pack_rows(in_ref[...])
    steps = spread(tasks, lambda c: packed.at[c], a_s, a_r)
    next(steps)
    out_ref[me] = in_ref[...]
    for got in steps:
        unpack_to(out_ref.at[got], packed[got], depth, width)


def gather_tasks(block, tasks):
    rows = tiles(*block.shape)[2]
    return pl.pallas_call(
        functools.partial(gather_kernel, tasks),
        out_shape=jax.ShapeDtypeStruct((tasks,) + block.shape, block.dtype),
        in_specs=[VMEM],
        out_specs=VMEM,
        scratch_shapes=[pltpu.VMEM((tasks, rows, 128), block.dtype), DMA((tasks,)), DMA((tasks,))],
        compiler_params=params(2),
        name="basis_gather",
    )(block)


def poly_kernel(chips, tasks, in_ref, out_ref, sib_buf, half, slots, column, matrix, final, slab, slab2, slab3,
                core_s, core_r, a_s, a_r, b_s, b_r, c_s, c_r, t1_s, t1_r, t2_s, t2_r, t3_s, t3_r):
    chip, core, sib = place(chips)
    me = lax.axis_index("task")
    depth, width = in_ref.shape[2:]
    per = width // depth
    greet(chips, tasks, True)
    swap = remote(in_ref.at[:, 1 - core], sib_buf, core_s.at[0], core_r.at[0], {"row": sib})
    swap.start()
    swap.wait()

    def add(c):
        both = in_ref[c, core].astype(f32) + sib_buf[c].astype(f32)
        half[c] = pack_rows(both).astype(bf16)

    loop(0, chips, add)
    src, dst = (lambda c: half.at[c]), (lambda d: slots.at[d])
    to_chips(chips, src, dst, a_s, a_r)
    wait_chips(chips, src, dst, a_s, a_r)
    gram = lax.fori_loop(
        1, chips, lambda d, t: t + slots[d].astype(f32), half[chip].astype(f32))
    mine = gram.astype(bf16)
    slab[me] = mine
    column[chip, core] = mine
    tsrc = lambda c: slab.at[me]
    start_tasks(tasks, tsrc, lambda c: slab.at[c], t1_s, t1_r)

    def gather(buf, sems, recvs, n):
        block = lambda c: buf.at[chip, core]
        to_chips(chips, block, lambda d: buf.at[chip, core], sems, recvs)
        wait_chips(chips, block, lambda d: buf.at[around(chip, chips - d, chips), core], sems, recvs)
        swap = remote(buf.at[:, core], buf.at[:, core], core_s.at[n], core_r.at[n], {"row": sib})
        swap.start()
        swap.wait_send()
        remote(buf.at[:, core], buf.at[:, 1 - core], core_s.at[n], core_r.at[n],
               {"row": sib}).wait_recv()

    gather(column, b_s, b_r, 1)
    loop(0, chips * 2, lambda i: unpack_to(
        matrix.at[i], column[i // 2, i % 2], depth, width))
    wait_tasks(tasks, tsrc, lambda c: slab.at[c], t1_s, t1_r)

    def times(left):
        def body(s, total):
            block = matrix[pl.ds(s * per, per)].reshape(width, width)
            return total + jnp.dot(
                unpack_rows(left[s], depth, width), block, preferred_element_type=f32)
        return lax.fori_loop(0, tasks, body, jnp.zeros((depth, width), f32))

    two = pack_rows(times(slab))
    slab2[me] = two.astype(bf16)
    src2 = lambda c: slab2.at[me]
    start_tasks(tasks, src2, lambda c: slab2.at[c], t2_s, t2_r)
    wait_tasks(tasks, src2, lambda c: slab2.at[c], t2_s, t2_r)
    three = pack_rows(times(slab2))
    slab3[me] = three.astype(bf16)
    src3 = lambda c: slab3.at[me]
    start_tasks(tasks, src3, lambda c: slab3.at[c], t3_s, t3_r)
    part = -2.4375 * gram + 1.6875 * two - 0.5625 * three
    wait_tasks(tasks, src3, lambda c: slab3.at[c], t3_s, t3_r)
    four = pack_rows(times(slab3))
    final[chip, core] = (part + 0.0625 * four).astype(bf16)
    gather(final, c_s, c_r, 2)
    loop(0, chips * 2, lambda i: unpack_to(
        out_ref.at[i // 2, i % 2], final[i // 2, i % 2], depth, width))


def polynomial(partial, chips, tasks):
    total, width = partial.shape
    depth = total // (2 * chips)
    shaped = partial.reshape(chips, 2, depth, width)
    rows = tiles(depth, width)[2]
    out = pl.pallas_call(
        functools.partial(poly_kernel, chips, tasks),
        out_shape=jax.ShapeDtypeStruct(shaped.shape, bf16),
        in_specs=[VMEM],
        out_specs=VMEM,
        scratch_shapes=[pltpu.VMEM((chips, depth, width), bf16)]
        + [pltpu.VMEM((chips, rows, 128), bf16)] * 2
        + [pltpu.VMEM((chips, 2, rows, 128), bf16), pltpu.VMEM((chips * 2, depth, width), bf16),
           pltpu.VMEM((chips, 2, rows, 128), bf16)]
        + [pltpu.VMEM((tasks, rows, 128), bf16)] * 3
        + [DMA((3,)), DMA((3,))] + [DMA((chips,))] * 6 + [DMA((tasks,))] * 6,
        compiler_params=params(3),
        name="polynomial",
    )(shaped)
    return out.reshape(total, width)


def pair_tiles(width):
    return 16 * (2 * (width // 128) + (1 if width % 128 else 0))


def pack_pair(one, two):
    width = one.shape[1]
    full = width // 128
    parts = [v[:, i * 128:(i + 1) * 128] for v in (one, two) for i in range(full)]
    if width % 128:
        parts.append(jnp.concatenate([one[:, full * 128:], two[:, full * 128:]], axis=1))
    return jnp.concatenate(parts, axis=0)


def unpack_pair(packed, width):
    full = width // 128
    out = []
    for v in range(2):
        parts = [packed[(v * full + i) * 16:(v * full + i + 1) * 16] for i in range(full)]
        if width % 128:
            parts.append(packed[2 * full * 16:, v * 64:v * 64 + 64])
        out.append(jnp.concatenate(parts, axis=1) if len(parts) > 1 else parts[0])
    return out


def coef_kernel(chips, tasks, in_ref, w_ref, out_ref, wall_ref, sib_buf, half, slots, other, other_in,
                mine, block, gathered, wpacked, core_s, core_r, a_s, a_r, b_s, b_r, y_sem,
                t1_s, t1_r, w_s, w_r):
    chip, core, sib = place(chips)
    me = lax.axis_index("task")
    width = in_ref.shape[-1]
    pairs = tasks // 2
    wdepth = w_ref.shape[0]
    greet_near(chips, tasks)
    swap = remote(in_ref.at[:, :, 1 - core], sib_buf, core_s.at[0], core_r.at[0], {"row": sib})
    swap.start()
    wpacked[me] = pack_rows(w_ref[...])
    wsteps = spread(tasks, lambda c: wpacked.at[c], w_s, w_r)
    next(wsteps)
    wall_ref[me] = w_ref[...]
    swap.wait()

    def add(c):
        for p in range(pairs):
            one, two = (
                in_ref[u, c, core].astype(f32) + sib_buf[u, c].astype(f32)
                for u in (2 * p, 2 * p + 1)
            )
            half[c, p] = pack_pair(one, two).astype(bf16)

    loop(0, chips, add)
    total = ring_reduce(chips, half, slots, other, other_in, a_s, a_r, y_sem)
    for p in range(pairs):
        for v, part in enumerate(unpack_pair(total[p], width)):
            mine[2 * p + v] = part.astype(bf16)
    block[me] = mine[me]
    tsrc, tdst = (lambda c: mine.at[c]), (lambda c: block.at[c])
    start_tasks(tasks, tsrc, tdst, t1_s, t1_r)
    for got in wsteps:
        unpack_to(wall_ref.at[got], wpacked[got], wdepth, width)
    wait_tasks(tasks, tsrc, tdst, t1_s, t1_r)
    for p in range(pairs):
        gathered[core, chip, p] = pack_pair(block[2 * p], block[2 * p + 1])
    ring_gather(chips, lambda c: gathered.at[core, c], b_s, b_r, y_sem)
    swap = remote(gathered.at[core], gathered.at[core], core_s.at[1], core_r.at[1], {"row": sib})
    swap.start()

    def spill(which):
        def body(c):
            for p in range(pairs):
                for v, part in enumerate(unpack_pair(gathered[which, c, p], width)):
                    out_ref[2 * p + v, c, which] = part
        loop(0, chips, body)

    spill(core)
    swap.wait_send()
    remote(gathered.at[core], gathered.at[1 - core], core_s.at[1], core_r.at[1],
           {"row": sib}).wait_recv()
    spill(1 - core)


def coefficients_and_weights(partial, weights, chips, tasks):
    features, width = partial.shape
    depth = features // (tasks * chips * 2)
    shaped = partial.reshape(tasks, chips, 2, depth, width)
    chunk = (tasks // 2, pair_tiles(width), 128)
    out, wall = pl.pallas_call(
        functools.partial(coef_kernel, chips, tasks),
        out_shape=(jax.ShapeDtypeStruct(shaped.shape, bf16),
                   jax.ShapeDtypeStruct((tasks,) + weights.shape, bf16)),
        in_specs=[VMEM, VMEM],
        out_specs=(VMEM, VMEM),
        scratch_shapes=[pltpu.VMEM((tasks, chips, depth, width), bf16),
                        pltpu.VMEM((chips,) + chunk, bf16), pltpu.VMEM((chips,) + chunk, bf16),
                        pltpu.VMEM(chunk, bf16), pltpu.VMEM(chunk, bf16)]
        + [pltpu.VMEM((tasks, depth, width), bf16)] * 2
        + [pltpu.VMEM((2, chips) + chunk, bf16),
           pltpu.VMEM((tasks, tiles(*weights.shape)[2], 128), bf16)]
        + [DMA((2,)), DMA((2,))] + [DMA((chips,))] * 4 + [DMA((4,))] + [DMA((tasks,))] * 4,
        compiler_params=params(4),
        name="coefficients",
    )(shaped, weights)
    return out.reshape(tasks, features // tasks, width), wall


def pack(square):
    n = square.shape[0]
    parts = []
    for at in range(0, n, 128):
        piece = square[at:, at:min(at + 128, n)]
        parts.append(jnp.pad(piece, ((0, 0), (0, 128 - piece.shape[1]))))
    return jnp.concatenate(parts, axis=0)


def unpack(packed, n):
    parts, top = [], 0
    for at in range(0, n, 128):
        piece = packed[top:top + n - at, :min(128, n - at)]
        parts.append(jnp.pad(piece, ((at, 0), (0, 0))))
        top += n - at
    return jnp.concatenate(parts, axis=1)


def local(delta, sketch, base):
    tasks = lax.axis_size("task")
    chips = lax.axis_size("row") // 2
    delta_rows, task_sketch = delta[0], sketch[0]
    width = task_sketch.shape[1]
    sketched = jnp.dot(delta_rows, task_sketch, preferred_element_type=f32)
    packed = pack(jnp.dot(sketched.T, sketched, precision=highest))
    unit = 16 * chips
    packed = jnp.pad(packed, ((0, -packed.shape[0] % unit), (0, 0)))
    square = unpack(all_reduce_square(packed, chips), width)
    inverse = inverse_factor(square)
    own = lax.dot_general(
        sketched, inverse, (((1,), (1,)), ((), ())), precision=highest
    ) * (1.0 / math.sqrt(tasks))
    stack = gather_tasks(own.astype(bf16), tasks)
    gram = lax.dot_general(
        stack, own.astype(bf16), (((1,), (0,)), ((), ())), preferred_element_type=f32
    ).reshape(tasks * width, width).astype(bf16)
    poly = polynomial(gram, chips, tasks).reshape(tasks, width, width)
    weights = (
        2.25 * own
        + lax.dot_general(stack, poly, (((0, 2), (0, 1)), ((), ())), preferred_element_type=f32)
    ).astype(bf16)
    partial = lax.dot_general(
        delta_rows, weights, (((0,), (0,)), ((), ())), preferred_element_type=f32
    ).astype(bf16)
    coefs, stack2 = coefficients_and_weights(partial, weights, chips, tasks)
    update = lax.dot_general(
        stack2, coefs, (((0, 2), (0, 2)), ((), ())), preferred_element_type=f32
    )
    return (base.astype(f32) + update).astype(bf16)


def solution(mesh):
    return jax.shard_map(
        local,
        mesh=mesh,
        in_specs=(P("task", "row", None), P("task", None, None), P("row", "task")),
        out_specs=P("row", "task"),
        check_vma=False,
    )
```

```python
import functools
import math

import jax
import jax.numpy as jnp
from jax import lax
from jax.experimental import pallas as pl
from jax.experimental.pallas import tpu as pltpu
from jax.sharding import PartitionSpec as P

highest = lax.Precision.HIGHEST
MESH = pl.DeviceIdType.MESH
VMEM = pl.BlockSpec(memory_space=pltpu.VMEM)
DMA = pltpu.SemaphoreType.DMA
f32 = jnp.float32
bf16 = jnp.bfloat16
CB = 64
PANEL = 8


def params(cid):
    return pltpu.CompilerParams(
        collective_id=cid, has_side_effects=True, vmem_limit_bytes=48 * 1024 * 1024
    )


def place(chips):
    row = lax.axis_index("row")
    chip, core = row // 2, row % 2
    return chip, core, chip * 2 + (1 - core)


def around(me, step, count):
    return (me + step) % count


def remote(src, dst, ssem, rsem, where):
    return pltpu.make_async_remote_copy(
        src_ref=src, dst_ref=dst, send_sem=ssem, recv_sem=rsem,
        device_id=where, device_id_type=MESH,
    )


def loop(lo, hi, body):
    def step(i, carry):
        body(i)
        return carry

    lax.fori_loop(lo, hi, step, 0)


def greet(chips, tasks, rows):
    barrier = pltpu.get_barrier_semaphore()
    total = 0
    if rows:
        chip, core, sib = place(chips)
        pl.semaphore_signal(barrier, inc=1, device_id={"row": sib}, device_id_type=MESH)
        loop(1, chips, lambda d: pl.semaphore_signal(
            barrier, inc=1, device_id={"row": around(chip, d, chips) * 2 + core},
            device_id_type=MESH))
        total += chips
    if tasks:
        me = lax.axis_index("task")
        loop(1, tasks, lambda d: pl.semaphore_signal(
            barrier, inc=1, device_id={"task": around(me, d, tasks)}, device_id_type=MESH))
        total += tasks - 1
    pl.semaphore_wait(barrier, total)


def to_chips(chips, src, dst, ssem, rsem):
    chip, core, _ = place(chips)

    def body(d):
        other = around(chip, d, chips)
        remote(src(other), dst(d), ssem.at[d], rsem.at[d], {"row": other * 2 + core}).start()

    loop(1, chips, body)


def wait_chips(chips, src, dst, ssem, rsem):
    chip, core, _ = place(chips)

    def body(d):
        other = around(chip, d, chips)
        copy = remote(src(other), dst(d), ssem.at[d], rsem.at[d], {"row": other * 2 + core})
        copy.wait()

    loop(1, chips, body)


def tiles(depth, width):
    full = width // 128
    top = -(-depth // 32) * 16 if width % 128 else 0
    return full, top, full * depth + top


def pack_rows(value):
    depth, width = value.shape
    full, top, _ = tiles(depth, width)
    parts = [value[:, i * 128:(i + 1) * 128] for i in range(full)]
    if top:
        tail = value[:, full * 128:]
        low = jnp.concatenate(
            [tail[top:], jnp.zeros((2 * top - depth, 64), value.dtype)], axis=0
        ) if 2 * top > depth else tail[top:]
        parts.append(jnp.concatenate([tail[:top], low], axis=1))
    return jnp.concatenate(parts, axis=0)


def unpack_rows(packed, depth, width):
    full, top, _ = tiles(depth, width)
    parts = [packed[i * depth:(i + 1) * depth] for i in range(full)]
    if top:
        tail = packed[full * depth:full * depth + top]
        parts.append(jnp.concatenate([tail[:, :64], tail[:depth - top, 64:]], axis=0))
    return jnp.concatenate(parts, axis=1)


def unpack_to(dst, packed, depth, width):
    full, top, _ = tiles(depth, width)
    for i in range(full):
        dst[:, i * 128:(i + 1) * 128] = packed[i * depth:(i + 1) * depth]
    if top:
        tail = packed[full * depth:full * depth + top]
        dst[:top, full * 128:] = tail[:, :64]
        dst[top:, full * 128:] = tail[:depth - top, 64:]


def hello(chips, tasks):
    barrier = pltpu.get_barrier_semaphore()
    chip, core, sib = place(chips)
    pl.semaphore_signal(barrier, inc=1, device_id={"row": sib}, device_id_type=MESH)
    loop(1, chips, lambda d: pl.semaphore_signal(
        barrier, inc=1, device_id={"row": around(chip, d, chips) * 2 + core}, device_id_type=MESH))
    me = lax.axis_index("task")
    loop(1, tasks, lambda d: pl.semaphore_signal(
        barrier, inc=1, device_id={"task": around(me, d, tasks)}, device_id_type=MESH))


def barrier_wait(chips, tasks):
    pl.semaphore_wait(pltpu.get_barrier_semaphore(), chips + tasks - 1)


def line(zs, z, y, core):
    return (((z + zs) % zs) * 2 + y) * 2 + core


def streams(zs, y):
    far, near = zs // 2, zs // 2 - 1
    return [(2, 1, near, 1 - y), (3, -1, far, 1 - y), (0, 1, far, y), (1, -1, near, y)]


def ring_reduce(chips, half, slots, other, other_in, ssem, rsem, ysem):
    chip, core, _ = place(chips)
    zs, z, y = chips // 2, chip // 2, chip % 2
    hops = zs // 2
    sent = []

    def term(zz, yy):
        return half[((zz + zs) % zs) * 2 + yy]

    def send(stream, step, src):
        k, way = stream[0], stream[1]
        n = k * hops + step - 1
        copy = remote(src, slots.at[n], ssem.at[n], rsem.at[n], {"row": line(zs, z + way, y, core)})
        copy.start()
        sent.append(copy)

    def arrive(stream, step):
        n = stream[0] * hops + step - 1
        remote(slots.at[n], slots.at[n], ssem.at[n], rsem.at[n], {"row": line(zs, z, y, core)}).wait_recv()
        return n

    for st in streams(zs, y):
        if st[2]:
            dest = ((z + st[1] * st[2] + zs) % zs) * 2 + st[3]
            send(st, 1, half.at[dest])
    for step in range(1, hops + 1):
        for st in streams(zs, y):
            if step <= st[2]:
                n = arrive(st, step)
                if step < st[2]:
                    dest = z + st[1] * (st[2] - step)
                    slots[n] = (slots[n].astype(f32) + term(dest, st[3]).astype(f32)).astype(bf16)
                    send(st, step + 1, slots.at[n])

    def final(plane, pair):
        total = term(z, plane).astype(f32)
        for k, n in pair:
            if n:
                total = total + slots[k * hops + n - 1].astype(f32)
        return total

    other[...] = final(1 - y, [(2, hops - 1), (3, hops)]).astype(bf16)
    swap = remote(other, other_in, ysem.at[0], ysem.at[1], {"row": line(zs, z, 1 - y, core)})
    swap.start()
    own = final(y, [(0, hops), (1, hops - 1)])
    swap.wait()
    for copy in sent:
        copy.wait_send()
    return own + other_in[...].astype(f32)


def ring_gather(chips, at, ssem, rsem, ysem):
    chip, core, _ = place(chips)
    zs, z, y = chips // 2, chip // 2, chip % 2
    hops = zs // 2
    sent = []

    def spot(zz, yy):
        return at(((zz + zs) % zs) * 2 + yy)

    def send(stream, step):
        k, way, _, yy = stream
        n = k * hops + step - 1
        block = spot(z - way * (step - 1), yy)
        copy = remote(block, block, ssem.at[n], rsem.at[n], {"row": line(zs, z + way, y, core)})
        copy.start()
        sent.append(copy)

    def arrive(stream, step):
        k, way, _, yy = stream
        n = k * hops + step - 1
        block = spot(z - way * step, yy)
        remote(block, block, ssem.at[n], rsem.at[n], {"row": line(zs, z, y, core)}).wait_recv()

    across = {"row": line(zs, z, 1 - y, core)}
    swap = remote(spot(z, y), spot(z, y), ysem.at[2], ysem.at[3], across)
    swap.start()
    order = streams(zs, y)[2:] + streams(zs, y)[:2]
    for st in order[:2]:
        if st[2]:
            send(st, 1)
    remote(spot(z, 1 - y), spot(z, 1 - y), ysem.at[2], ysem.at[3], across).wait_recv()
    for st in order[2:]:
        if st[2]:
            send(st, 1)
    for step in range(1, hops + 1):
        for st in order:
            if step <= st[2]:
                arrive(st, step)
                if step < st[2]:
                    send(st, step + 1)
    swap.wait_send()
    for copy in sent:
        copy.wait_send()


def square_kernel(chips, in_ref, out_ref, sib_buf, half, slots, core_s, core_r, a_s, a_r, b_s, b_r):
    chip, core, sib = place(chips)
    greet(chips, 0, True)
    swap = remote(in_ref.at[1 - core], sib_buf, core_s.at[0], core_r.at[0], {"row": sib})
    swap.start()
    swap.wait()
    half[...] = in_ref[core] + sib_buf[...]
    src, dst = (lambda c: half.at[c]), (lambda d: slots.at[d])
    to_chips(chips, src, dst, a_s, a_r)
    wait_chips(chips, src, dst, a_s, a_r)
    total = lax.fori_loop(1, chips, lambda d, t: t + slots[d], half[chip])
    out_ref[core, chip] = total
    src = lambda c: out_ref.at[core, chip]
    to_chips(chips, src, lambda d: out_ref.at[core, chip], b_s, b_r)
    wait_chips(chips, src, lambda d: out_ref.at[core, around(chip, chips - d, chips)], b_s, b_r)
    swap = remote(out_ref.at[core], out_ref.at[core], core_s.at[1], core_r.at[1], {"row": sib})
    swap.start()
    swap.wait_send()
    remote(out_ref.at[core], out_ref.at[1 - core], core_s.at[1], core_r.at[1], {"row": sib}).wait_recv()


def all_reduce_square(packed, chips):
    rows, lanes = packed.shape
    part = rows // (2 * chips)
    shaped = packed.reshape(2, chips, part, lanes)
    out = pl.pallas_call(
        functools.partial(square_kernel, chips),
        out_shape=jax.ShapeDtypeStruct(shaped.shape, f32),
        in_specs=[VMEM],
        out_specs=VMEM,
        scratch_shapes=[pltpu.VMEM((chips, part, lanes), f32)] * 3
        + [DMA((2,)), DMA((2,))] + [DMA((chips,))] * 4,
        compiler_params=params(1),
        name="square_sum",
    )(shaped)
    return out.reshape(rows, lanes)


def dot_nt(a, b):
    return lax.dot_general(a, b, (((1,), (1,)), ((), ())), precision=highest,
                           preferred_element_type=f32)


def dot_nn(a, b):
    return lax.dot_general(a, b, (((1,), (0,)), ((), ())), precision=highest,
                           preferred_element_type=f32)


def basis_kernel(shrink, packed, x_ref, own_ref, cols, fac, inv):
    n = x_ref.shape[1]
    blocks = n // CB
    row_id = lax.broadcasted_iota(jnp.int32, (CB, 2 * CB), 0)
    lane_id = lax.broadcasted_iota(jnp.int32, (CB, 2 * CB), 1)
    eye = (lane_id == row_id + CB).astype(f32)
    inv[...] = jnp.zeros_like(inv)
    for k in range(blocks):
        wide, off = divmod(k * CB, 128)
        top = sum(n - 128 * w for w in range(wide))
        cols[k, k * CB:, :] = packed[top + off:top + n - 128 * wide, off:off + CB]
    for k in range(blocks):
        at = k * CB
        both = jnp.concatenate([cols[k, at:at + CB, :], jnp.zeros((CB, CB), f32)], axis=1) + eye
        for first in range(0, CB, PANEL):
            wide = [jnp.broadcast_to(both[:, first + m:first + m + 1], both.shape)
                    for m in range(PANEL)]
            for m in range(PANEL):
                j = first + m
                f = jnp.where(row_id > j, wide[m] * (1.0 / wide[m][j:j + 1, :]), 0.0)
                for q in range(m + 1, PANEL):
                    wide[q] = wide[q] - f * wide[q][j:j + 1, :]
                both = both - f * both[j:j + 1, :]
        diag = jnp.sum(jnp.where(lane_id == row_id, both, 0.0), axis=1, keepdims=True)
        zkk = both[:, CB:] * lax.rsqrt(diag)
        if k + 1 < blocks:
            panel = dot_nt(cols[k, at + CB:, :], zkk)
            fac[k, at + CB:, :] = panel
            for j in range(k + 1, blocks):
                off = (j - k - 1) * CB
                cols[j, j * CB:, :] = cols[j, j * CB:, :] - dot_nt(
                    panel[off:, :], panel[off:off + CB, :])
        for c in range(k):
            acc = dot_nn(fac[c, at:at + CB, :], inv[c, c * CB:(c + 1) * CB, :])
            for m in range(c + 1, k):
                acc = acc + dot_nn(fac[m, at:at + CB, :], inv[c, m * CB:(m + 1) * CB, :])
            inv[c, at:at + CB, :] = -dot_nn(zkk, acc)
        inv[k, at:at + CB, :] = zkk
    z = jnp.concatenate([inv[c] for c in range(blocks)], axis=1)
    own_ref[...] = dot_nt(x_ref[...], z) * shrink


def basis_of(packed, sketched, shrink):
    n = sketched.shape[1]
    return pl.pallas_call(
        functools.partial(basis_kernel, shrink),
        out_shape=jax.ShapeDtypeStruct(sketched.shape, f32),
        in_specs=[VMEM, VMEM],
        out_specs=VMEM,
        scratch_shapes=[pltpu.VMEM((n // CB, n, CB), f32)] * 3,
        compiler_params=pltpu.CompilerParams(vmem_limit_bytes=32 * 1024 * 1024),
        name="basis",
    )(packed, sketched)


def start_tasks(tasks, src, dst, ssem, rsem):
    me = lax.axis_index("task")

    def body(d):
        other = around(me, d, tasks)
        remote(src(other), dst(me), ssem.at[d], rsem.at[d], {"task": other}).start()

    loop(1, tasks, body)


def wait_tasks(tasks, src, dst, ssem, rsem):
    me = lax.axis_index("task")

    def body(d):
        other = around(me, d, tasks)
        back = around(me, tasks - d, tasks)
        remote(src(other), dst(back), ssem.at[d], rsem.at[d], {"task": other}).wait()

    loop(1, tasks, body)


def spread(tasks, at, ssem, rsem):
    me = lax.axis_index("task")
    xs = tasks // 2
    x, y = me % xs, me // xs
    sent = []

    def send(n, block, to):
        copy = remote(block, block, ssem.at[n], rsem.at[n], {"task": to})
        copy.start()
        sent.append(copy)

    def arrive(n, block):
        remote(block, block, ssem.at[n], rsem.at[n], {"task": me}).wait_recv()

    def name(xx, yy):
        return yy * xs + xx % xs

    own = at(me)
    send(0, own, name(x, 1 - y))
    for d in range(1, xs):
        send(d, own, name(x + d, y))
    yield
    twin = at(name(x, 1 - y))
    arrive(0, twin)
    yield name(x, 1 - y)
    across = [d for d in range(1, xs) if d == xs // 2]
    along = [d for d in range(1, xs) if d != xs // 2]
    for d in along:
        send(xs + d, twin, name(x + d, y))
    for d in across:
        block = at(name(x + xs - d, y))
        arrive(d, block)
        send(xs + d, block, name(x, 1 - y))
        yield name(x + xs - d, y)
    for d in along:
        block = name(x + xs - d, y)
        arrive(d, at(block))
        yield block
    for d in along + across:
        block = name(x + xs - d, 1 - y)
        arrive(xs + d, at(block))
        yield block
    for copy in sent:
        copy.wait_send()


def pair_tiles(width):
    return 16 * (2 * (width // 128) + (1 if width % 128 else 0))


def pack_pair(one, two):
    width = one.shape[1]
    full = width // 128
    parts = [v[:, i * 128:(i + 1) * 128] for v in (one, two) for i in range(full)]
    if width % 128:
        parts.append(jnp.concatenate([one[:, full * 128:], two[:, full * 128:]], axis=1))
    return jnp.concatenate(parts, axis=0)


def unpack_pair(packed, width):
    full = width // 128
    out = []
    for v in range(2):
        parts = [packed[(v * full + i) * 16:(v * full + i + 1) * 16] for i in range(full)]
        if width % 128:
            parts.append(packed[2 * full * 16:, v * 64:v * 64 + 64])
        out.append(jnp.concatenate(parts, axis=1) if len(parts) > 1 else parts[0])
    return out


def joint_kernel(
    chips, tasks, own_ref, delta_hbm, out_ref, wall_ref,
    delta, turned, stack, packed, terms, sib_buf, half, slots, column, matrix, final,
    slab, slab2, slab3, parts, sib_parts, half2, slots2, other, other_in, mine, block, gathered, wpacked,
    local_s, g_s, g_r, sw_s, sw_r, core_s, core_r, a_s, a_r, b_s, b_r, c_s, c_r,
    t1_s, t1_r, t2_s, t2_r, t3_s, t3_r, w_s, w_r, sp_s, sp_r, d_s, d_r, e_s, e_r, y_sem, t4_s, t4_r,
):
    chip, core, sib = place(chips)
    me = lax.axis_index("task")
    rows, width = own_ref.shape
    depth = terms.shape[2]
    per = width // depth
    pairs = tasks // 2
    hello(chips, tasks)
    load = pltpu.make_async_copy(delta_hbm, delta, local_s.at[0])
    load.start()
    own = own_ref[...].astype(bf16)
    stack[me] = own
    packed[me] = pack_rows(own)
    barrier_wait(chips, tasks)

    def swap_term(s, i):
        at = pl.ds(s * (per // 2), per // 2)
        return remote(terms.at[at, 1 - core], sib_buf.at[at], sw_s.at[i], sw_r.at[i], {"row": sib})

    def gram_term(s, i):
        term = lax.dot_general(stack[s], stack[me], (((0,), (0,)), ((), ())),
                               preferred_element_type=f32).astype(bf16)
        terms[pl.ds(s * (per // 2), per // 2)] = term.reshape(per // 2, 2, depth, width)
        swap_term(s, i).start()

    def to_owner(s, i):
        swap_term(s, i).wait()
        for e in range(per // 2):
            c = s * (per // 2) + e
            both = terms[c, core].astype(f32) + sib_buf[c].astype(f32)
            half[c] = pack_rows(both).astype(bf16)
            d = around(c, chips - chip, chips)

            @pl.when(c != chip)
            def _():
                remote(half.at[c], slots.at[d], a_s.at[d], a_r.at[d], {"row": c * 2 + core}).start()

    steps = spread(tasks, lambda c: packed.at[c], g_s, g_r)
    next(steps)
    gram_term(me, 0)
    ready = [me]
    for got in steps:
        unpack_to(stack.at[got], packed[got], rows, width)
        ready.append(got)
        gram_term(got, len(ready) - 1)
        to_owner(ready[-2], len(ready) - 2)
    to_owner(ready[-1], len(ready) - 1)
    wait_chips(chips, lambda c: half.at[c], lambda d: slots.at[d], a_s, a_r)
    gram = lax.fori_loop(
        1, chips, lambda d, t: t + slots[d].astype(f32), half[chip].astype(f32))
    first = gram.astype(bf16)
    slab[me] = first
    column[chip, core] = first

    tsrc = lambda c: slab.at[me]
    start_tasks(tasks, tsrc, lambda c: slab.at[c], t1_s, t1_r)

    def gather(buf, sems, recvs, n, beside):
        mine_at = lambda c: buf.at[chip, core]
        to_chips(chips, mine_at, lambda d: buf.at[chip, core], sems, recvs)
        beside()
        wait_chips(chips, mine_at, lambda d: buf.at[around(chip, chips - d, chips), core], sems, recvs)
        swap = remote(buf.at[:, core], buf.at[:, core], core_s.at[n], core_r.at[n], {"row": sib})
        swap.start()
        swap.wait_send()
        remote(buf.at[:, core], buf.at[:, 1 - core], core_s.at[n], core_r.at[n],
               {"row": sib}).wait_recv()

    span = turned.shape[0] // tasks

    def turn():
        load.wait()
        loop(0, tasks, lambda u: turned.__setitem__(
            pl.ds(pl.multiple_of(u * span, span), span),
            delta[:, pl.ds(pl.multiple_of(u * span, span), span)].T))

    gather(column, b_s, b_r, 1, turn)
    loop(0, chips * 2, lambda i: unpack_to(
        matrix.at[i], column[i // 2, i % 2], depth, width))
    wait_tasks(tasks, tsrc, lambda c: slab.at[c], t1_s, t1_r)

    def times(left):
        def body(s, total):
            right = matrix[pl.ds(s * per, per)].reshape(width, width)
            return total + jnp.dot(
                unpack_rows(left[s], depth, width), right, preferred_element_type=f32)
        return lax.fori_loop(0, tasks, body, jnp.zeros((depth, width), f32))

    two = pack_rows(times(slab))
    slab2[me] = two.astype(bf16)
    src2 = lambda c: slab2.at[me]
    start_tasks(tasks, src2, lambda c: slab2.at[c], t2_s, t2_r)
    wait_tasks(tasks, src2, lambda c: slab2.at[c], t2_s, t2_r)
    three = pack_rows(times(slab2))
    slab3[me] = three.astype(bf16)
    src3 = lambda c: slab3.at[me]
    start_tasks(tasks, src3, lambda c: slab3.at[c], t3_s, t3_r)
    part = -2.4375 * gram + 1.6875 * two - 0.5625 * three
    wait_tasks(tasks, src3, lambda c: slab3.at[c], t3_s, t3_r)
    final[chip, core] = (part + 0.0625 * pack_rows(times(slab3))).astype(bf16)
    gather(final, c_s, c_r, 2, lambda: None)
    loop(0, chips * 2, lambda i: unpack_to(
        matrix.at[i], final[i // 2, i % 2], depth, width))

    def apply(s, total):
        right = matrix[pl.ds(s * per, per)].reshape(width, width)
        return total + jnp.dot(stack[s], right, preferred_element_type=f32)

    weights = lax.fori_loop(0, tasks, apply, 2.25 * own_ref[...]).astype(bf16)
    wall_ref[me] = weights
    wpacked[me] = pack_rows(weights)
    wsteps = spread(tasks, lambda c: wpacked.at[c], w_s, w_r)
    next(wsteps)

    def swap_part(u):
        return remote(parts.at[u, :, 1 - core], sib_parts.at[u], sp_s.at[u], sp_r.at[u], {"row": sib})

    def coef_term(u):
        rows_u = turned[pl.ds(pl.multiple_of(u * span, span), span)]
        term = jnp.dot(rows_u, wall_ref[me], preferred_element_type=f32).astype(bf16)
        parts[u] = term.reshape(parts.shape[1:])
        swap_part(u).start()

    loop(0, tasks, coef_term)
    loop(0, tasks, lambda u: swap_part(u).wait())

    def add(c):
        for p in range(pairs):
            one, two = (
                parts[u, c, core].astype(f32) + sib_parts[u, c].astype(f32)
                for u in (2 * p, 2 * p + 1)
            )
            half2[c, p] = pack_pair(one, two).astype(bf16)

    loop(0, chips, add)
    total = ring_reduce(chips, half2, slots2, other, other_in, d_s, d_r, y_sem)
    for p in range(pairs):
        for v, piece in enumerate(unpack_pair(total[p], width)):
            mine[2 * p + v] = piece.astype(bf16)
    block[me] = mine[me]
    tsrc4, tdst4 = (lambda c: mine.at[c]), (lambda c: block.at[c])
    start_tasks(tasks, tsrc4, tdst4, t4_s, t4_r)
    for got in wsteps:
        unpack_to(wall_ref.at[got], wpacked[got], rows, width)
    wait_tasks(tasks, tsrc4, tdst4, t4_s, t4_r)
    for p in range(pairs):
        gathered[core, chip, p] = pack_pair(block[2 * p], block[2 * p + 1])
    ring_gather(chips, lambda c: gathered.at[core, c], e_s, e_r, y_sem)
    swap = remote(gathered.at[core], gathered.at[core], core_s.at[0], core_r.at[0], {"row": sib})
    swap.start()

    def spill(which):
        def body(c):
            for p in range(pairs):
                for v, piece in enumerate(unpack_pair(gathered[which, c, p], width)):
                    out_ref[2 * p + v, c, which] = piece
        loop(0, chips, body)

    spill(core)
    swap.wait_send()
    remote(gathered.at[core], gathered.at[1 - core], core_s.at[0], core_r.at[0],
           {"row": sib}).wait_recv()
    spill(1 - core)


def joint(own, delta, chips, tasks):
    rows, width = own.shape
    features = delta.shape[1]
    depth = tasks * width // (2 * chips)
    piece = features // (tasks * chips * 2)
    chunk = (tasks // 2, pair_tiles(width), 128)
    high = tiles(depth, width)[2]
    tall = tiles(rows, width)[2]
    buf = lambda *shape: pltpu.VMEM(shape, bf16)
    pair = lambda n: [DMA((n,)), DMA((n,))]
    return pl.pallas_call(
        functools.partial(joint_kernel, chips, tasks),
        out_shape=(jax.ShapeDtypeStruct((tasks, chips, 2, piece, width), bf16),
                   jax.ShapeDtypeStruct((tasks, rows, width), bf16)),
        in_specs=[VMEM, pl.BlockSpec(memory_space=pl.ANY)],
        out_specs=(VMEM, VMEM),
        scratch_shapes=[
            buf(rows, features), buf(features, rows), buf(tasks, rows, width), buf(tasks, tall, 128),
            buf(chips, 2, depth, width), buf(chips, depth, width), buf(chips, high, 128),
            buf(chips, high, 128), buf(chips, 2, high, 128), buf(chips * 2, depth, width),
            buf(chips, 2, high, 128),
            buf(tasks, high, 128), buf(tasks, high, 128), buf(tasks, high, 128),
            buf(tasks, chips, 2, piece, width), buf(tasks, chips, piece, width),
            buf(chips, *chunk), buf(chips, *chunk), buf(*chunk), buf(*chunk),
            buf(tasks, piece, width), buf(tasks, piece, width), buf(2, chips, *chunk),
            buf(tasks, tall, 128), DMA((1,)),
        ] + pair(tasks) + pair(tasks) + pair(3) + pair(chips) * 3
        + pair(tasks) * 5 + pair(chips) * 2 + [DMA((4,))] + pair(tasks),
        compiler_params=params(2),
        name="joint",
    )(own, delta)


def pack(square):
    n = square.shape[0]
    parts = []
    for at in range(0, n, 128):
        piece = square[at:, at:min(at + 128, n)]
        parts.append(jnp.pad(piece, ((0, 0), (0, 128 - piece.shape[1]))))
    return jnp.concatenate(parts, axis=0)


def local(delta, sketch, base):
    tasks = lax.axis_size("task")
    chips = lax.axis_size("row") // 2
    delta_rows, task_sketch = delta[0], sketch[0]
    width = task_sketch.shape[1]
    sketched = jnp.dot(delta_rows, task_sketch, preferred_element_type=f32)
    packed = pack(jnp.dot(sketched.T, sketched, precision=highest))
    unit = 16 * chips
    packed = jnp.pad(packed, ((0, -packed.shape[0] % unit), (0, 0)))
    packed = all_reduce_square(packed, chips)
    own = basis_of(packed, sketched, 1.0 / math.sqrt(tasks))
    coefs, stack = joint(own, delta_rows, chips, tasks)
    coefs = coefs.reshape(tasks, -1, width)
    update = lax.dot_general(
        stack, coefs, (((0, 2), (0, 2)), ((), ())), preferred_element_type=f32
    )
    return (base.astype(f32) + update).astype(bf16)


def solution(mesh):
    return jax.shard_map(
        local,
        mesh=mesh,
        in_specs=(P("task", "row", None), P("task", None, None), P("row", "task")),
        out_specs=P("row", "task"),
        check_vma=False,
    )
```

```python
import functools
import math

import jax
import jax.numpy as jnp
from jax import lax
from jax.experimental import pallas as pl
from jax.experimental.pallas import tpu as pltpu
from jax.sharding import PartitionSpec as P

highest = lax.Precision.HIGHEST
MESH = pl.DeviceIdType.MESH
VMEM = pl.BlockSpec(memory_space=pltpu.VMEM)
DMA = pltpu.SemaphoreType.DMA
f32 = jnp.float32
bf16 = jnp.bfloat16
CB = 64
PANEL = 8
LOADS = 4


def params(cid):
    return pltpu.CompilerParams(
        collective_id=cid, has_side_effects=True, vmem_limit_bytes=48 * 1024 * 1024
    )


def place(chips):
    row = lax.axis_index("row")
    chip, core = row // 2, row % 2
    return chip, core, chip * 2 + (1 - core)


def around(me, step, count):
    return (me + step) % count


def remote(src, dst, ssem, rsem, where):
    return pltpu.make_async_remote_copy(
        src_ref=src, dst_ref=dst, send_sem=ssem, recv_sem=rsem,
        device_id=where, device_id_type=MESH,
    )


def loop(lo, hi, body):
    def step(i, carry):
        body(i)
        return carry

    lax.fori_loop(lo, hi, step, 0)


def to_chips(chips, src, dst, ssem, rsem):
    chip, core, _ = place(chips)

    def body(d):
        other = around(chip, d, chips)
        remote(src(other), dst(d), ssem.at[d], rsem.at[d], {"row": other * 2 + core}).start()

    loop(1, chips, body)


def wait_chips(chips, src, dst, ssem, rsem):
    chip, core, _ = place(chips)

    def body(d):
        other = around(chip, d, chips)
        copy = remote(src(other), dst(d), ssem.at[d], rsem.at[d], {"row": other * 2 + core})
        copy.wait()

    loop(1, chips, body)


def tiles(depth, width):
    full = width // 128
    top = -(-depth // 32) * 16 if width % 128 else 0
    return full, top, full * depth + top


def pack_rows(value):
    depth, width = value.shape
    full, top, _ = tiles(depth, width)
    parts = [value[:, i * 128:(i + 1) * 128] for i in range(full)]
    if top:
        tail = value[:, full * 128:]
        low = jnp.concatenate(
            [tail[top:], jnp.zeros((2 * top - depth, 64), value.dtype)], axis=0
        ) if 2 * top > depth else tail[top:]
        parts.append(jnp.concatenate([tail[:top], low], axis=1))
    return jnp.concatenate(parts, axis=0)


def unpack_rows(packed, depth, width):
    full, top, _ = tiles(depth, width)
    parts = [packed[i * depth:(i + 1) * depth] for i in range(full)]
    if top:
        tail = packed[full * depth:full * depth + top]
        parts.append(jnp.concatenate([tail[:, :64], tail[:depth - top, 64:]], axis=0))
    return jnp.concatenate(parts, axis=1)


def unpack_to(dst, packed, depth, width):
    full, top, _ = tiles(depth, width)
    for i in range(full):
        dst[:, i * 128:(i + 1) * 128] = packed[i * depth:(i + 1) * depth]
    if top:
        tail = packed[full * depth:full * depth + top]
        dst[:top, full * 128:] = tail[:, :64]
        dst[top:, full * 128:] = tail[:depth - top, 64:]


def hello(chips, tasks):
    barrier = pltpu.get_barrier_semaphore()
    chip, core, sib = place(chips)
    pl.semaphore_signal(barrier, inc=1, device_id={"row": sib}, device_id_type=MESH)
    loop(1, chips, lambda d: pl.semaphore_signal(
        barrier, inc=1, device_id={"row": around(chip, d, chips) * 2 + core}, device_id_type=MESH))
    if tasks:
        me = lax.axis_index("task")
        loop(1, tasks, lambda d: pl.semaphore_signal(
            barrier, inc=1, device_id={"task": around(me, d, tasks)}, device_id_type=MESH))


def barrier_wait(chips, tasks):
    pl.semaphore_wait(pltpu.get_barrier_semaphore(), chips + tasks - 1)


def line(zs, z, y, core):
    return (((z + zs) % zs) * 2 + y) * 2 + core


def streams(zs, y):
    far, near = zs // 2, zs // 2 - 1
    return [(2, 1, near, 1 - y), (3, -1, far, 1 - y), (0, 1, far, y), (1, -1, near, y)]


def ring_reduce(chips, half, slots, other, other_in, ssem, rsem, ysem):
    chip, core, _ = place(chips)
    zs, z, y = chips // 2, chip // 2, chip % 2
    hops = zs // 2
    sent = []

    def term(zz, yy):
        return half[((zz + zs) % zs) * 2 + yy]

    def send(stream, step, src):
        k, way = stream[0], stream[1]
        n = k * hops + step - 1
        copy = remote(src, slots.at[n], ssem.at[n], rsem.at[n], {"row": line(zs, z + way, y, core)})
        copy.start()
        sent.append(copy)

    def arrive(stream, step):
        n = stream[0] * hops + step - 1
        remote(slots.at[n], slots.at[n], ssem.at[n], rsem.at[n], {"row": line(zs, z, y, core)}).wait_recv()
        return n

    for st in streams(zs, y):
        if st[2]:
            dest = ((z + st[1] * st[2] + zs) % zs) * 2 + st[3]
            send(st, 1, half.at[dest])
    for step in range(1, hops + 1):
        for st in streams(zs, y):
            if step <= st[2]:
                n = arrive(st, step)
                if step < st[2]:
                    dest = z + st[1] * (st[2] - step)
                    slots[n] = (slots[n].astype(f32) + term(dest, st[3]).astype(f32)).astype(bf16)
                    send(st, step + 1, slots.at[n])

    def final(plane, pair):
        total = term(z, plane).astype(f32)
        for k, n in pair:
            if n:
                total = total + slots[k * hops + n - 1].astype(f32)
        return total

    other[...] = final(1 - y, [(2, hops - 1), (3, hops)]).astype(bf16)
    swap = remote(other, other_in, ysem.at[0], ysem.at[1], {"row": line(zs, z, 1 - y, core)})
    swap.start()
    own = final(y, [(0, hops), (1, hops - 1)])
    swap.wait()
    for copy in sent:
        copy.wait_send()
    return own + other_in[...].astype(f32)


def ring_gather(chips, at, ssem, rsem, ysem, landed):
    chip, core, _ = place(chips)
    zs, z, y = chips // 2, chip // 2, chip % 2
    hops = zs // 2
    sent = []

    def spot(zz, yy):
        return at(((zz + zs) % zs) * 2 + yy)

    def send(stream, step):
        k, way, _, yy = stream
        n = k * hops + step - 1
        block = spot(z - way * (step - 1), yy)
        copy = remote(block, block, ssem.at[n], rsem.at[n], {"row": line(zs, z + way, y, core)})
        copy.start()
        sent.append(copy)

    def arrive(stream, step):
        k, way, _, yy = stream
        n = k * hops + step - 1
        where = ((z - way * step + zs) % zs) * 2 + yy
        remote(at(where), at(where), ssem.at[n], rsem.at[n], {"row": line(zs, z, y, core)}).wait_recv()
        return where

    across = {"row": line(zs, z, 1 - y, core)}
    swap = remote(spot(z, y), spot(z, y), ysem.at[2], ysem.at[3], across)
    swap.start()
    order = streams(zs, y)[2:] + streams(zs, y)[:2]
    for st in order[:2]:
        if st[2]:
            send(st, 1)
    remote(spot(z, 1 - y), spot(z, 1 - y), ysem.at[2], ysem.at[3], across).wait_recv()
    for st in order[2:]:
        if st[2]:
            send(st, 1)
    landed(z * 2 + y)
    landed(z * 2 + 1 - y)
    for step in range(1, hops + 1):
        for st in order:
            if step <= st[2]:
                where = arrive(st, step)
                if step < st[2]:
                    send(st, step + 1)
                landed(where)
    swap.wait_send()
    for copy in sent:
        copy.wait_send()


def square_kernel(chips, delta_hbm, sketch_hbm, x_ref, out_ref, delta, sketch, term, sib_buf, half,
                  slots, load_s, core_s, core_r, a_s, a_r, b_s, b_r):
    chip, core, sib = place(chips)
    hello(chips, 0)
    n = x_ref.shape[1]
    part = slots.shape[1]
    side = chips * part
    loads = []
    deep = delta.shape[1] // LOADS
    for i in range(LOADS):
        at = slice(i * deep, (i + 1) * deep)
        loads.append((
            pltpu.make_async_copy(delta_hbm.at[:, at], delta.at[:, at], load_s.at[2 * i]),
            pltpu.make_async_copy(sketch_hbm.at[at], sketch.at[at], load_s.at[2 * i + 1]),
        ))
        for copy in loads[-1]:
            copy.start()
    for i in range(LOADS):
        for copy in loads[i]:
            copy.wait()
        at = slice(i * deep, (i + 1) * deep)
        product = jnp.dot(delta[:, at], sketch[at], preferred_element_type=f32)
        x_ref[...] = x_ref[...] + product if i else product
    across = x_ref[...].T
    top = 0
    for at in range(0, n, 128):
        wide = min(128, n - at)
        piece = dot_nn(across[at:], x_ref[:, at:at + wide])
        if wide < 128:
            piece = jnp.concatenate([piece, jnp.zeros((n - at, 128 - wide), f32)], axis=1)
        term[top:top + n - at] = piece
        top += n - at
    if top < 2 * side:
        term[top:] = jnp.zeros((2 * side - top, 128), f32)
    barrier_wait(chips, 1)

    def of_side(which):
        return pl.ds(pl.multiple_of(which * side, part), side)

    def of_chip(ref, at):
        return ref.at[pl.ds(pl.multiple_of(at * part, part), part)]

    swap = remote(term.at[of_side(1 - core)], sib_buf, core_s.at[0], core_r.at[0], {"row": sib})
    swap.start()
    swap.wait()
    half[...] = term[of_side(core)] + sib_buf[...]
    src, dst = (lambda c: of_chip(half, c)), (lambda d: slots.at[d])
    to_chips(chips, src, dst, a_s, a_r)
    wait_chips(chips, src, dst, a_s, a_r)
    own = pl.ds(pl.multiple_of(chip * part, part), part)
    total = lax.fori_loop(1, chips, lambda d, t: t + slots[d], half[own])
    out_ref[pl.ds(pl.multiple_of((core * chips + chip) * part, part), part)] = total
    src = lambda c: of_chip(out_ref, core * chips + chip)
    to_chips(chips, src, lambda d: src(0), b_s, b_r)
    wait_chips(chips, src, lambda d: of_chip(out_ref, core * chips + around(chip, chips - d, chips)),
               b_s, b_r)
    mine, theirs = out_ref.at[of_side(core)], out_ref.at[of_side(1 - core)]
    swap = remote(mine, mine, core_s.at[1], core_r.at[1], {"row": sib})
    swap.start()
    swap.wait_send()
    remote(mine, theirs, core_s.at[1], core_r.at[1], {"row": sib}).wait_recv()


def sketch_and_square(delta, sketch, chips):
    rows, features = delta.shape
    n = sketch.shape[1]
    packed = sum(n - at for at in range(0, n, 128))
    part = -(-packed // (16 * chips)) * 8
    anywhere = pl.BlockSpec(memory_space=pl.ANY)
    return pl.pallas_call(
        functools.partial(square_kernel, chips),
        out_shape=(jax.ShapeDtypeStruct((rows, n), f32),
                   jax.ShapeDtypeStruct((2 * chips * part, 128), f32)),
        in_specs=[anywhere, anywhere],
        out_specs=(VMEM, VMEM),
        scratch_shapes=[pltpu.VMEM(delta.shape, bf16), pltpu.VMEM(sketch.shape, bf16),
                        pltpu.VMEM((2 * chips * part, 128), f32)]
        + [pltpu.VMEM((chips * part, 128), f32)] * 2
        + [pltpu.VMEM((chips, part, 128), f32), DMA((2 * LOADS,)), DMA((2,)), DMA((2,))]
        + [DMA((chips,))] * 4,
        compiler_params=params(1),
        name="square_sum",
    )(delta, sketch)


def dot_nt(a, b):
    return lax.dot_general(a, b, (((1,), (1,)), ((), ())), precision=highest,
                           preferred_element_type=f32)


def dot_nn(a, b):
    return lax.dot_general(a, b, (((1,), (0,)), ((), ())), precision=highest,
                           preferred_element_type=f32)


def basis_kernel(shrink, packed, x_ref, own_ref, cols, fac, inv):
    n = x_ref.shape[1]
    blocks = n // CB
    row_id = lax.broadcasted_iota(jnp.int32, (CB, 2 * CB), 0)
    lane_id = lax.broadcasted_iota(jnp.int32, (CB, 2 * CB), 1)
    eye = (lane_id == row_id + CB).astype(f32)
    inv[...] = jnp.zeros_like(inv)
    for k in range(blocks):
        wide, off = divmod(k * CB, 128)
        top = sum(n - 128 * w for w in range(wide))
        cols[k, k * CB:, :] = packed[top + off:top + n - 128 * wide, off:off + CB]
    for k in range(blocks):
        at = k * CB
        both = jnp.concatenate([cols[k, at:at + CB, :], jnp.zeros((CB, CB), f32)], axis=1) + eye
        for first in range(0, CB, PANEL):
            wide = [jnp.broadcast_to(both[:, first + m:first + m + 1], both.shape)
                    for m in range(PANEL)]
            for m in range(PANEL):
                j = first + m
                f = jnp.where(row_id > j, wide[m] * (1.0 / wide[m][j:j + 1, :]), 0.0)
                for q in range(m + 1, PANEL):
                    wide[q] = wide[q] - f * wide[q][j:j + 1, :]
                both = both - f * both[j:j + 1, :]
        diag = jnp.sum(jnp.where(lane_id == row_id, both, 0.0), axis=1, keepdims=True)
        zkk = both[:, CB:] * lax.rsqrt(diag)
        if k + 1 < blocks:
            panel = dot_nt(cols[k, at + CB:, :], zkk)
            fac[k, at + CB:, :] = panel
            for j in range(k + 1, blocks):
                off = (j - k - 1) * CB
                cols[j, j * CB:, :] = cols[j, j * CB:, :] - dot_nt(
                    panel[off:, :], panel[off:off + CB, :])
        for c in range(k):
            acc = dot_nn(fac[c, at:at + CB, :], inv[c, c * CB:(c + 1) * CB, :])
            for m in range(c + 1, k):
                acc = acc + dot_nn(fac[m, at:at + CB, :], inv[c, m * CB:(m + 1) * CB, :])
            inv[c, at:at + CB, :] = -dot_nn(zkk, acc)
        inv[k, at:at + CB, :] = zkk
    z = jnp.concatenate([inv[c] for c in range(blocks)], axis=1)
    own_ref[...] = dot_nt(x_ref[...], z) * shrink


def basis_of(packed, sketched, shrink):
    n = sketched.shape[1]
    return pl.pallas_call(
        functools.partial(basis_kernel, shrink),
        out_shape=jax.ShapeDtypeStruct(sketched.shape, f32),
        in_specs=[VMEM, VMEM],
        out_specs=VMEM,
        scratch_shapes=[pltpu.VMEM((n // CB, n, CB), f32)] * 3,
        compiler_params=pltpu.CompilerParams(vmem_limit_bytes=32 * 1024 * 1024),
        name="basis",
    )(packed, sketched)


def start_tasks(tasks, src, dst, ssem, rsem):
    me = lax.axis_index("task")

    def body(d):
        other = around(me, d, tasks)
        remote(src(other), dst(me), ssem.at[d], rsem.at[d], {"task": other}).start()

    loop(1, tasks, body)


def wait_tasks(tasks, src, dst, ssem, rsem):
    me = lax.axis_index("task")

    def body(d):
        other = around(me, d, tasks)
        back = around(me, tasks - d, tasks)
        remote(src(other), dst(back), ssem.at[d], rsem.at[d], {"task": other}).wait()

    loop(1, tasks, body)


def spread(tasks, at, ssem, rsem):
    me = lax.axis_index("task")
    xs = tasks // 2
    x, y = me % xs, me // xs
    sent = []

    def send(n, block, to):
        copy = remote(block, block, ssem.at[n], rsem.at[n], {"task": to})
        copy.start()
        sent.append(copy)

    def arrive(n, block):
        remote(block, block, ssem.at[n], rsem.at[n], {"task": me}).wait_recv()

    def name(xx, yy):
        return yy * xs + xx % xs

    own = at(me)
    send(0, own, name(x, 1 - y))
    for d in range(1, xs):
        send(d, own, name(x + d, y))
    yield
    twin = at(name(x, 1 - y))
    arrive(0, twin)
    yield name(x, 1 - y)
    across = [d for d in range(1, xs) if d == xs // 2]
    along = [d for d in range(1, xs) if d != xs // 2]
    for d in along:
        send(xs + d, twin, name(x + d, y))
    for d in across:
        block = at(name(x + xs - d, y))
        arrive(d, block)
        send(xs + d, block, name(x, 1 - y))
        yield name(x + xs - d, y)
    for d in along:
        block = name(x + xs - d, y)
        arrive(d, at(block))
        yield block
    for d in along + across:
        block = name(x + xs - d, 1 - y)
        arrive(xs + d, at(block))
        yield block
    for copy in sent:
        copy.wait_send()


def pair_tiles(width):
    return 16 * (2 * (width // 128) + (1 if width % 128 else 0))


def pack_pair(one, two):
    width = one.shape[1]
    full = width // 128
    parts = [v[:, i * 128:(i + 1) * 128] for v in (one, two) for i in range(full)]
    if width % 128:
        parts.append(jnp.concatenate([one[:, full * 128:], two[:, full * 128:]], axis=1))
    return jnp.concatenate(parts, axis=0)


def unpack_pair(packed, width):
    full = width // 128
    out = []
    for v in range(2):
        parts = [packed[(v * full + i) * 16:(v * full + i + 1) * 16] for i in range(full)]
        if width % 128:
            parts.append(packed[2 * full * 16:, v * 64:v * 64 + 64])
        out.append(jnp.concatenate(parts, axis=1) if len(parts) > 1 else parts[0])
    return out


def joint_kernel(
    chips, tasks, own_ref, delta_hbm, out_ref, wall_ref,
    delta, turned, stack, packed, terms, sib_buf, half, slots, column, matrix, final,
    slab, slab2, slab3, parts, sib_parts, half2, slots2, other, other_in, mine, block, gathered, wpacked,
    local_s, g_s, g_r, sw_s, sw_r, a_s, a_r, b_s, b_r, c_s, c_r, p_s, p_r, q_s, q_r,
    t1_s, t1_r, t2_s, t2_r, t3_s, t3_r, w_s, w_r, sp_s, sp_r, d_s, d_r, e_s, e_r, y_sem, t4_s, t4_r, f_s, f_r,
):
    chip, core, sib = place(chips)
    me = lax.axis_index("task")
    rows, width = own_ref.shape
    depth = terms.shape[2]
    per = width // depth
    pairs = tasks // 2
    hello(chips, tasks)
    load = pltpu.make_async_copy(delta_hbm, delta, local_s.at[0])
    load.start()
    own = own_ref[...].astype(bf16)
    stack[me] = own
    packed[me] = pack_rows(own)
    barrier_wait(chips, tasks)

    def swap_term(s, i):
        at = pl.ds(s * (per // 2), per // 2)
        return remote(terms.at[at, 1 - core], sib_buf.at[at], sw_s.at[i], sw_r.at[i], {"row": sib})

    def gram_term(s, i):
        term = lax.dot_general(stack[s], stack[me], (((0,), (0,)), ((), ())),
                               preferred_element_type=f32).astype(bf16)
        terms[pl.ds(s * (per // 2), per // 2)] = term.reshape(per // 2, 2, depth, width)
        swap_term(s, i).start()

    def to_owner(s, i):
        swap_term(s, i).wait()
        for e in range(per // 2):
            c = s * (per // 2) + e
            both = terms[c, core].astype(f32) + sib_buf[c].astype(f32)
            half[c] = pack_rows(both).astype(bf16)
            d = around(c, chips - chip, chips)

            @pl.when(c != chip)
            def _():
                remote(half.at[c], slots.at[d], a_s.at[d], a_r.at[d], {"row": c * 2 + core}).start()

    steps = spread(tasks, lambda c: packed.at[c], g_s, g_r)
    next(steps)
    gram_term(me, 0)
    ready = [me]
    for got in steps:
        unpack_to(stack.at[got], packed[got], rows, width)
        ready.append(got)
        gram_term(got, len(ready) - 1)
        to_owner(ready[-2], len(ready) - 2)
    to_owner(ready[-1], len(ready) - 1)
    wait_chips(chips, lambda c: half.at[c], lambda d: slots.at[d], a_s, a_r)
    gram = lax.fori_loop(
        1, chips, lambda d, t: t + slots[d].astype(f32), half[chip].astype(f32))
    first = gram.astype(bf16)
    slab[me] = first
    column[chip, core] = first

    tsrc = lambda c: slab.at[me]
    start_tasks(tasks, tsrc, lambda c: slab.at[c], t1_s, t1_r)

    span = turned.shape[0] // (2 * chips)

    def turn(i):
        at = pl.ds(pl.multiple_of(i * span, span), span)
        turned[at] = delta[:, at].T

    def gather(buf, sems, recvs, ps, pr, number):
        def spot(c, which):
            return buf.at[c, which]

        def pass_on(c):
            return remote(spot(c, core), spot(c, core), ps.at[c], pr.at[c], {"row": sib})

        def place_in(c, which):
            unpack_to(matrix.at[c * 2 + which], buf[c, which], depth, width)

        to_chips(chips, lambda c: spot(chip, core), lambda d: spot(chip, core), sems, recvs)
        pass_on(chip).start()
        place_in(chip, core)
        turn(number * chips)

        def arrival(d):
            turn(number * chips + d)
            c = around(chip, chips - d, chips)
            remote(spot(c, core), spot(c, core), sems.at[d], recvs.at[d], {"row": sib}).wait_recv()
            pass_on(c).start()
            place_in(c, core)

        loop(1, chips, arrival)

        def other_core(d):
            c = around(chip, chips - d, chips)
            remote(spot(c, core), spot(c, 1 - core), ps.at[c], pr.at[c], {"row": sib}).wait_recv()
            place_in(c, 1 - core)

        loop(0, chips, other_core)
        loop(0, chips, lambda c: pass_on(c).wait_send())
        loop(1, chips, lambda d: remote(
            spot(chip, core), spot(chip, core), sems.at[d], recvs.at[d], {"row": sib}).wait_send())

    load.wait()
    gather(column, b_s, b_r, p_s, p_r, 0)
    wait_tasks(tasks, tsrc, lambda c: slab.at[c], t1_s, t1_r)

    def times(left):
        def body(s, total):
            right = matrix[pl.ds(s * per, per)].reshape(width, width)
            return total + jnp.dot(
                unpack_rows(left[s], depth, width), right, preferred_element_type=f32)
        return lax.fori_loop(0, tasks, body, jnp.zeros((depth, width), f32))

    two = pack_rows(times(slab))
    slab2[me] = two.astype(bf16)
    src2 = lambda c: slab2.at[me]
    start_tasks(tasks, src2, lambda c: slab2.at[c], t2_s, t2_r)
    wait_tasks(tasks, src2, lambda c: slab2.at[c], t2_s, t2_r)
    three = pack_rows(times(slab2))
    slab3[me] = three.astype(bf16)
    src3 = lambda c: slab3.at[me]
    start_tasks(tasks, src3, lambda c: slab3.at[c], t3_s, t3_r)
    part = -2.4375 * gram + 1.6875 * two - 0.5625 * three
    wait_tasks(tasks, src3, lambda c: slab3.at[c], t3_s, t3_r)
    final[chip, core] = (part + 0.0625 * pack_rows(times(slab3))).astype(bf16)
    gather(final, c_s, c_r, q_s, q_r, 1)

    def apply(s, total):
        right = matrix[pl.ds(s * per, per)].reshape(width, width)
        return total + jnp.dot(stack[s], right, preferred_element_type=f32)

    weights = lax.fori_loop(0, tasks, apply, 2.25 * own_ref[...]).astype(bf16)
    wall_ref[me] = weights
    wpacked[me] = pack_rows(weights)
    wsteps = spread(tasks, lambda c: wpacked.at[c], w_s, w_r)
    next(wsteps)

    def swap_part(u):
        return remote(parts.at[u, :, 1 - core], sib_parts.at[u], sp_s.at[u], sp_r.at[u], {"row": sib})

    def coef_term(u):
        tall = turned.shape[0] // tasks
        rows_u = turned[pl.ds(pl.multiple_of(u * tall, tall), tall)]
        term = jnp.dot(rows_u, wall_ref[me], preferred_element_type=f32).astype(bf16)
        parts[u] = term.reshape(parts.shape[1:])
        swap_part(u).start()

    loop(0, tasks, coef_term)
    loop(0, tasks, lambda u: swap_part(u).wait())

    def add(c):
        for p in range(pairs):
            one, two = (
                parts[u, c, core].astype(f32) + sib_parts[u, c].astype(f32)
                for u in (2 * p, 2 * p + 1)
            )
            half2[c, p] = pack_pair(one, two).astype(bf16)

    loop(0, chips, add)
    total = ring_reduce(chips, half2, slots2, other, other_in, d_s, d_r, y_sem)
    for p in range(pairs):
        for v, piece in enumerate(unpack_pair(total[p], width)):
            mine[2 * p + v] = piece.astype(bf16)
    block[me] = mine[me]
    tsrc4, tdst4 = (lambda c: mine.at[c]), (lambda c: block.at[c])
    start_tasks(tasks, tsrc4, tdst4, t4_s, t4_r)
    for got in wsteps:
        unpack_to(wall_ref.at[got], wpacked[got], rows, width)
    wait_tasks(tasks, tsrc4, tdst4, t4_s, t4_r)
    for p in range(pairs):
        gathered[core, chip, p] = pack_pair(block[2 * p], block[2 * p + 1])
    seen = []

    def spill(c, which):
        for p in range(pairs):
            for v, piece in enumerate(unpack_pair(gathered[which, c, p], width)):
                out_ref[2 * p + v, c, which] = piece

    def pass_on(c):
        spot = gathered.at[core, c]
        return remote(spot, spot, f_s.at[c], f_r.at[c], {"row": sib})

    def landed(c):
        pass_on(c).start()
        seen.append(c)
        spill(c, core)

    ring_gather(chips, lambda c: gathered.at[core, c], e_s, e_r, y_sem, landed)
    for c in seen:
        remote(gathered.at[core, c], gathered.at[1 - core, c], f_s.at[c], f_r.at[c],
               {"row": sib}).wait_recv()
        spill(c, 1 - core)
    loop(0, chips, lambda c: pass_on(c).wait_send())


def joint(own, delta, chips, tasks):
    rows, width = own.shape
    features = delta.shape[1]
    depth = tasks * width // (2 * chips)
    piece = features // (tasks * chips * 2)
    chunk = (tasks // 2, pair_tiles(width), 128)
    high = tiles(depth, width)[2]
    tall = tiles(rows, width)[2]
    buf = lambda *shape: pltpu.VMEM(shape, bf16)
    pair = lambda n: [DMA((n,)), DMA((n,))]
    return pl.pallas_call(
        functools.partial(joint_kernel, chips, tasks),
        out_shape=(jax.ShapeDtypeStruct((tasks, chips, 2, piece, width), bf16),
                   jax.ShapeDtypeStruct((tasks, rows, width), bf16)),
        in_specs=[VMEM, pl.BlockSpec(memory_space=pl.ANY)],
        out_specs=(VMEM, VMEM),
        scratch_shapes=[
            buf(rows, features), buf(features, rows), buf(tasks, rows, width), buf(tasks, tall, 128),
            buf(chips, 2, depth, width), buf(chips, depth, width), buf(chips, high, 128),
            buf(chips, high, 128), buf(chips, 2, high, 128), buf(chips * 2, depth, width),
            buf(chips, 2, high, 128),
            buf(tasks, high, 128), buf(tasks, high, 128), buf(tasks, high, 128),
            buf(tasks, chips, 2, piece, width), buf(tasks, chips, piece, width),
            buf(chips, *chunk), buf(chips, *chunk), buf(*chunk), buf(*chunk),
            buf(tasks, piece, width), buf(tasks, piece, width), buf(2, chips, *chunk),
            buf(tasks, tall, 128), DMA((1,)),
        ] + pair(tasks) + pair(tasks) + pair(chips) * 5
        + pair(tasks) * 5 + pair(chips) * 2 + [DMA((4,))] + pair(tasks) + pair(chips),
        compiler_params=params(2),
        name="joint",
    )(own, delta)


def local(delta, sketch, base):
    tasks = lax.axis_size("task")
    chips = lax.axis_size("row") // 2
    delta_rows, task_sketch = delta[0], sketch[0]
    width = task_sketch.shape[1]
    sketched, packed = sketch_and_square(delta_rows, task_sketch, chips)
    own = basis_of(packed, sketched, 1.0 / math.sqrt(tasks))
    coefs, stack = joint(own, delta_rows, chips, tasks)
    coefs = coefs.reshape(tasks, -1, width)
    update = lax.dot_general(
        stack, coefs, (((0, 2), (0, 2)), ((), ())), preferred_element_type=f32
    )
    return (base.astype(f32) + update).astype(bf16)


def solution(mesh):
    return jax.shard_map(
        local,
        mesh=mesh,
        in_specs=(P("task", "row", None), P("task", None, None), P("row", "task")),
        out_specs=P("row", "task"),
        check_vma=False,
    )
```

```python
import functools
import math

import jax
import jax.numpy as jnp
from jax import lax
from jax.experimental import pallas as pl
from jax.experimental.pallas import tpu as pltpu
from jax.sharding import PartitionSpec as P

highest = lax.Precision.HIGHEST
MESH = pl.DeviceIdType.MESH
VMEM = pl.BlockSpec(memory_space=pltpu.VMEM)
DMA = pltpu.SemaphoreType.DMA
f32 = jnp.float32
bf16 = jnp.bfloat16
CB = 64
PANEL = 8
LOADS = 4


def params(cid):
    return pltpu.CompilerParams(
        collective_id=cid, has_side_effects=True, vmem_limit_bytes=48 * 1024 * 1024
    )


def place(chips):
    row = lax.axis_index("row")
    chip, core = row // 2, row % 2
    return chip, core, chip * 2 + (1 - core)


def around(me, step, count):
    return (me + step) % count


def remote(src, dst, ssem, rsem, where):
    return pltpu.make_async_remote_copy(
        src_ref=src, dst_ref=dst, send_sem=ssem, recv_sem=rsem,
        device_id=where, device_id_type=MESH,
    )


def loop(lo, hi, body):
    def step(i, carry):
        body(i)
        return carry

    lax.fori_loop(lo, hi, step, 0)


def to_chips(chips, src, dst, ssem, rsem):
    chip, core, _ = place(chips)

    def body(d):
        other = around(chip, d, chips)
        remote(src(other), dst(d), ssem.at[d], rsem.at[d], {"row": other * 2 + core}).start()

    loop(1, chips, body)


def wait_chips(chips, src, dst, ssem, rsem):
    chip, core, _ = place(chips)

    def body(d):
        other = around(chip, d, chips)
        copy = remote(src(other), dst(d), ssem.at[d], rsem.at[d], {"row": other * 2 + core})
        copy.wait()

    loop(1, chips, body)


def tiles(depth, width):
    full = width // 128
    top = -(-depth // 32) * 16 if width % 128 else 0
    return full, top, full * depth + top


def pack_rows(value):
    depth, width = value.shape
    full, top, _ = tiles(depth, width)
    parts = [value[:, i * 128:(i + 1) * 128] for i in range(full)]
    if top:
        tail = value[:, full * 128:]
        low = jnp.concatenate(
            [tail[top:], jnp.zeros((2 * top - depth, 64), value.dtype)], axis=0
        ) if 2 * top > depth else tail[top:]
        parts.append(jnp.concatenate([tail[:top], low], axis=1))
    return jnp.concatenate(parts, axis=0)


def unpack_rows(packed, depth, width):
    full, top, _ = tiles(depth, width)
    parts = [packed[i * depth:(i + 1) * depth] for i in range(full)]
    if top:
        tail = packed[full * depth:full * depth + top]
        parts.append(jnp.concatenate([tail[:, :64], tail[:depth - top, 64:]], axis=0))
    return jnp.concatenate(parts, axis=1)


def unpack_to(dst, packed, depth, width):
    full, top, _ = tiles(depth, width)
    for i in range(full):
        dst[:, i * 128:(i + 1) * 128] = packed[i * depth:(i + 1) * depth]
    if top:
        tail = packed[full * depth:full * depth + top]
        dst[:top, full * 128:] = tail[:, :64]
        dst[top:, full * 128:] = tail[:depth - top, 64:]


def hello(chips, tasks):
    barrier = pltpu.get_barrier_semaphore()
    chip, core, sib = place(chips)
    pl.semaphore_signal(barrier, inc=1, device_id={"row": sib}, device_id_type=MESH)
    loop(1, chips, lambda d: pl.semaphore_signal(
        barrier, inc=1, device_id={"row": around(chip, d, chips) * 2 + core}, device_id_type=MESH))
    if tasks:
        me = lax.axis_index("task")
        loop(1, tasks, lambda d: pl.semaphore_signal(
            barrier, inc=1, device_id={"task": around(me, d, tasks)}, device_id_type=MESH))


def barrier_wait(chips, tasks):
    pl.semaphore_wait(pltpu.get_barrier_semaphore(), chips + tasks - 1)


def line(zs, z, y, core):
    return (((z + zs) % zs) * 2 + y) * 2 + core


def streams(zs, y):
    far, near = zs // 2, zs // 2 - 1
    return [(2, 1, near, 1 - y), (3, -1, far, 1 - y), (0, 1, far, y), (1, -1, near, y)]


def ring_reduce(chips, half, slots, other, other_in, ssem, rsem, ysem):
    chip, core, _ = place(chips)
    zs, z, y = chips // 2, chip // 2, chip % 2
    hops = zs // 2
    sent = []

    def term(zz, yy):
        return half[((zz + zs) % zs) * 2 + yy]

    def send(stream, step, src):
        k, way = stream[0], stream[1]
        n = k * hops + step - 1
        copy = remote(src, slots.at[n], ssem.at[n], rsem.at[n], {"row": line(zs, z + way, y, core)})
        copy.start()
        sent.append(copy)

    def arrive(stream, step):
        n = stream[0] * hops + step - 1
        remote(slots.at[n], slots.at[n], ssem.at[n], rsem.at[n], {"row": line(zs, z, y, core)}).wait_recv()
        return n

    for st in streams(zs, y):
        if st[2]:
            dest = ((z + st[1] * st[2] + zs) % zs) * 2 + st[3]
            send(st, 1, half.at[dest])
    for step in range(1, hops + 1):
        for st in streams(zs, y):
            if step <= st[2]:
                n = arrive(st, step)
                if step < st[2]:
                    dest = z + st[1] * (st[2] - step)
                    slots[n] = (slots[n].astype(f32) + term(dest, st[3]).astype(f32)).astype(bf16)
                    send(st, step + 1, slots.at[n])

    def final(plane, pair):
        total = term(z, plane).astype(f32)
        for k, n in pair:
            if n:
                total = total + slots[k * hops + n - 1].astype(f32)
        return total

    other[...] = final(1 - y, [(2, hops - 1), (3, hops)]).astype(bf16)
    swap = remote(other, other_in, ysem.at[0], ysem.at[1], {"row": line(zs, z, 1 - y, core)})
    swap.start()
    own = final(y, [(0, hops), (1, hops - 1)])
    swap.wait()
    for copy in sent:
        copy.wait_send()
    return own + other_in[...].astype(f32)


def ring_gather(chips, at, ssem, rsem, ysem, landed, between=lambda step: None):
    chip, core, _ = place(chips)
    zs, z, y = chips // 2, chip // 2, chip % 2
    hops = zs // 2
    sent = []

    def spot(zz, yy):
        return at(((zz + zs) % zs) * 2 + yy)

    def send(stream, step):
        k, way, _, yy = stream
        n = k * hops + step - 1
        block = spot(z - way * (step - 1), yy)
        copy = remote(block, block, ssem.at[n], rsem.at[n], {"row": line(zs, z + way, y, core)})
        copy.start()
        sent.append(copy)

    def arrive(stream, step):
        k, way, _, yy = stream
        n = k * hops + step - 1
        where = ((z - way * step + zs) % zs) * 2 + yy
        remote(at(where), at(where), ssem.at[n], rsem.at[n], {"row": line(zs, z, y, core)}).wait_recv()
        return where

    across = {"row": line(zs, z, 1 - y, core)}
    swap = remote(spot(z, y), spot(z, y), ysem.at[2], ysem.at[3], across)
    swap.start()
    order = streams(zs, y)[2:] + streams(zs, y)[:2]
    for st in order[:2]:
        if st[2]:
            send(st, 1)
    remote(spot(z, 1 - y), spot(z, 1 - y), ysem.at[2], ysem.at[3], across).wait_recv()
    for st in order[2:]:
        if st[2]:
            send(st, 1)
    landed(z * 2 + y)
    landed(z * 2 + 1 - y)
    for step in range(1, hops + 1):
        for st in order:
            if step <= st[2]:
                where = arrive(st, step)
                if step < st[2]:
                    send(st, step + 1)
                landed(where)
        between(step)
    swap.wait_send()
    for copy in sent:
        copy.wait_send()


def square_kernel(chips, delta_hbm, sketch_hbm, x_ref, out_ref, delta, sketch, term, sib_buf, half,
                  slots, load_s, core_s, core_r, a_s, a_r, b_s, b_r):
    chip, core, sib = place(chips)
    hello(chips, 0)
    n = x_ref.shape[1]
    part = slots.shape[1]
    side = chips * part
    loads = []
    deep = delta.shape[1] // LOADS
    for i in range(LOADS):
        at = slice(i * deep, (i + 1) * deep)
        loads.append((
            pltpu.make_async_copy(delta_hbm.at[:, at], delta.at[:, at], load_s.at[2 * i]),
            pltpu.make_async_copy(sketch_hbm.at[:, at], sketch.at[:, at], load_s.at[2 * i + 1]),
        ))
        for copy in loads[-1]:
            copy.start()
    for i in range(LOADS):
        for copy in loads[i]:
            copy.wait()
        at = slice(i * deep, (i + 1) * deep)
        product = lax.dot_general(delta[:, at], sketch[:, at], (((1,), (1,)), ((), ())),
                                  preferred_element_type=f32)
        x_ref[...] = x_ref[...] + product if i else product
    across = x_ref[...].T
    top = 0
    for at in range(0, n, 128):
        wide = min(128, n - at)
        piece = dot_nn(across[at:], x_ref[:, at:at + wide])
        if wide < 128:
            piece = jnp.concatenate([piece, jnp.zeros((n - at, 128 - wide), f32)], axis=1)
        term[top:top + n - at] = piece
        top += n - at
    if top < 2 * side:
        term[top:] = jnp.zeros((2 * side - top, 128), f32)
    barrier_wait(chips, 1)

    def of_side(which):
        return pl.ds(pl.multiple_of(which * side, part), side)

    def of_chip(ref, at):
        return ref.at[pl.ds(pl.multiple_of(at * part, part), part)]

    swap = remote(term.at[of_side(1 - core)], sib_buf, core_s.at[0], core_r.at[0], {"row": sib})
    swap.start()
    swap.wait()
    half[...] = term[of_side(core)] + sib_buf[...]
    src, dst = (lambda c: of_chip(half, c)), (lambda d: slots.at[d])
    to_chips(chips, src, dst, a_s, a_r)
    wait_chips(chips, src, dst, a_s, a_r)
    own = pl.ds(pl.multiple_of(chip * part, part), part)
    total = lax.fori_loop(1, chips, lambda d, t: t + slots[d], half[own])
    out_ref[pl.ds(pl.multiple_of((core * chips + chip) * part, part), part)] = total
    src = lambda c: of_chip(out_ref, core * chips + chip)
    to_chips(chips, src, lambda d: src(0), b_s, b_r)
    wait_chips(chips, src, lambda d: of_chip(out_ref, core * chips + around(chip, chips - d, chips)),
               b_s, b_r)
    mine, theirs = out_ref.at[of_side(core)], out_ref.at[of_side(1 - core)]
    swap = remote(mine, mine, core_s.at[1], core_r.at[1], {"row": sib})
    swap.start()
    swap.wait_send()
    remote(mine, theirs, core_s.at[1], core_r.at[1], {"row": sib}).wait_recv()


def sketch_and_square(delta, sketch, chips):
    rows, features = delta.shape
    n = sketch.shape[0]
    packed = sum(n - at for at in range(0, n, 128))
    part = -(-packed // (16 * chips)) * 8
    anywhere = pl.BlockSpec(memory_space=pl.ANY)
    return pl.pallas_call(
        functools.partial(square_kernel, chips),
        out_shape=(jax.ShapeDtypeStruct((rows, n), f32),
                   jax.ShapeDtypeStruct((2 * chips * part, 128), f32)),
        in_specs=[anywhere, anywhere],
        out_specs=(VMEM, VMEM),
        scratch_shapes=[pltpu.VMEM(delta.shape, bf16), pltpu.VMEM(sketch.shape, bf16),
                        pltpu.VMEM((2 * chips * part, 128), f32)]
        + [pltpu.VMEM((chips * part, 128), f32)] * 2
        + [pltpu.VMEM((chips, part, 128), f32), DMA((2 * LOADS,)), DMA((2,)), DMA((2,))]
        + [DMA((chips,))] * 4,
        compiler_params=params(1),
        name="square_sum",
    )(delta, sketch)


def dot_nt(a, b):
    return lax.dot_general(a, b, (((1,), (1,)), ((), ())), precision=highest,
                           preferred_element_type=f32)


def dot_nn(a, b):
    return lax.dot_general(a, b, (((1,), (0,)), ((), ())), precision=highest,
                           preferred_element_type=f32)


def basis_kernel(shrink, packed, x_ref, own_ref, cols, fac, inv):
    n = x_ref.shape[1]
    blocks = n // CB
    row_id = lax.broadcasted_iota(jnp.int32, (CB, 2 * CB), 0)
    lane_id = lax.broadcasted_iota(jnp.int32, (CB, 2 * CB), 1)
    eye = (lane_id == row_id + CB).astype(f32)
    inv[...] = jnp.zeros_like(inv)
    for k in range(blocks):
        wide, off = divmod(k * CB, 128)
        top = sum(n - 128 * w for w in range(wide))
        cols[k, k * CB:, :] = packed[top + off:top + n - 128 * wide, off:off + CB]
    for k in range(blocks):
        at = k * CB
        both = jnp.concatenate([cols[k, at:at + CB, :], jnp.zeros((CB, CB), f32)], axis=1) + eye
        for first in range(0, CB, PANEL):
            wide = [jnp.broadcast_to(both[:, first + m:first + m + 1], both.shape)
                    for m in range(PANEL)]
            for m in range(PANEL):
                j = first + m
                f = jnp.where(row_id > j, wide[m] * (1.0 / wide[m][j:j + 1, :]), 0.0)
                for q in range(m + 1, PANEL):
                    wide[q] = wide[q] - f * wide[q][j:j + 1, :]
                both = both - f * both[j:j + 1, :]
        diag = jnp.sum(jnp.where(lane_id == row_id, both, 0.0), axis=1, keepdims=True)
        zkk = both[:, CB:] * lax.rsqrt(diag)
        if k + 1 < blocks:
            panel = dot_nt(cols[k, at + CB:, :], zkk)
            fac[k, at + CB:, :] = panel
            for j in range(k + 1, blocks):
                off = (j - k - 1) * CB
                cols[j, j * CB:, :] = cols[j, j * CB:, :] - dot_nt(
                    panel[off:, :], panel[off:off + CB, :])
        for c in range(k):
            acc = dot_nn(fac[c, at:at + CB, :], inv[c, c * CB:(c + 1) * CB, :])
            for m in range(c + 1, k):
                acc = acc + dot_nn(fac[m, at:at + CB, :], inv[c, m * CB:(m + 1) * CB, :])
            inv[c, at:at + CB, :] = -dot_nn(zkk, acc)
        inv[k, at:at + CB, :] = zkk
    z = jnp.concatenate([inv[c] for c in range(blocks)], axis=1)
    own_ref[...] = dot_nt(x_ref[...], z) * shrink


def basis_of(packed, sketched, shrink):
    n = sketched.shape[1]
    return pl.pallas_call(
        functools.partial(basis_kernel, shrink),
        out_shape=jax.ShapeDtypeStruct(sketched.shape, f32),
        in_specs=[VMEM, VMEM],
        out_specs=VMEM,
        scratch_shapes=[pltpu.VMEM((n // CB, n, CB), f32)] * 3,
        compiler_params=pltpu.CompilerParams(vmem_limit_bytes=32 * 1024 * 1024),
        name="basis",
    )(packed, sketched)


def start_tasks(tasks, src, dst, ssem, rsem):
    me = lax.axis_index("task")

    def body(d):
        other = around(me, d, tasks)
        remote(src(other), dst(me), ssem.at[d], rsem.at[d], {"task": other}).start()

    loop(1, tasks, body)


def wait_tasks(tasks, src, dst, ssem, rsem):
    me = lax.axis_index("task")

    def body(d):
        other = around(me, d, tasks)
        back = around(me, tasks - d, tasks)
        remote(src(other), dst(back), ssem.at[d], rsem.at[d], {"task": other}).wait()

    loop(1, tasks, body)


def spread(tasks, at, ssem, rsem):
    me = lax.axis_index("task")
    xs = tasks // 2
    x, y = me % xs, me // xs
    sent = []

    def send(n, block, to):
        copy = remote(block, block, ssem.at[n], rsem.at[n], {"task": to})
        copy.start()
        sent.append(copy)

    def arrive(n, block):
        remote(block, block, ssem.at[n], rsem.at[n], {"task": me}).wait_recv()

    def name(xx, yy):
        return yy * xs + xx % xs

    own = at(me)
    send(0, own, name(x, 1 - y))
    for d in range(1, xs):
        send(d, own, name(x + d, y))
    yield
    twin = at(name(x, 1 - y))
    arrive(0, twin)
    yield name(x, 1 - y)
    across = [d for d in range(1, xs) if d == xs // 2]
    along = [d for d in range(1, xs) if d != xs // 2]
    for d in along:
        send(xs + d, twin, name(x + d, y))
    for d in across:
        block = at(name(x + xs - d, y))
        arrive(d, block)
        send(xs + d, block, name(x, 1 - y))
        yield name(x + xs - d, y)
    for d in along:
        block = name(x + xs - d, y)
        arrive(d, at(block))
        yield block
    for d in along + across:
        block = name(x + xs - d, 1 - y)
        arrive(xs + d, at(block))
        yield block
    for copy in sent:
        copy.wait_send()


def pair_tiles(width):
    return 16 * (2 * (width // 128) + (1 if width % 128 else 0))


def pack_pair(one, two):
    width = one.shape[1]
    full = width // 128
    parts = [v[:, i * 128:(i + 1) * 128] for v in (one, two) for i in range(full)]
    if width % 128:
        parts.append(jnp.concatenate([one[:, full * 128:], two[:, full * 128:]], axis=1))
    return jnp.concatenate(parts, axis=0)


def unpack_pair(packed, width):
    full = width // 128
    out = []
    for v in range(2):
        parts = [packed[(v * full + i) * 16:(v * full + i + 1) * 16] for i in range(full)]
        if width % 128:
            parts.append(packed[2 * full * 16:, v * 64:v * 64 + 64])
        out.append(jnp.concatenate(parts, axis=1) if len(parts) > 1 else parts[0])
    return out


def joint_kernel(
    chips, tasks, own_ref, delta_hbm, out_ref, wall_ref,
    delta, turned, stack, packed, terms, sib_buf, half, slots, column, matrix, final,
    slab, slab2, slab3, parts, sib_parts, half2, slots2, other, other_in, mine, block, gathered, wpacked,
    local_s, g_s, g_r, sw_s, sw_r, a_s, a_r, b_s, b_r, c_s, c_r, power, total_w, y1_s, y2_s, p_s, p_r, q_s, q_r,
    t1_s, t1_r, t2_s, t2_r, t3_s, t3_r, w_s, w_r, sp_s, sp_r, d_s, d_r, e_s, e_r, y_sem, t4_s, t4_r, f_s, f_r,
):
    chip, core, sib = place(chips)
    me = lax.axis_index("task")
    rows, width = own_ref.shape
    depth = terms.shape[2]
    per = width // depth
    pairs = tasks // 2
    hello(chips, tasks)
    load = pltpu.make_async_copy(delta_hbm, delta, local_s.at[0])
    load.start()
    own = own_ref[...].astype(bf16)
    stack[me] = own
    packed[me] = pack_rows(own)
    barrier_wait(chips, tasks)

    def swap_term(s, i):
        at = pl.ds(s * (per // 2), per // 2)
        return remote(terms.at[at, 1 - core], sib_buf.at[at], sw_s.at[i], sw_r.at[i], {"row": sib})

    def gram_term(s, i):
        term = lax.dot_general(stack[s], stack[me], (((0,), (0,)), ((), ())),
                               preferred_element_type=f32).astype(bf16)
        terms[pl.ds(s * (per // 2), per // 2)] = term.reshape(per // 2, 2, depth, width)
        swap_term(s, i).start()

    def to_owner(s, i):
        swap_term(s, i).wait()
        for e in range(per // 2):
            c = s * (per // 2) + e
            both = terms[c, core].astype(f32) + sib_buf[c].astype(f32)
            half[c] = pack_rows(both).astype(bf16)
            d = around(c, chips - chip, chips)

            @pl.when(c != chip)
            def _():
                remote(half.at[c], slots.at[d], a_s.at[d], a_r.at[d], {"row": c * 2 + core}).start()

    load.wait()
    span = turned.shape[0] // (2 * chips)
    turned_count = [0]

    def turns(n):
        for _ in range(n):
            i = turned_count[0]
            if i < 2 * chips:
                turned[i * span:(i + 1) * span] = delta[:, i * span:(i + 1) * span].T
                turned_count[0] += 1

    steps = spread(tasks, lambda c: packed.at[c], g_s, g_r)
    next(steps)
    gram_term(me, 0)
    ready = [me]
    for got in steps:
        unpack_to(stack.at[got], packed[got], rows, width)
        ready.append(got)
        gram_term(got, len(ready) - 1)
        turns(2)
        to_owner(ready[-2], len(ready) - 2)
    to_owner(ready[-1], len(ready) - 1)
    wait_chips(chips, lambda c: half.at[c], lambda d: slots.at[d], a_s, a_r)
    gram = lax.fori_loop(
        1, chips, lambda d, t: t + slots[d].astype(f32), half[chip].astype(f32))
    first = gram.astype(bf16)
    slab[me] = first

    tsrc = lambda c: slab.at[me]
    start_tasks(tasks, tsrc, lambda c: slab.at[c], t1_s, t1_r)

    def gather(buf, sems, recvs, ys, ps, pr, prepare, use):
        seen, used = [], []

        def pass_on(c):
            return remote(buf.at[c, core], buf.at[c, core], ps.at[c], pr.at[c], {"row": sib})

        def landed(c):
            pass_on(c).start()
            seen.append(c)
            unpack_to(matrix.at[c * 2 + core], buf[c, core], depth, width)

        def finish(upto):
            for c in seen[len(used):upto]:
                remote(buf.at[c, core], buf.at[c, 1 - core], ps.at[c], pr.at[c], {"row": sib}).wait_recv()
                unpack_to(matrix.at[c * 2 + 1 - core], buf[c, 1 - core], depth, width)
                used.append(c)

        def between(step):
            if step == 1:
                prepare()
            finish(2 + 4 * (step - 1))
            whole()
            turns(1)

        tasks_used = []

        def whole():
            if per != 4:
                return
            zs, z = chips // 2, chip // 2
            order = [0]
            for step in range(1, zs // 2):
                order += [-step, step]
            order += [zs // 2]
            for n, off in enumerate(order):
                needs = 2 if n == 0 else 2 + 4 * ((n + 1) // 2)
                if n == len(order) - 1:
                    needs = chips
                if n not in tasks_used and len(used) >= needs:
                    tasks_used.append(n)
                    use((z + off + zs) % zs)

        ring_gather(chips, lambda c: buf.at[c, core], sems, recvs, ys, landed, between)
        finish(chips)
        whole()
        if per != 4:
            loop(0, tasks, use)
        loop(0, chips, lambda c: pass_on(c).wait_send())

    def times_one(left, s):
        right = matrix[pl.ds(s * per, per)].reshape(width, width)
        return jnp.dot(unpack_rows(left[s], depth, width), right, preferred_element_type=f32)

    def square_one(s):
        power[...] += times_one(slab, s)

    def times(left):
        return lax.fori_loop(
            0, tasks, lambda s, total: total + times_one(left, s), jnp.zeros((depth, width), f32))

    power[...] = jnp.zeros_like(power)
    column[chip, core] = first
    gather(column, b_s, b_r, y1_s, p_s, p_r,
           lambda: wait_tasks(tasks, tsrc, lambda c: slab.at[c], t1_s, t1_r), square_one)
    two = pack_rows(power[...])
    slab2[me] = two.astype(bf16)
    src2 = lambda c: slab2.at[me]
    start_tasks(tasks, src2, lambda c: slab2.at[c], t2_s, t2_r)
    turns(5)
    wait_tasks(tasks, src2, lambda c: slab2.at[c], t2_s, t2_r)
    three = pack_rows(times(slab2))
    slab3[me] = three.astype(bf16)
    src3 = lambda c: slab3.at[me]
    start_tasks(tasks, src3, lambda c: slab3.at[c], t3_s, t3_r)
    part = -2.4375 * gram + 1.6875 * two - 0.5625 * three
    turns(5)
    wait_tasks(tasks, src3, lambda c: slab3.at[c], t3_s, t3_r)
    final[chip, core] = (part + 0.0625 * pack_rows(times(slab3))).astype(bf16)

    def apply(s):
        right = matrix[pl.ds(s * per, per)].reshape(width, width)
        total_w[...] += jnp.dot(stack[s], right, preferred_element_type=f32)

    total_w[...] = 2.25 * own_ref[...]
    gather(final, c_s, c_r, y2_s, q_s, q_r, lambda: None, apply)
    weights = total_w[...].astype(bf16)
    wall_ref[me] = weights
    wpacked[me] = pack_rows(weights)
    wsteps = spread(tasks, lambda c: wpacked.at[c], w_s, w_r)
    next(wsteps)

    def swap_part(u):
        return remote(parts.at[u, :, 1 - core], sib_parts.at[u], sp_s.at[u], sp_r.at[u], {"row": sib})

    def coef_term(u):
        tall = turned.shape[0] // tasks
        rows_u = turned[pl.ds(pl.multiple_of(u * tall, tall), tall)]
        term = jnp.dot(rows_u, wall_ref[me], preferred_element_type=f32).astype(bf16)
        parts[u] = term.reshape(parts.shape[1:])
        swap_part(u).start()

    turns(2 * chips)
    loop(0, tasks, coef_term)
    loop(0, tasks, lambda u: swap_part(u).wait())

    def add(c):
        for p in range(pairs):
            one, two = (
                parts[u, c, core].astype(f32) + sib_parts[u, c].astype(f32)
                for u in (2 * p, 2 * p + 1)
            )
            half2[c, p] = pack_pair(one, two).astype(bf16)

    loop(0, chips, add)
    total = ring_reduce(chips, half2, slots2, other, other_in, d_s, d_r, y_sem)
    for p in range(pairs):
        for v, piece in enumerate(unpack_pair(total[p], width)):
            mine[2 * p + v] = piece.astype(bf16)
    block[me] = mine[me]
    tsrc4, tdst4 = (lambda c: mine.at[c]), (lambda c: block.at[c])
    start_tasks(tasks, tsrc4, tdst4, t4_s, t4_r)
    for got in wsteps:
        unpack_to(wall_ref.at[got], wpacked[got], rows, width)
    wait_tasks(tasks, tsrc4, tdst4, t4_s, t4_r)
    for p in range(pairs):
        gathered[core, chip, p] = pack_pair(block[2 * p], block[2 * p + 1])
    seen = []

    def spill(c, which):
        for p in range(pairs):
            for v, piece in enumerate(unpack_pair(gathered[which, c, p], width)):
                out_ref[2 * p + v, c, which] = piece

    def pass_on(c):
        spot = gathered.at[core, c]
        return remote(spot, spot, f_s.at[c], f_r.at[c], {"row": sib})

    def landed(c):
        pass_on(c).start()
        seen.append(c)
        spill(c, core)

    ring_gather(chips, lambda c: gathered.at[core, c], e_s, e_r, y_sem, landed)
    for c in seen:
        remote(gathered.at[core, c], gathered.at[1 - core, c], f_s.at[c], f_r.at[c],
               {"row": sib}).wait_recv()
        spill(c, 1 - core)
    loop(0, chips, lambda c: pass_on(c).wait_send())


def joint(own, delta, chips, tasks):
    rows, width = own.shape
    features = delta.shape[1]
    depth = tasks * width // (2 * chips)
    piece = features // (tasks * chips * 2)
    chunk = (tasks // 2, pair_tiles(width), 128)
    high = tiles(depth, width)[2]
    tall = tiles(rows, width)[2]
    buf = lambda *shape: pltpu.VMEM(shape, bf16)
    pair = lambda n: [DMA((n,)), DMA((n,))]
    return pl.pallas_call(
        functools.partial(joint_kernel, chips, tasks),
        out_shape=(jax.ShapeDtypeStruct((tasks, chips, 2, piece, width), bf16),
                   jax.ShapeDtypeStruct((tasks, rows, width), bf16)),
        in_specs=[VMEM, pl.BlockSpec(memory_space=pl.ANY)],
        out_specs=(VMEM, VMEM),
        scratch_shapes=[
            buf(rows, features), buf(features, rows), buf(tasks, rows, width), buf(tasks, tall, 128),
            buf(chips, 2, depth, width), buf(chips, depth, width), buf(chips, high, 128),
            buf(chips, high, 128), buf(chips, 2, high, 128), buf(chips * 2, depth, width),
            buf(chips, 2, high, 128),
            buf(tasks, high, 128), buf(tasks, high, 128), buf(tasks, high, 128),
            buf(tasks, chips, 2, piece, width), buf(tasks, chips, piece, width),
            buf(chips, *chunk), buf(chips, *chunk), buf(*chunk), buf(*chunk),
            buf(tasks, piece, width), buf(tasks, piece, width), buf(2, chips, *chunk),
            buf(tasks, tall, 128), DMA((1,)),
        ] + pair(tasks) + pair(tasks) + pair(chips) * 3
        + [pltpu.VMEM((depth, width), f32), pltpu.VMEM((rows, width), f32), DMA((4,)), DMA((4,))]
        + pair(chips) * 2
        + pair(tasks) * 5 + pair(chips) * 2 + [DMA((4,))] + pair(tasks) + pair(chips),
        compiler_params=params(2),
        name="joint",
    )(own, delta)


def local(delta, sketch, base):
    tasks = lax.axis_size("task")
    chips = lax.axis_size("row") // 2
    delta_rows, task_sketch = delta[0], sketch[0]
    width = task_sketch.shape[1]
    sketched, packed = sketch_and_square(delta_rows, task_sketch.T, chips)
    own = basis_of(packed, sketched, 1.0 / math.sqrt(tasks))
    coefs, stack = joint(own, delta_rows, chips, tasks)
    coefs = coefs.reshape(tasks, -1, width)
    update = lax.dot_general(
        stack, coefs, (((0, 2), (0, 2)), ((), ())), preferred_element_type=f32
    )
    return (base.astype(f32) + update).astype(bf16)


def solution(mesh):
    return jax.shard_map(
        local,
        mesh=mesh,
        in_specs=(P("task", "row", None), P("task", None, None), P("row", "task")),
        out_specs=P("row", "task"),
        check_vma=False,
    )
```

```python
import functools
import math

import jax
import jax.numpy as jnp
from jax import lax
from jax.experimental import pallas as pl
from jax.experimental.pallas import tpu as pltpu
from jax.sharding import PartitionSpec as P

highest = lax.Precision.HIGHEST
MESH = pl.DeviceIdType.MESH
VMEM = pl.BlockSpec(memory_space=pltpu.VMEM)
DMA = pltpu.SemaphoreType.DMA
f32 = jnp.float32
bf16 = jnp.bfloat16
CB = 64
PANEL = 8
LOADS = 4


def params(cid):
    return pltpu.CompilerParams(
        collective_id=cid, has_side_effects=True, vmem_limit_bytes=56 * 1024 * 1024
    )


def place(chips):
    row = lax.axis_index("row")
    chip, core = row // 2, row % 2
    return chip, core, chip * 2 + (1 - core)


def around(me, step, count):
    return (me + step) % count


def remote(src, dst, ssem, rsem, where):
    return pltpu.make_async_remote_copy(
        src_ref=src, dst_ref=dst, send_sem=ssem, recv_sem=rsem,
        device_id=where, device_id_type=MESH,
    )


def loop(lo, hi, body):
    def step(i, carry):
        body(i)
        return carry

    lax.fori_loop(lo, hi, step, 0)


def to_chips(chips, src, dst, ssem, rsem):
    chip, core, _ = place(chips)

    def body(d):
        other = around(chip, d, chips)
        remote(src(other), dst(d), ssem.at[d], rsem.at[d], {"row": other * 2 + core}).start()

    loop(1, chips, body)


def wait_chips(chips, src, dst, ssem, rsem):
    chip, core, _ = place(chips)

    def body(d):
        other = around(chip, d, chips)
        copy = remote(src(other), dst(d), ssem.at[d], rsem.at[d], {"row": other * 2 + core})
        copy.wait()

    loop(1, chips, body)


def tiles(depth, width):
    full = width // 128
    top = -(-depth // 32) * 16 if width % 128 else 0
    return full, top, full * depth + top


def pack_rows(value):
    depth, width = value.shape
    full, top, _ = tiles(depth, width)
    parts = [value[:, i * 128:(i + 1) * 128] for i in range(full)]
    if top:
        tail = value[:, full * 128:]
        low = jnp.concatenate(
            [tail[top:], jnp.zeros((2 * top - depth, 64), value.dtype)], axis=0
        ) if 2 * top > depth else tail[top:]
        parts.append(jnp.concatenate([tail[:top], low], axis=1))
    return jnp.concatenate(parts, axis=0)


def unpack_rows(packed, depth, width):
    full, top, _ = tiles(depth, width)
    parts = [packed[i * depth:(i + 1) * depth] for i in range(full)]
    if top:
        tail = packed[full * depth:full * depth + top]
        parts.append(jnp.concatenate([tail[:, :64], tail[:depth - top, 64:]], axis=0))
    return jnp.concatenate(parts, axis=1)


def unpack_to(dst, packed, depth, width):
    full, top, _ = tiles(depth, width)
    for i in range(full):
        dst[:, i * 128:(i + 1) * 128] = packed[i * depth:(i + 1) * depth]
    if top:
        tail = packed[full * depth:full * depth + top]
        dst[:top, full * 128:] = tail[:, :64]
        dst[top:, full * 128:] = tail[:depth - top, 64:]


def hello(chips, tasks):
    barrier = pltpu.get_barrier_semaphore()
    chip, core, sib = place(chips)
    pl.semaphore_signal(barrier, inc=1, device_id={"row": sib}, device_id_type=MESH)
    loop(1, chips, lambda d: pl.semaphore_signal(
        barrier, inc=1, device_id={"row": around(chip, d, chips) * 2 + core}, device_id_type=MESH))
    if tasks:
        me = lax.axis_index("task")
        loop(1, tasks, lambda d: pl.semaphore_signal(
            barrier, inc=1, device_id={"task": around(me, d, tasks)}, device_id_type=MESH))


def barrier_wait(chips, tasks):
    pl.semaphore_wait(pltpu.get_barrier_semaphore(), chips + tasks - 1)


def line(zs, z, y, core):
    return (((z + zs) % zs) * 2 + y) * 2 + core


def streams(zs, y):
    far, near = zs // 2, zs // 2 - 1
    return [(2, 1, near, 1 - y), (3, -1, far, 1 - y), (0, 1, far, y), (1, -1, near, y)]


def ring_reduce(chips, half, slots, other, other_in, ssem, rsem, ysem, between):
    chip, core, _ = place(chips)
    zs, z, y = chips // 2, chip // 2, chip % 2
    hops = zs // 2
    sent = []

    def term(zz, yy):
        return half[((zz + zs) % zs) * 2 + yy]

    def send(stream, step, src):
        k, way = stream[0], stream[1]
        n = k * hops + step - 1
        copy = remote(src, slots.at[n], ssem.at[n], rsem.at[n], {"row": line(zs, z + way, y, core)})
        copy.start()
        sent.append(copy)

    def arrive(stream, step):
        n = stream[0] * hops + step - 1
        remote(slots.at[n], slots.at[n], ssem.at[n], rsem.at[n], {"row": line(zs, z, y, core)}).wait_recv()
        return n

    for st in streams(zs, y):
        if st[2]:
            dest = ((z + st[1] * st[2] + zs) % zs) * 2 + st[3]
            send(st, 1, half.at[dest])
    for step in range(1, hops + 1):
        for st in streams(zs, y):
            if step <= st[2]:
                n = arrive(st, step)
                if step < st[2]:
                    dest = z + st[1] * (st[2] - step)
                    slots[n] = (slots[n].astype(f32) + term(dest, st[3]).astype(f32)).astype(bf16)
                    send(st, step + 1, slots.at[n])
        between()

    def final(plane, pair):
        total = term(z, plane).astype(f32)
        for k, n in pair:
            if n:
                total = total + slots[k * hops + n - 1].astype(f32)
        return total

    other[...] = final(1 - y, [(2, hops - 1), (3, hops)]).astype(bf16)
    swap = remote(other, other_in, ysem.at[0], ysem.at[1], {"row": line(zs, z, 1 - y, core)})
    swap.start()
    own = final(y, [(0, hops), (1, hops - 1)])
    swap.wait()
    for copy in sent:
        copy.wait_send()
    return own + other_in[...].astype(f32)


def ring_gather(chips, at, ssem, rsem, ysem, landed, between=lambda step: None):
    chip, core, _ = place(chips)
    zs, z, y = chips // 2, chip // 2, chip % 2
    hops = zs // 2
    sent = []

    def spot(zz, yy):
        return at(((zz + zs) % zs) * 2 + yy)

    def send(stream, step):
        k, way, _, yy = stream
        n = k * hops + step - 1
        block = spot(z - way * (step - 1), yy)
        copy = remote(block, block, ssem.at[n], rsem.at[n], {"row": line(zs, z + way, y, core)})
        copy.start()
        sent.append(copy)

    def arrive(stream, step):
        k, way, _, yy = stream
        n = k * hops + step - 1
        where = ((z - way * step + zs) % zs) * 2 + yy
        remote(at(where), at(where), ssem.at[n], rsem.at[n], {"row": line(zs, z, y, core)}).wait_recv()
        return where

    across = {"row": line(zs, z, 1 - y, core)}
    swap = remote(spot(z, y), spot(z, y), ysem.at[2], ysem.at[3], across)
    swap.start()
    order = streams(zs, y)[2:] + streams(zs, y)[:2]
    for st in order[:2]:
        if st[2]:
            send(st, 1)
    remote(spot(z, 1 - y), spot(z, 1 - y), ysem.at[2], ysem.at[3], across).wait_recv()
    for st in order[2:]:
        if st[2]:
            send(st, 1)
    landed(z * 2 + y)
    landed(z * 2 + 1 - y)
    for step in range(1, hops + 1):
        new = []
        for st in order:
            if step <= st[2]:
                new.append(arrive(st, step))
                if step < st[2]:
                    send(st, step + 1)
        for where in new:
            landed(where)
        between(step)
    swap.wait_send()
    for copy in sent:
        copy.wait_send()


def square_stage(chips, tasks, turns, delta_hbm, sketch_hbm, x_ref, out_ref, delta, sketch, term,
                 sib_buf, half, slots, load_s, core_s, core_r, a_s, a_r, b_s, b_r):
    chip, core, sib = place(chips)
    hello(chips, tasks)
    n = x_ref.shape[1]
    part = slots.shape[1]
    side = chips * part
    loads = []
    deep = delta.shape[1] // LOADS
    for i in range(LOADS):
        at = slice(i * deep, (i + 1) * deep)
        loads.append((
            pltpu.make_async_copy(delta_hbm.at[:, at], delta.at[:, at], load_s.at[2 * i]),
            pltpu.make_async_copy(sketch_hbm.at[:, at], sketch.at[:, at], load_s.at[2 * i + 1]),
        ))
        for copy in loads[-1]:
            copy.start()
    for i in range(LOADS):
        for copy in loads[i]:
            copy.wait()
        at = slice(i * deep, (i + 1) * deep)
        product = lax.dot_general(delta[:, at], sketch[:, at], (((1,), (1,)), ((), ())),
                                  preferred_element_type=f32)
        x_ref[...] = x_ref[...] + product if i else product
    across = x_ref[...].T
    top = 0
    for at in range(0, n, 128):
        wide = min(128, n - at)
        piece = dot_nn(across[at:], x_ref[:, at:at + wide])
        if wide < 128:
            piece = jnp.concatenate([piece, jnp.zeros((n - at, 128 - wide), f32)], axis=1)
        term[top:top + n - at] = piece
        top += n - at
    if top < 2 * side:
        term[top:] = jnp.zeros((2 * side - top, 128), f32)
    turns(4)
    barrier_wait(chips, tasks)

    def of_side(which):
        return pl.ds(pl.multiple_of(which * side, part), side)

    def of_chip(ref, at):
        return ref.at[pl.ds(pl.multiple_of(at * part, part), part)]

    swap = remote(term.at[of_side(1 - core)], sib_buf, core_s.at[0], core_r.at[0], {"row": sib})
    swap.start()
    turns(2)
    swap.wait()
    half[...] = term[of_side(core)] + sib_buf[...]
    src, dst = (lambda c: of_chip(half, c)), (lambda d: slots.at[d])
    to_chips(chips, src, dst, a_s, a_r)
    turns(6)
    wait_chips(chips, src, dst, a_s, a_r)
    own = pl.ds(pl.multiple_of(chip * part, part), part)
    total = lax.fori_loop(1, chips, lambda d, t: t + slots[d], half[own])
    out_ref[pl.ds(pl.multiple_of((core * chips + chip) * part, part), part)] = total
    src = lambda c: of_chip(out_ref, core * chips + chip)
    to_chips(chips, src, lambda d: src(0), b_s, b_r)
    turns(6)
    wait_chips(chips, src, lambda d: of_chip(out_ref, core * chips + around(chip, chips - d, chips)),
               b_s, b_r)
    mine, theirs = out_ref.at[of_side(core)], out_ref.at[of_side(1 - core)]
    swap = remote(mine, mine, core_s.at[1], core_r.at[1], {"row": sib})
    swap.start()
    turns(2)
    swap.wait_send()
    remote(mine, theirs, core_s.at[1], core_r.at[1], {"row": sib}).wait_recv()


def square_scratch(delta, sketch, chips):
    n = sketch.shape[0]
    packed = sum(n - at for at in range(0, n, 128))
    part = -(-packed // (16 * chips)) * 8
    return [pltpu.VMEM((delta.shape[0], n), f32), pltpu.VMEM((2 * chips * part, 128), f32),
            pltpu.VMEM(delta.shape, bf16), pltpu.VMEM(sketch.shape, bf16),
            pltpu.VMEM((2 * chips * part, 128), f32)] + [pltpu.VMEM((chips * part, 128), f32)] * 2 + [
            pltpu.VMEM((chips, part, 128), f32), DMA((2 * LOADS,)), DMA((2,)), DMA((2,))
    ] + [DMA((chips,))] * 4


def dot_nt(a, b):
    return lax.dot_general(a, b, (((1,), (1,)), ((), ())), precision=highest,
                           preferred_element_type=f32)


def dot_nn(a, b):
    return lax.dot_general(a, b, (((1,), (0,)), ((), ())), precision=highest,
                           preferred_element_type=f32)


def basis_stage(shrink, packed, x_ref, own_ref, cols, fac, inv):
    n = x_ref.shape[1]
    blocks = n // CB
    row_id = lax.broadcasted_iota(jnp.int32, (CB, 2 * CB), 0)
    lane_id = lax.broadcasted_iota(jnp.int32, (CB, 2 * CB), 1)
    eye = (lane_id == row_id + CB).astype(f32)
    inv[...] = jnp.zeros_like(inv)
    for k in range(blocks):
        wide, off = divmod(k * CB, 128)
        top = sum(n - 128 * w for w in range(wide))
        cols[k, k * CB:, :] = packed[top + off:top + n - 128 * wide, off:off + CB]
    for k in range(blocks):
        at = k * CB
        both = jnp.concatenate([cols[k, at:at + CB, :], jnp.zeros((CB, CB), f32)], axis=1) + eye
        for first in range(0, CB, PANEL):
            wide = [jnp.broadcast_to(both[:, first + m:first + m + 1], both.shape)
                    for m in range(PANEL)]
            for m in range(PANEL):
                j = first + m
                f = jnp.where(row_id > j, wide[m] * (1.0 / wide[m][j:j + 1, :]), 0.0)
                for q in range(m + 1, PANEL):
                    wide[q] = wide[q] - f * wide[q][j:j + 1, :]
                both = both - f * both[j:j + 1, :]
        diag = jnp.sum(jnp.where(lane_id == row_id, both, 0.0), axis=1, keepdims=True)
        zkk = both[:, CB:] * lax.rsqrt(diag)
        if k + 1 < blocks:
            panel = dot_nt(cols[k, at + CB:, :], zkk)
            fac[k, at + CB:, :] = panel
            for j in range(k + 1, blocks):
                off = (j - k - 1) * CB
                cols[j, j * CB:, :] = cols[j, j * CB:, :] - dot_nt(
                    panel[off:, :], panel[off:off + CB, :])
        for c in range(k):
            acc = dot_nn(fac[c, at:at + CB, :], inv[c, c * CB:(c + 1) * CB, :])
            for m in range(c + 1, k):
                acc = acc + dot_nn(fac[m, at:at + CB, :], inv[c, m * CB:(m + 1) * CB, :])
            inv[c, at:at + CB, :] = -dot_nn(zkk, acc)
        inv[k, at:at + CB, :] = zkk
    z = jnp.concatenate([inv[c] for c in range(blocks)], axis=1)
    own_ref[...] = dot_nt(x_ref[...], z) * shrink


def start_tasks(tasks, src, dst, ssem, rsem):
    me = lax.axis_index("task")

    def body(d):
        other = around(me, d, tasks)
        remote(src(other), dst(me), ssem.at[d], rsem.at[d], {"task": other}).start()

    loop(1, tasks, body)


def wait_tasks(tasks, src, dst, ssem, rsem):
    me = lax.axis_index("task")

    def body(d):
        other = around(me, d, tasks)
        back = around(me, tasks - d, tasks)
        remote(src(other), dst(back), ssem.at[d], rsem.at[d], {"task": other}).wait()

    loop(1, tasks, body)


def spread(tasks, at, ssem, rsem):
    me = lax.axis_index("task")
    xs = tasks // 2
    x, y = me % xs, me // xs
    sent = []

    def send(n, block, to):
        copy = remote(block, block, ssem.at[n], rsem.at[n], {"task": to})
        copy.start()
        sent.append(copy)

    def arrive(n, block):
        remote(block, block, ssem.at[n], rsem.at[n], {"task": me}).wait_recv()

    def name(xx, yy):
        return yy * xs + xx % xs

    own = at(me)
    send(0, own, name(x, 1 - y))
    for d in range(1, xs):
        send(d, own, name(x + d, y))
    yield
    twin = at(name(x, 1 - y))
    across = [d for d in range(1, xs) if d == xs // 2]
    along = [d for d in range(1, xs) if d != xs // 2]
    arrive(0, twin)
    for d in along:
        send(xs + d, twin, name(x + d, y))
    yield name(x, 1 - y)
    for d in across:
        block = at(name(x + xs - d, y))
        arrive(d, block)
        send(xs + d, block, name(x, 1 - y))
        yield name(x + xs - d, y)
    for d in along:
        block = name(x + xs - d, y)
        arrive(d, at(block))
        yield block
    for d in along + across:
        block = name(x + xs - d, 1 - y)
        arrive(xs + d, at(block))
        yield block
    for copy in sent:
        copy.wait_send()


def pair_tiles(width):
    return 16 * (2 * (width // 128) + (1 if width % 128 else 0))


def pack_pair(one, two):
    width = one.shape[1]
    full = width // 128
    parts = [v[:, i * 128:(i + 1) * 128] for v in (one, two) for i in range(full)]
    if width % 128:
        parts.append(jnp.concatenate([one[:, full * 128:], two[:, full * 128:]], axis=1))
    return jnp.concatenate(parts, axis=0)


def unpack_pair(packed, width):
    full = width // 128
    out = []
    for v in range(2):
        parts = [packed[(v * full + i) * 16:(v * full + i + 1) * 16] for i in range(full)]
        if width % 128:
            parts.append(packed[2 * full * 16:, v * 64:v * 64 + 64])
        out.append(jnp.concatenate(parts, axis=1) if len(parts) > 1 else parts[0])
    return out


def joint_kernel(
    chips, tasks, delta_hbm, sketch_hbm, out_ref, wall_ref, square_refs, basis_refs,
    turned, stack, packed, terms, sib_buf, half, slots, column, matrix, final,
    slab, slab2, slab3, parts, sib_parts, half2, slots2, other, other_in, mine, block, gathered, wpacked,
    g_s, g_r, sw_s, sw_r, a_s, a_r, b_s, b_r, c_s, c_r, power, total_w, y1_s, y2_s,
    p_s, p_r, q_s, q_r,
    t1_s, t1_r, t2_s, t2_r, t3_s, t3_r, w_s, w_r, sp_s, sp_r, d_s, d_r, e_s, e_r, y_sem, t4_s, t4_r, f_s, f_r,
):
    chip, core, sib = place(chips)
    me = lax.axis_index("task")
    x_ref, gram_ref, delta = square_refs[:3]
    own_ref = basis_refs[0]
    rows, width = own_ref.shape
    depth = terms.shape[2]
    per = width // depth
    pairs = tasks // 2
    span = turned.shape[0] // (2 * chips)
    turned_count = [0]

    def turns(n):
        for _ in range(n):
            i = turned_count[0]
            if i < 2 * chips:
                turned[i * span:(i + 1) * span] = delta[:, i * span:(i + 1) * span].T
                turned_count[0] += 1

    square_stage(chips, tasks, turns, delta_hbm, sketch_hbm, *square_refs)
    basis_stage(1.0 / math.sqrt(tasks), gram_ref, x_ref, *basis_refs)
    own = own_ref[...].astype(bf16)
    stack[me] = own
    packed[me] = pack_rows(own)

    def swap_term(s, i):
        at = pl.ds(s * (per // 2), per // 2)
        return remote(terms.at[at, 1 - core], sib_buf.at[at], sw_s.at[i], sw_r.at[i], {"row": sib})

    def gram_term(s, i):
        term = lax.dot_general(stack[s], stack[me], (((0,), (0,)), ((), ())),
                               preferred_element_type=f32).astype(bf16)
        terms[pl.ds(s * (per // 2), per // 2)] = term.reshape(per // 2, 2, depth, width)
        swap_term(s, i).start()

    def to_owner(s, i):
        swap_term(s, i).wait()
        for e in range(per // 2):
            c = s * (per // 2) + e
            both = terms[c, core].astype(f32) + sib_buf[c].astype(f32)
            half[c] = pack_rows(both).astype(bf16)
            d = around(c, chips - chip, chips)

            @pl.when(c != chip)
            def _():
                remote(half.at[c], slots.at[d], a_s.at[d], a_r.at[d], {"row": c * 2 + core}).start()

    steps = spread(tasks, lambda c: packed.at[c], g_s, g_r)
    next(steps)
    gram_term(me, 0)
    ready = [me]
    for got in steps:
        unpack_to(stack.at[got], packed[got], rows, width)
        ready.append(got)
        gram_term(got, len(ready) - 1)
        to_owner(ready[-2], len(ready) - 2)
    to_owner(ready[-1], len(ready) - 1)
    wait_chips(chips, lambda c: half.at[c], lambda d: slots.at[d], a_s, a_r)
    gram = lax.fori_loop(
        1, chips, lambda d, t: t + slots[d].astype(f32), half[chip].astype(f32))
    first = gram.astype(bf16)
    slab[me] = first

    tsrc = lambda c: slab.at[me]
    start_tasks(tasks, tsrc, lambda c: slab.at[c], t1_s, t1_r)

    def gather(buf, sems, recvs, ys, ps, pr, prepare, use):
        seen, used = [], []

        def pass_on(c):
            return remote(buf.at[c, core], buf.at[c, core], ps.at[c], pr.at[c], {"row": sib})

        def landed(c):
            pass_on(c).start()
            seen.append(c)
            unpack_to(matrix.at[c * 2 + core], buf[c, core], depth, width)

        def finish(upto):
            for c in seen[len(used):upto]:
                remote(buf.at[c, core], buf.at[c, 1 - core], ps.at[c], pr.at[c], {"row": sib}).wait_recv()
                unpack_to(matrix.at[c * 2 + 1 - core], buf[c, 1 - core], depth, width)
                used.append(c)

        def between(step):
            if step == 1:
                prepare()
            finish(2 + 4 * (step - 1))
            whole()

        tasks_used = []

        def whole():
            if per != 4:
                return
            zs, z = chips // 2, chip // 2
            order = [0]
            for step in range(1, zs // 2):
                order += [-step, step]
            order += [zs // 2]
            for n, off in enumerate(order):
                needs = 2 if n == 0 else 2 + 4 * ((n + 1) // 2)
                if n == len(order) - 1:
                    needs = chips
                if n not in tasks_used and len(used) >= needs:
                    tasks_used.append(n)
                    use((z + off + zs) % zs)

        ring_gather(chips, lambda c: buf.at[c, core], sems, recvs, ys, landed, between)
        finish(chips)
        whole()
        if per != 4:
            loop(0, tasks, use)
        loop(0, chips, lambda c: pass_on(c).wait_send())

    def times_one(left, s):
        right = matrix[pl.ds(s * per, per)].reshape(width, width)
        return jnp.dot(unpack_rows(left[s], depth, width), right, preferred_element_type=f32)

    def square_one(s):
        power[...] += times_one(slab, s)

    def times(left):
        return lax.fori_loop(
            0, tasks, lambda s, total: total + times_one(left, s), jnp.zeros((depth, width), f32))

    power[...] = jnp.zeros_like(power)
    column[chip, core] = first
    gather(column, b_s, b_r, y1_s, p_s, p_r,
           lambda: wait_tasks(tasks, tsrc, lambda c: slab.at[c], t1_s, t1_r), square_one)
    two = pack_rows(power[...])
    slab2[me] = two.astype(bf16)
    src2 = lambda c: slab2.at[me]
    start_tasks(tasks, src2, lambda c: slab2.at[c], t2_s, t2_r)
    turns(6)
    wait_tasks(tasks, src2, lambda c: slab2.at[c], t2_s, t2_r)
    three = pack_rows(times(slab2))
    slab3[me] = three.astype(bf16)
    src3 = lambda c: slab3.at[me]
    start_tasks(tasks, src3, lambda c: slab3.at[c], t3_s, t3_r)
    part = -2.4375 * gram + 1.6875 * two - 0.5625 * three
    turns(6)
    wait_tasks(tasks, src3, lambda c: slab3.at[c], t3_s, t3_r)
    final[chip, core] = (part + 0.0625 * pack_rows(times(slab3))).astype(bf16)

    def apply(s):
        right = matrix[pl.ds(s * per, per)].reshape(width, width)
        total_w[...] += jnp.dot(stack[s], right, preferred_element_type=f32)

    total_w[...] = 2.25 * own_ref[...]
    gather(final, c_s, c_r, y2_s, q_s, q_r, lambda: None, apply)
    weights = total_w[...].astype(bf16)
    wall_ref[me] = weights
    wpacked[me] = pack_rows(weights)
    wsteps = spread(tasks, lambda c: wpacked.at[c], w_s, w_r)
    next(wsteps)

    def swap_part(u):
        return remote(parts.at[u, :, 1 - core], sib_parts.at[u], sp_s.at[u], sp_r.at[u], {"row": sib})

    def coef_term(u):
        tall = turned.shape[0] // tasks
        rows_u = turned[pl.ds(pl.multiple_of(u * tall, tall), tall)]
        term = jnp.dot(rows_u, wall_ref[me], preferred_element_type=f32).astype(bf16)
        parts[u] = term.reshape(parts.shape[1:])
        swap_part(u).start()

    turns(2 * chips)
    loop(0, tasks, coef_term)
    twin = next(wsteps)
    unpack_to(wall_ref.at[twin], wpacked[twin], rows, width)
    loop(0, tasks, lambda u: swap_part(u).wait())

    def add(c):
        for p in range(pairs):
            one, two = (
                parts[u, c, core].astype(f32) + sib_parts[u, c].astype(f32)
                for u in (2 * p, 2 * p + 1)
            )
            half2[c, p] = pack_pair(one, two).astype(bf16)

    loop(0, chips, add)

    def advance():
        for got in wsteps:
            unpack_to(wall_ref.at[got], wpacked[got], rows, width)
            break

    total = ring_reduce(chips, half2, slots2, other, other_in, d_s, d_r, y_sem, advance)
    for p in range(pairs):
        for v, piece in enumerate(unpack_pair(total[p], width)):
            mine[2 * p + v] = piece.astype(bf16)
    block[me] = mine[me]
    tsrc4, tdst4 = (lambda c: mine.at[c]), (lambda c: block.at[c])
    start_tasks(tasks, tsrc4, tdst4, t4_s, t4_r)
    for got in wsteps:
        unpack_to(wall_ref.at[got], wpacked[got], rows, width)
    wait_tasks(tasks, tsrc4, tdst4, t4_s, t4_r)
    for p in range(pairs):
        gathered[core, chip, p] = pack_pair(block[2 * p], block[2 * p + 1])
    seen = []

    def spill(c, which):
        for p in range(pairs):
            for v, piece in enumerate(unpack_pair(gathered[which, c, p], width)):
                out_ref[2 * p + v, c, which] = piece

    def pass_on(c):
        spot = gathered.at[core, c]
        return remote(spot, spot, f_s.at[c], f_r.at[c], {"row": sib})

    def landed(c):
        pass_on(c).start()
        seen.append(c)
        spill(c, core)

    ring_gather(chips, lambda c: gathered.at[core, c], e_s, e_r, y_sem, landed)
    for c in seen:
        remote(gathered.at[core, c], gathered.at[1 - core, c], f_s.at[c], f_r.at[c],
               {"row": sib}).wait_recv()
        spill(c, 1 - core)
    loop(0, chips, lambda c: pass_on(c).wait_send())


def joint(delta, sketch, chips, tasks):
    rows, features = delta.shape
    width = sketch.shape[0]
    depth = tasks * width // (2 * chips)
    piece = features // (tasks * chips * 2)
    chunk = (tasks // 2, pair_tiles(width), 128)
    high = tiles(depth, width)[2]
    tall = tiles(rows, width)[2]
    buf = lambda *shape: pltpu.VMEM(shape, bf16)
    pair = lambda n: [DMA((n,)), DMA((n,))]
    return pl.pallas_call(
        functools.partial(joint_kernel, chips, tasks),
        out_shape=(jax.ShapeDtypeStruct((tasks, chips, 2, piece, width), bf16),
                   jax.ShapeDtypeStruct((tasks, rows, width), bf16)),
        in_specs=[pl.BlockSpec(memory_space=pl.ANY)] * 2,
        out_specs=(VMEM, VMEM),
        scratch_shapes=[
            tuple(square_scratch(delta, sketch, chips)),
            (pltpu.VMEM((rows, width), f32),) + (pltpu.VMEM((width // CB, width, CB), f32),) * 3,
            buf(features, rows), buf(tasks, rows, width), buf(tasks, tall, 128),
            buf(chips, 2, depth, width), buf(chips, depth, width), buf(chips, high, 128),
            buf(chips, high, 128), buf(chips, 2, high, 128), buf(chips * 2, depth, width),
            buf(chips, 2, high, 128),
            buf(tasks, high, 128), buf(tasks, high, 128), buf(tasks, high, 128),
            buf(tasks, chips, 2, piece, width), buf(tasks, chips, piece, width),
            buf(chips, *chunk), buf(chips, *chunk), buf(*chunk), buf(*chunk),
            buf(tasks, piece, width), buf(tasks, piece, width), buf(2, chips, *chunk),
            buf(tasks, tall, 128),
        ] + pair(tasks) + pair(tasks) + pair(chips) * 3
        + [pltpu.VMEM((depth, width), f32), pltpu.VMEM((rows, width), f32), DMA((4,)), DMA((4,))]
        + pair(chips) * 2
        + pair(tasks) * 5 + pair(chips) * 2 + [DMA((4,))] + pair(tasks) + pair(chips),
        compiler_params=params(2),
        name="joint",
    )(delta, sketch)


def local(delta, sketch, base):
    tasks = lax.axis_size("task")
    chips = lax.axis_size("row") // 2
    delta_rows, task_sketch = delta[0], sketch[0]
    width = task_sketch.shape[1]
    coefs, stack = joint(delta_rows, task_sketch.T, chips, tasks)
    coefs = coefs.reshape(tasks, -1, width)
    update = lax.dot_general(
        stack, coefs, (((0, 2), (0, 2)), ((), ())), preferred_element_type=f32
    )
    return (base.astype(f32) + update).astype(bf16)


def solution(mesh):
    return jax.shard_map(
        local,
        mesh=mesh,
        in_specs=(P("task", "row", None), P("task", None, None), P("row", "task")),
        out_specs=P("row", "task"),
        check_vma=False,
    )
```

```python
import functools
import math

import jax
import jax.numpy as jnp
from jax import lax
from jax.experimental import pallas as pl
from jax.experimental.pallas import tpu as pltpu
from jax.sharding import PartitionSpec as P

highest = lax.Precision.HIGHEST
MESH = pl.DeviceIdType.MESH
VMEM = pl.BlockSpec(memory_space=pltpu.VMEM)
DMA = pltpu.SemaphoreType.DMA
f32 = jnp.float32
bf16 = jnp.bfloat16
CB = 64
PANEL = 8
LOADS = 4


def params(cid):
    return pltpu.CompilerParams(
        collective_id=cid, has_side_effects=True, vmem_limit_bytes=56 * 1024 * 1024
    )


def place(chips):
    row = lax.axis_index("row")
    chip, core = row // 2, row % 2
    return chip, core, chip * 2 + (1 - core)


def around(me, step, count):
    return (me + step) % count


def remote(src, dst, ssem, rsem, where):
    return pltpu.make_async_remote_copy(
        src_ref=src, dst_ref=dst, send_sem=ssem, recv_sem=rsem,
        device_id=where, device_id_type=MESH,
    )


def loop(lo, hi, body):
    def step(i, carry):
        body(i)
        return carry

    lax.fori_loop(lo, hi, step, 0)


def to_chips(chips, src, dst, ssem, rsem):
    chip, core, _ = place(chips)

    def body(d):
        other = around(chip, d, chips)
        remote(src(other), dst(d), ssem.at[d], rsem.at[d], {"row": other * 2 + core}).start()

    loop(1, chips, body)


def wait_chips(chips, src, dst, ssem, rsem):
    chip, core, _ = place(chips)

    def body(d):
        other = around(chip, d, chips)
        copy = remote(src(other), dst(d), ssem.at[d], rsem.at[d], {"row": other * 2 + core})
        copy.wait()

    loop(1, chips, body)


def tiles(depth, width):
    full = width // 128
    top = -(-depth // 32) * 16 if width % 128 else 0
    return full, top, full * depth + top


def pack_rows(value):
    depth, width = value.shape
    full, top, _ = tiles(depth, width)
    parts = [value[:, i * 128:(i + 1) * 128] for i in range(full)]
    if top:
        tail = value[:, full * 128:]
        low = jnp.concatenate(
            [tail[top:], jnp.zeros((2 * top - depth, 64), value.dtype)], axis=0
        ) if 2 * top > depth else tail[top:]
        parts.append(jnp.concatenate([tail[:top], low], axis=1))
    return jnp.concatenate(parts, axis=0)


def unpack_rows(packed, depth, width):
    full, top, _ = tiles(depth, width)
    parts = [packed[i * depth:(i + 1) * depth] for i in range(full)]
    if top:
        tail = packed[full * depth:full * depth + top]
        parts.append(jnp.concatenate([tail[:, :64], tail[:depth - top, 64:]], axis=0))
    return jnp.concatenate(parts, axis=1)


def unpack_to(dst, packed, depth, width):
    full, top, _ = tiles(depth, width)
    for i in range(full):
        dst[:, i * 128:(i + 1) * 128] = packed[i * depth:(i + 1) * depth]
    if top:
        tail = packed[full * depth:full * depth + top]
        dst[:top, full * 128:] = tail[:, :64]
        dst[top:, full * 128:] = tail[:depth - top, 64:]


def hello(chips, tasks):
    barrier = pltpu.get_barrier_semaphore()
    chip, core, sib = place(chips)
    pl.semaphore_signal(barrier, inc=1, device_id={"row": sib}, device_id_type=MESH)
    loop(1, chips, lambda d: pl.semaphore_signal(
        barrier, inc=1, device_id={"row": around(chip, d, chips) * 2 + core}, device_id_type=MESH))
    if tasks:
        me = lax.axis_index("task")
        loop(1, tasks, lambda d: pl.semaphore_signal(
            barrier, inc=1, device_id={"task": around(me, d, tasks)}, device_id_type=MESH))


def barrier_wait(chips, tasks):
    pl.semaphore_wait(pltpu.get_barrier_semaphore(), chips + tasks - 1)


def line(zs, z, y, core):
    return (((z + zs) % zs) * 2 + y) * 2 + core


def streams(zs, y):
    far, near = zs // 2, zs // 2 - 1
    return [(2, 1, near, 1 - y), (3, -1, far, 1 - y), (0, 1, far, y), (1, -1, near, y)]


def ring_reduce(chips, half, slots, other, other_in, ssem, rsem, ysem, between):
    chip, core, _ = place(chips)
    zs, z, y = chips // 2, chip // 2, chip % 2
    hops = zs // 2
    sent = []

    def term(zz, yy):
        return half[((zz + zs) % zs) * 2 + yy]

    def send(stream, step, src):
        k, way = stream[0], stream[1]
        n = k * hops + step - 1
        copy = remote(src, slots.at[n], ssem.at[n], rsem.at[n], {"row": line(zs, z + way, y, core)})
        copy.start()
        sent.append(copy)

    def arrive(stream, step):
        n = stream[0] * hops + step - 1
        remote(slots.at[n], slots.at[n], ssem.at[n], rsem.at[n], {"row": line(zs, z, y, core)}).wait_recv()
        return n

    for st in streams(zs, y):
        if st[2]:
            dest = ((z + st[1] * st[2] + zs) % zs) * 2 + st[3]
            send(st, 1, half.at[dest])
    for step in range(1, hops + 1):
        for st in streams(zs, y):
            if step <= st[2]:
                n = arrive(st, step)
                if step < st[2]:
                    dest = z + st[1] * (st[2] - step)
                    slots[n] = (slots[n].astype(f32) + term(dest, st[3]).astype(f32)).astype(bf16)
                    send(st, step + 1, slots.at[n])
        between()

    def final(plane, pair):
        total = term(z, plane).astype(f32)
        for k, n in pair:
            if n:
                total = total + slots[k * hops + n - 1].astype(f32)
        return total

    other[...] = final(1 - y, [(2, hops - 1), (3, hops)]).astype(bf16)
    swap = remote(other, other_in, ysem.at[0], ysem.at[1], {"row": line(zs, z, 1 - y, core)})
    swap.start()
    own = final(y, [(0, hops), (1, hops - 1)])
    swap.wait()
    for copy in sent:
        copy.wait_send()
    return own + other_in[...].astype(f32)


def ring_gather(chips, at, ssem, rsem, ysem, landed, between=lambda step: None):
    chip, core, _ = place(chips)
    zs, z, y = chips // 2, chip // 2, chip % 2
    hops = zs // 2
    sent = []

    def spot(zz, yy):
        return at(((zz + zs) % zs) * 2 + yy)

    def send(stream, step):
        k, way, _, yy = stream
        n = k * hops + step - 1
        block = spot(z - way * (step - 1), yy)
        copy = remote(block, block, ssem.at[n], rsem.at[n], {"row": line(zs, z + way, y, core)})
        copy.start()
        sent.append(copy)

    def arrive(stream, step):
        k, way, _, yy = stream
        n = k * hops + step - 1
        where = ((z - way * step + zs) % zs) * 2 + yy
        remote(at(where), at(where), ssem.at[n], rsem.at[n], {"row": line(zs, z, y, core)}).wait_recv()
        return where

    across = {"row": line(zs, z, 1 - y, core)}
    swap = remote(spot(z, y), spot(z, y), ysem.at[2], ysem.at[3], across)
    swap.start()
    order = streams(zs, y)[2:] + streams(zs, y)[:2]
    for st in order[:2]:
        if st[2]:
            send(st, 1)
    remote(spot(z, 1 - y), spot(z, 1 - y), ysem.at[2], ysem.at[3], across).wait_recv()
    for st in order[2:]:
        if st[2]:
            send(st, 1)
    landed(z * 2 + y)
    landed(z * 2 + 1 - y)
    for step in range(1, hops + 1):
        new = []
        for st in order:
            if step <= st[2]:
                new.append(arrive(st, step))
                if step < st[2]:
                    send(st, step + 1)
        for where in new:
            landed(where)
        between(step)
    swap.wait_send()
    for copy in sent:
        copy.wait_send()


def square_stage(chips, tasks, turns, delta_hbm, sketch_hbm, x_ref, out_ref, delta, sketch, term,
                 sib_buf, half, slots, load_s, core_s, core_r, a_s, a_r, b_s, b_r):
    chip, core, sib = place(chips)
    hello(chips, tasks)
    n = x_ref.shape[1]
    part = slots.shape[1]
    side = chips * part
    loads = []
    deep = delta.shape[1] // LOADS
    for i in range(LOADS):
        at = slice(i * deep, (i + 1) * deep)
        loads.append((
            pltpu.make_async_copy(delta_hbm.at[:, at], delta.at[:, at], load_s.at[2 * i]),
            pltpu.make_async_copy(sketch_hbm.at[:, at], sketch.at[:, at], load_s.at[2 * i + 1]),
        ))
        for copy in loads[-1]:
            copy.start()
    for i in range(LOADS):
        for copy in loads[i]:
            copy.wait()
        at = slice(i * deep, (i + 1) * deep)
        product = lax.dot_general(delta[:, at], sketch[:, at], (((1,), (1,)), ((), ())),
                                  preferred_element_type=f32)
        x_ref[...] = x_ref[...] + product if i else product
    across = x_ref[...].T
    top = 0
    for at in range(0, n, 128):
        wide = min(128, n - at)
        piece = dot_nn(across[at:], x_ref[:, at:at + wide])
        if wide < 128:
            piece = jnp.concatenate([piece, jnp.zeros((n - at, 128 - wide), f32)], axis=1)
        term[top:top + n - at] = piece
        top += n - at
    if top < 2 * side:
        term[top:] = jnp.zeros((2 * side - top, 128), f32)
    turns(3)
    barrier_wait(chips, tasks)

    def of_side(which):
        return pl.ds(pl.multiple_of(which * side, part), side)

    def of_chip(ref, at):
        return ref.at[pl.ds(pl.multiple_of(at * part, part), part)]

    swap = remote(term.at[of_side(1 - core)], sib_buf, core_s.at[0], core_r.at[0], {"row": sib})
    swap.start()
    turns(1)
    swap.wait()
    half[...] = term[of_side(core)] + sib_buf[...]
    src, dst = (lambda c: of_chip(half, c)), (lambda d: slots.at[d])
    to_chips(chips, src, dst, a_s, a_r)
    turns(4)
    wait_chips(chips, src, dst, a_s, a_r)
    own = pl.ds(pl.multiple_of(chip * part, part), part)
    total = lax.fori_loop(1, chips, lambda d, t: t + slots[d], half[own])
    out_ref[pl.ds(pl.multiple_of((core * chips + chip) * part, part), part)] = total
    src = lambda c: of_chip(out_ref, core * chips + chip)
    to_chips(chips, src, lambda d: src(0), b_s, b_r)
    turns(4)
    wait_chips(chips, src, lambda d: of_chip(out_ref, core * chips + around(chip, chips - d, chips)),
               b_s, b_r)
    mine, theirs = out_ref.at[of_side(core)], out_ref.at[of_side(1 - core)]
    swap = remote(mine, mine, core_s.at[1], core_r.at[1], {"row": sib})
    swap.start()
    turns(1)
    swap.wait_send()
    remote(mine, theirs, core_s.at[1], core_r.at[1], {"row": sib}).wait_recv()


def square_scratch(delta, sketch, chips):
    n = sketch.shape[0]
    packed = sum(n - at for at in range(0, n, 128))
    part = -(-packed // (16 * chips)) * 8
    return [pltpu.VMEM((delta.shape[0], n), f32), pltpu.VMEM((2 * chips * part, 128), f32),
            pltpu.VMEM(delta.shape, bf16), pltpu.VMEM(sketch.shape, bf16),
            pltpu.VMEM((2 * chips * part, 128), f32)] + [pltpu.VMEM((chips * part, 128), f32)] * 2 + [
            pltpu.VMEM((chips, part, 128), f32), DMA((2 * LOADS,)), DMA((2,)), DMA((2,))
    ] + [DMA((chips,))] * 4


def dot_nt(a, b):
    return lax.dot_general(a, b, (((1,), (1,)), ((), ())), precision=highest,
                           preferred_element_type=f32)


def dot_nn(a, b):
    return lax.dot_general(a, b, (((1,), (0,)), ((), ())), precision=highest,
                           preferred_element_type=f32)


def basis_stage(shrink, packed, x_ref, own_ref, cols, fac, inv):
    n = x_ref.shape[1]
    blocks = n // CB
    row_id = lax.broadcasted_iota(jnp.int32, (CB, 2 * CB), 0)
    lane_id = lax.broadcasted_iota(jnp.int32, (CB, 2 * CB), 1)
    eye = (lane_id == row_id + CB).astype(f32)
    inv[...] = jnp.zeros_like(inv)
    for k in range(blocks):
        wide, off = divmod(k * CB, 128)
        top = sum(n - 128 * w for w in range(wide))
        cols[k, k * CB:, :] = packed[top + off:top + n - 128 * wide, off:off + CB]
    for k in range(blocks):
        at = k * CB
        both = jnp.concatenate([cols[k, at:at + CB, :], jnp.zeros((CB, CB), f32)], axis=1) + eye
        for first in range(0, CB, PANEL):
            wide = [jnp.broadcast_to(both[:, first + m:first + m + 1], both.shape)
                    for m in range(PANEL)]
            for m in range(PANEL):
                j = first + m
                f = jnp.where(row_id > j, wide[m] * (1.0 / wide[m][j:j + 1, :]), 0.0)
                for q in range(m + 1, PANEL):
                    wide[q] = wide[q] - f * wide[q][j:j + 1, :]
                both = both - f * both[j:j + 1, :]
        diag = jnp.sum(jnp.where(lane_id == row_id, both, 0.0), axis=1, keepdims=True)
        zkk = both[:, CB:] * lax.rsqrt(diag)
        if k + 1 < blocks:
            panel = dot_nt(cols[k, at + CB:, :], zkk)
            fac[k, at + CB:, :] = panel
            for j in range(k + 1, blocks):
                off = (j - k - 1) * CB
                cols[j, j * CB:, :] = cols[j, j * CB:, :] - dot_nt(
                    panel[off:, :], panel[off:off + CB, :])
        for c in range(k):
            acc = dot_nn(fac[c, at:at + CB, :], inv[c, c * CB:(c + 1) * CB, :])
            for m in range(c + 1, k):
                acc = acc + dot_nn(fac[m, at:at + CB, :], inv[c, m * CB:(m + 1) * CB, :])
            inv[c, at:at + CB, :] = -dot_nn(zkk, acc)
        inv[k, at:at + CB, :] = zkk
    z = jnp.concatenate([inv[c] for c in range(blocks)], axis=1)
    own_ref[...] = dot_nt(x_ref[...], z) * shrink


def start_tasks(tasks, src, dst, ssem, rsem):
    me = lax.axis_index("task")

    def body(d):
        other = around(me, d, tasks)
        remote(src(other), dst(me), ssem.at[d], rsem.at[d], {"task": other}).start()

    loop(1, tasks, body)


def wait_tasks(tasks, src, dst, ssem, rsem):
    me = lax.axis_index("task")

    def body(d):
        other = around(me, d, tasks)
        back = around(me, tasks - d, tasks)
        remote(src(other), dst(back), ssem.at[d], rsem.at[d], {"task": other}).wait()

    loop(1, tasks, body)


def spread(tasks, at, ssem, rsem):
    me = lax.axis_index("task")
    xs = tasks // 2
    x, y = me % xs, me // xs
    sent = []

    def send(n, block, to):
        copy = remote(block, block, ssem.at[n], rsem.at[n], {"task": to})
        copy.start()
        sent.append(copy)

    def arrive(n, block):
        remote(block, block, ssem.at[n], rsem.at[n], {"task": me}).wait_recv()

    def name(xx, yy):
        return yy * xs + xx % xs

    own = at(me)
    halves = xs == 4
    across = [d for d in range(1, xs) if d == xs // 2]
    along = [d for d in range(1, xs) if d != xs // 2]
    send(0, own, name(x, 1 - y))
    for d in along if halves else along + across:
        send(d, own, name(x + d, y))
    yield
    twin = at(name(x, 1 - y))
    arrive(0, twin)
    for d in along:
        send(xs + d, twin, name(x + d, y))
    yield name(x, 1 - y)

    def half(block, which):
        size = block.shape[0] // 2
        return block.at[pl.ds(which * size, size)]

    if halves:
        for d, n, which in ((1, 2, 0), (3, xs, 1)):
            source = name(x + xs - d, y)
            arrive(d, at(source))
            send(n, half(at(source), which), name(x + d, y))
            yield source
    for d in across:
        block = at(name(x + xs - d, y))
        if halves:
            arrive(2, half(block, 0))
            arrive(xs, half(block, 1))
        else:
            arrive(d, block)
        send(xs + d, block, name(x, 1 - y))
        yield name(x + xs - d, y)
    for d in [] if halves else along:
        block = name(x + xs - d, y)
        arrive(d, at(block))
        yield block
    for d in along + across:
        block = name(x + xs - d, 1 - y)
        arrive(xs + d, at(block))
        yield block
    for copy in sent:
        copy.wait_send()


def pair_tiles(width):
    return 16 * (2 * (width // 128) + (1 if width % 128 else 0))


def pack_pair(one, two):
    width = one.shape[1]
    full = width // 128
    parts = [v[:, i * 128:(i + 1) * 128] for v in (one, two) for i in range(full)]
    if width % 128:
        parts.append(jnp.concatenate([one[:, full * 128:], two[:, full * 128:]], axis=1))
    return jnp.concatenate(parts, axis=0)


def unpack_pair(packed, width):
    full = width // 128
    out = []
    for v in range(2):
        parts = [packed[(v * full + i) * 16:(v * full + i + 1) * 16] for i in range(full)]
        if width % 128:
            parts.append(packed[2 * full * 16:, v * 64:v * 64 + 64])
        out.append(jnp.concatenate(parts, axis=1) if len(parts) > 1 else parts[0])
    return out


def joint_kernel(
    chips, tasks, delta_hbm, sketch_hbm, base_ref, merged_ref, out_ref, wall_ref, square_refs, basis_refs,
    turned, stack, packed, terms, sib_buf, half, slots, column, matrix, final,
    slab, slab2, slab3, parts, sib_parts, half2, slots2, other, other_in, mine, block, gathered, acc,
    g_s, g_r, sw_s, sw_r, a_s, a_r, b_s, b_r, c_s, c_r, power, total_w, y1_s, y2_s,
    p_s, p_r, q_s, q_r,
    t1_s, t1_r, t2_s, t2_r, t3_s, t3_r, w_s, w_r, sp_s, sp_r, d_s, d_r, e_s, e_r, y_sem, t4_s, t4_r, f_s, f_r,
):
    chip, core, sib = place(chips)
    me = lax.axis_index("task")
    x_ref, gram_ref, delta = square_refs[:3]
    own_ref = basis_refs[0]
    rows, width = own_ref.shape
    depth = terms.shape[2]
    per = width // depth
    pairs = tasks // 2
    span = turned.shape[0] // (2 * chips)
    turned_count = [0]

    def turns(n):
        for _ in range(n):
            i = turned_count[0]
            if i < 2 * chips:
                turned[i * span:(i + 1) * span] = delta[:, i * span:(i + 1) * span].T
                turned_count[0] += 1

    square_stage(chips, tasks, turns, delta_hbm, sketch_hbm, *square_refs)
    basis_stage(1.0 / math.sqrt(tasks), gram_ref, x_ref, *basis_refs)
    own = own_ref[...].astype(bf16)
    stack[me] = own
    packed[me] = pack_rows(own)

    def swap_term(s, i):
        at = pl.ds(s * (per // 2), per // 2)
        return remote(terms.at[at, 1 - core], sib_buf.at[at], sw_s.at[i], sw_r.at[i], {"row": sib})

    def gram_term(s, i):
        term = lax.dot_general(stack[s], stack[me], (((0,), (0,)), ((), ())),
                               preferred_element_type=f32).astype(bf16)
        terms[pl.ds(s * (per // 2), per // 2)] = term.reshape(per // 2, 2, depth, width)
        swap_term(s, i).start()

    def to_owner(s, i):
        swap_term(s, i).wait()
        for e in range(per // 2):
            c = s * (per // 2) + e
            both = terms[c, core].astype(f32) + sib_buf[c].astype(f32)
            half[c] = pack_rows(both).astype(bf16)
            d = around(c, chips - chip, chips)

            @pl.when(c != chip)
            def _():
                remote(half.at[c], slots.at[d], a_s.at[d], a_r.at[d], {"row": c * 2 + core}).start()

    steps = spread(tasks, lambda c: packed.at[c], g_s, g_r)
    next(steps)
    gram_term(me, 0)
    ready = [me]
    for got in steps:
        unpack_to(stack.at[got], packed[got], rows, width)
        ready.append(got)
        gram_term(got, len(ready) - 1)
        turns(1)
        to_owner(ready[-2], len(ready) - 2)
    to_owner(ready[-1], len(ready) - 1)
    wait_chips(chips, lambda c: half.at[c], lambda d: slots.at[d], a_s, a_r)
    gram = lax.fori_loop(
        1, chips, lambda d, t: t + slots[d].astype(f32), half[chip].astype(f32))
    first = gram.astype(bf16)
    slab[me] = first

    tsrc = lambda c: slab.at[me]
    start_tasks(tasks, tsrc, lambda c: slab.at[c], t1_s, t1_r)

    def gather(buf, sems, recvs, ys, ps, pr, prepare, use):
        seen, used = [], []

        def pass_on(c):
            return remote(buf.at[c, core], buf.at[c, core], ps.at[c], pr.at[c], {"row": sib})

        def landed(c):
            pass_on(c).start()
            seen.append(c)
            unpack_to(matrix.at[c * 2 + core], buf[c, core], depth, width)

        def finish(upto):
            for c in seen[len(used):upto]:
                remote(buf.at[c, core], buf.at[c, 1 - core], ps.at[c], pr.at[c], {"row": sib}).wait_recv()
                unpack_to(matrix.at[c * 2 + 1 - core], buf[c, 1 - core], depth, width)
                used.append(c)

        def between(step):
            if step == 1:
                prepare()
            finish(2 + 4 * (step - 1))
            whole()

        tasks_used = []

        def whole():
            if per != 4:
                return
            zs, z = chips // 2, chip // 2
            order = [0]
            for step in range(1, zs // 2):
                order += [-step, step]
            order += [zs // 2]
            for n, off in enumerate(order):
                needs = 2 if n == 0 else 2 + 4 * ((n + 1) // 2)
                if n == len(order) - 1:
                    needs = chips
                if n not in tasks_used and len(used) >= needs:
                    tasks_used.append(n)
                    use((z + off + zs) % zs)

        ring_gather(chips, lambda c: buf.at[c, core], sems, recvs, ys, landed, between)
        finish(chips)
        whole()
        if per != 4:
            loop(0, tasks, use)
        loop(0, chips, lambda c: pass_on(c).wait_send())

    def times_one(left, s):
        right = matrix[pl.ds(s * per, per)].reshape(width, width)
        return jnp.dot(unpack_rows(left[s], depth, width), right, preferred_element_type=f32)

    def square_one(s):
        power[...] += times_one(slab, s)

    def times(left):
        return lax.fori_loop(
            0, tasks, lambda s, total: total + times_one(left, s), jnp.zeros((depth, width), f32))

    power[...] = jnp.zeros_like(power)
    column[chip, core] = first
    gather(column, b_s, b_r, y1_s, p_s, p_r,
           lambda: wait_tasks(tasks, tsrc, lambda c: slab.at[c], t1_s, t1_r), square_one)
    two = pack_rows(power[...])
    slab2[me] = two.astype(bf16)
    src2 = lambda c: slab2.at[me]
    start_tasks(tasks, src2, lambda c: slab2.at[c], t2_s, t2_r)
    turns(6)
    wait_tasks(tasks, src2, lambda c: slab2.at[c], t2_s, t2_r)
    three = pack_rows(times(slab2))
    slab3[me] = three.astype(bf16)
    src3 = lambda c: slab3.at[me]
    start_tasks(tasks, src3, lambda c: slab3.at[c], t3_s, t3_r)
    part = -2.4375 * gram + 1.6875 * two - 0.5625 * three
    turns(6)
    wait_tasks(tasks, src3, lambda c: slab3.at[c], t3_s, t3_r)
    final[chip, core] = (part + 0.0625 * pack_rows(times(slab3))).astype(bf16)

    def apply(s):
        right = matrix[pl.ds(s * per, per)].reshape(width, width)
        total_w[...] += jnp.dot(stack[s], right, preferred_element_type=f32)

    total_w[...] = 2.25 * own_ref[...]
    gather(final, c_s, c_r, y2_s, q_s, q_r, lambda: None, apply)
    weights = total_w[...].astype(bf16)
    wall_ref[me] = weights
    packed[me] = pack_rows(weights)
    wsteps = spread(tasks, lambda c: packed.at[c], w_s, w_r)
    next(wsteps)

    def swap_part(u):
        return remote(parts.at[u, :, 1 - core], sib_parts.at[u], sp_s.at[u], sp_r.at[u], {"row": sib})

    def coef_term(u):
        tall = turned.shape[0] // tasks
        rows_u = turned[pl.ds(pl.multiple_of(u * tall, tall), tall)]
        term = jnp.dot(rows_u, wall_ref[me], preferred_element_type=f32).astype(bf16)
        parts[u] = term.reshape(parts.shape[1:])
        swap_part(u).start()

    turns(2 * chips)
    loop(0, tasks, coef_term)
    twin = next(wsteps)
    unpack_to(wall_ref.at[twin], packed[twin], rows, width)
    loop(0, tasks, lambda u: swap_part(u).wait())

    def add(c):
        for p in range(pairs):
            one, two = (
                parts[u, c, core].astype(f32) + sib_parts[u, c].astype(f32)
                for u in (2 * p, 2 * p + 1)
            )
            half2[c, p] = pack_pair(one, two).astype(bf16)

    loop(0, chips, add)

    def advance():
        for got in wsteps:
            unpack_to(wall_ref.at[got], packed[got], rows, width)
            break

    total = ring_reduce(chips, half2, slots2, other, other_in, d_s, d_r, y_sem, advance)
    for p in range(pairs):
        for v, piece in enumerate(unpack_pair(total[p], width)):
            mine[2 * p + v] = piece.astype(bf16)
    block[me] = mine[me]
    tsrc4, tdst4 = (lambda c: mine.at[c]), (lambda c: block.at[c])
    start_tasks(tasks, tsrc4, tdst4, t4_s, t4_r)
    for got in wsteps:
        unpack_to(wall_ref.at[got], packed[got], rows, width)
    wait_tasks(tasks, tsrc4, tdst4, t4_s, t4_r)
    for p in range(pairs):
        gathered[core, chip, p] = pack_pair(block[2 * p], block[2 * p + 1])
    seen = []

    def spill(c, which):
        for p in range(pairs):
            for v, piece in enumerate(unpack_pair(gathered[which, c, p], width)):
                out_ref[2 * p + v, c, which] = piece

    def pass_on(c):
        spot = gathered.at[core, c]
        return remote(spot, spot, f_s.at[c], f_r.at[c], {"row": sib})

    def landed(c):
        pass_on(c).start()
        seen.append(c)
        spill(c, core)

    ring_gather(chips, lambda c: gathered.at[core, c], e_s, e_r, y_sem, landed)
    for c in seen:
        remote(gathered.at[core, c], gathered.at[1 - core, c], f_s.at[c], f_r.at[c],
               {"row": sib}).wait_recv()
        spill(c, 1 - core)
    loop(0, chips, lambda c: pass_on(c).wait_send())

    def update(t):
        block = out_ref[t].reshape(acc.shape[1], width)
        acc[...] += lax.dot_general(wall_ref[t], block, (((1,), (1,)), ((), ())),
                                    preferred_element_type=f32)

    acc[...] = base_ref[...].astype(f32)
    loop(0, tasks, update)
    merged_ref[...] = acc[...].astype(bf16)


def joint(delta, sketch, base, chips, tasks):
    rows, features = delta.shape
    width = sketch.shape[0]
    depth = tasks * width // (2 * chips)
    piece = features // (tasks * chips * 2)
    chunk = (tasks // 2, pair_tiles(width), 128)
    high = tiles(depth, width)[2]
    tall = tiles(rows, width)[2]
    buf = lambda *shape: pltpu.VMEM(shape, bf16)
    pair = lambda n: [DMA((n,)), DMA((n,))]
    return pl.pallas_call(
        functools.partial(joint_kernel, chips, tasks),
        out_shape=jax.ShapeDtypeStruct(base.shape, bf16),
        in_specs=[pl.BlockSpec(memory_space=pl.ANY)] * 2 + [VMEM],
        out_specs=VMEM,
        scratch_shapes=[
            buf(tasks, chips, 2, piece, width), buf(tasks, rows, width),
            tuple(square_scratch(delta, sketch, chips)),
            (pltpu.VMEM((rows, width), f32),) + (pltpu.VMEM((width // CB, width, CB), f32),) * 3,
            buf(features, rows), buf(tasks, rows, width), buf(tasks, tall, 128),
            buf(chips, 2, depth, width), buf(chips, depth, width), buf(chips, high, 128),
            buf(chips, high, 128), buf(chips, 2, high, 128), buf(chips * 2, depth, width),
            buf(chips, 2, high, 128),
            buf(tasks, high, 128), buf(tasks, high, 128), buf(tasks, high, 128),
            buf(tasks, chips, 2, piece, width), buf(tasks, chips, piece, width),
            buf(chips, *chunk), buf(chips, *chunk), buf(*chunk), buf(*chunk),
            buf(tasks, piece, width), buf(tasks, piece, width), buf(2, chips, *chunk),
            pltpu.VMEM((rows, features // tasks), f32),
        ] + pair(tasks) + pair(tasks) + pair(chips) * 3
        + [pltpu.VMEM((depth, width), f32), pltpu.VMEM((rows, width), f32), DMA((4,)), DMA((4,))]
        + pair(chips) * 2
        + pair(tasks) * 5 + pair(chips) * 2 + [DMA((4,))] + pair(tasks) + pair(chips),
        compiler_params=params(2),
        name="joint",
    )(delta, sketch, base)


def local(delta, sketch, base):
    tasks = lax.axis_size("task")
    chips = lax.axis_size("row") // 2
    delta_rows, task_sketch = delta[0], sketch[0]
    return joint(delta_rows, task_sketch.T, base, chips, tasks)


def solution(mesh):
    return jax.shard_map(
        local,
        mesh=mesh,
        in_specs=(P("task", "row", None), P("task", None, None), P("row", "task")),
        out_specs=P("row", "task"),
        check_vma=False,
    )
```

```python
import functools
import math

import jax
import jax.numpy as jnp
from jax import lax
from jax.experimental import pallas as pl
from jax.experimental.pallas import tpu as pltpu
from jax.sharding import PartitionSpec as P

highest = lax.Precision.HIGHEST
MESH = pl.DeviceIdType.MESH
VMEM = pl.BlockSpec(memory_space=pltpu.VMEM)
DMA = pltpu.SemaphoreType.DMA
f32 = jnp.float32
bf16 = jnp.bfloat16
CB = 64
PANEL = 8
LOADS = 4


def params(cid):
    return pltpu.CompilerParams(
        collective_id=cid, has_side_effects=True, vmem_limit_bytes=50 * 1024 * 1024
    )


def place(chips):
    row = lax.axis_index("row")
    chip, core = row // 2, row % 2
    return chip, core, chip * 2 + (1 - core)


def around(me, step, count):
    return (me + step) % count


def remote(src, dst, ssem, rsem, where):
    return pltpu.make_async_remote_copy(
        src_ref=src, dst_ref=dst, send_sem=ssem, recv_sem=rsem,
        device_id=where, device_id_type=MESH,
    )


def loop(lo, hi, body):
    def step(i, carry):
        body(i)
        return carry

    lax.fori_loop(lo, hi, step, 0)


def to_chips(chips, src, dst, ssem, rsem):
    chip, core, _ = place(chips)

    def body(d):
        other = around(chip, d, chips)
        remote(src(other), dst(d), ssem.at[d], rsem.at[d], {"row": other * 2 + core}).start()

    loop(1, chips, body)


def wait_chips(chips, src, dst, ssem, rsem):
    chip, core, _ = place(chips)

    def body(d):
        other = around(chip, d, chips)
        copy = remote(src(other), dst(d), ssem.at[d], rsem.at[d], {"row": other * 2 + core})
        copy.wait()

    loop(1, chips, body)


def tiles(depth, width):
    full = width // 128
    top = -(-depth // 32) * 16 if width % 128 else 0
    return full, top, full * depth + top


def pack_rows(value):
    depth, width = value.shape
    full, top, _ = tiles(depth, width)
    parts = [value[:, i * 128:(i + 1) * 128] for i in range(full)]
    if top:
        tail = value[:, full * 128:]
        low = jnp.concatenate(
            [tail[top:], jnp.zeros((2 * top - depth, 64), value.dtype)], axis=0
        ) if 2 * top > depth else tail[top:]
        parts.append(jnp.concatenate([tail[:top], low], axis=1))
    return jnp.concatenate(parts, axis=0)


def unpack_rows(packed, depth, width):
    full, top, _ = tiles(depth, width)
    parts = [packed[i * depth:(i + 1) * depth] for i in range(full)]
    if top:
        tail = packed[full * depth:full * depth + top]
        parts.append(jnp.concatenate([tail[:, :64], tail[:depth - top, 64:]], axis=0))
    return jnp.concatenate(parts, axis=1)


def unpack_to(dst, packed, depth, width):
    full, top, _ = tiles(depth, width)
    for i in range(full):
        dst[:, i * 128:(i + 1) * 128] = packed[i * depth:(i + 1) * depth]
    if top:
        tail = packed[full * depth:full * depth + top]
        dst[:top, full * 128:] = tail[:, :64]
        dst[top:, full * 128:] = tail[:depth - top, 64:]


def hello(chips, tasks):
    barrier = pltpu.get_barrier_semaphore()
    chip, core, sib = place(chips)
    pl.semaphore_signal(barrier, inc=1, device_id={"row": sib}, device_id_type=MESH)
    loop(1, chips, lambda d: pl.semaphore_signal(
        barrier, inc=1, device_id={"row": around(chip, d, chips) * 2 + core}, device_id_type=MESH))
    if tasks:
        me = lax.axis_index("task")
        loop(1, tasks, lambda d: pl.semaphore_signal(
            barrier, inc=1, device_id={"task": around(me, d, tasks)}, device_id_type=MESH))


def barrier_wait(chips, tasks):
    pl.semaphore_wait(pltpu.get_barrier_semaphore(), chips + tasks - 1)


def line(zs, z, y, core):
    return (((z + zs) % zs) * 2 + y) * 2 + core


def streams(zs, y):
    far, near = zs // 2, zs // 2 - 1
    return [(2, 1, near, 1 - y), (3, -1, far, 1 - y), (0, 1, far, y), (1, -1, near, y)]


def ring_reduce(chips, half, slots, other, other_in, ssem, rsem, ysem, between):
    chip, core, _ = place(chips)
    zs, z, y = chips // 2, chip // 2, chip % 2
    hops = zs // 2
    sent = []

    def term(zz, yy):
        return half[((zz + zs) % zs) * 2 + yy]

    def send(stream, step, src):
        k, way = stream[0], stream[1]
        n = k * hops + step - 1
        copy = remote(src, slots.at[n], ssem.at[n], rsem.at[n], {"row": line(zs, z + way, y, core)})
        copy.start()
        sent.append(copy)

    def arrive(stream, step):
        n = stream[0] * hops + step - 1
        remote(slots.at[n], slots.at[n], ssem.at[n], rsem.at[n], {"row": line(zs, z, y, core)}).wait_recv()
        return n

    for st in streams(zs, y):
        if st[2]:
            dest = ((z + st[1] * st[2] + zs) % zs) * 2 + st[3]
            send(st, 1, half.at[dest])
    for step in range(1, hops + 1):
        for st in streams(zs, y):
            if step <= st[2]:
                n = arrive(st, step)
                if step < st[2]:
                    dest = z + st[1] * (st[2] - step)
                    slots[n] = (slots[n].astype(f32) + term(dest, st[3]).astype(f32)).astype(bf16)
                    send(st, step + 1, slots.at[n])
        between()

    def final(plane, pair):
        total = term(z, plane).astype(f32)
        for k, n in pair:
            if n:
                total = total + slots[k * hops + n - 1].astype(f32)
        return total

    other[...] = final(1 - y, [(2, hops - 1), (3, hops)]).astype(bf16)
    swap = remote(other, other_in, ysem.at[0], ysem.at[1], {"row": line(zs, z, 1 - y, core)})
    swap.start()
    own = final(y, [(0, hops), (1, hops - 1)])
    swap.wait()
    for copy in sent:
        copy.wait_send()
    return own + other_in[...].astype(f32)


def ring_gather(chips, at, ssem, rsem, ysem, landed, between=lambda step: None):
    chip, core, _ = place(chips)
    zs, z, y = chips // 2, chip // 2, chip % 2
    hops = zs // 2
    sent = []

    def spot(zz, yy):
        return at(((zz + zs) % zs) * 2 + yy)

    def send(stream, step):
        k, way, _, yy = stream
        n = k * hops + step - 1
        block = spot(z - way * (step - 1), yy)
        copy = remote(block, block, ssem.at[n], rsem.at[n], {"row": line(zs, z + way, y, core)})
        copy.start()
        sent.append(copy)

    def arrive(stream, step):
        k, way, _, yy = stream
        n = k * hops + step - 1
        where = ((z - way * step + zs) % zs) * 2 + yy
        remote(at(where), at(where), ssem.at[n], rsem.at[n], {"row": line(zs, z, y, core)}).wait_recv()
        return where

    across = {"row": line(zs, z, 1 - y, core)}
    swap = remote(spot(z, y), spot(z, y), ysem.at[2], ysem.at[3], across)
    swap.start()
    order = streams(zs, y)[2:] + streams(zs, y)[:2]
    for st in order[:2]:
        if st[2]:
            send(st, 1)
    remote(spot(z, 1 - y), spot(z, 1 - y), ysem.at[2], ysem.at[3], across).wait_recv()
    for st in order[2:]:
        if st[2]:
            send(st, 1)
    landed(z * 2 + y)
    landed(z * 2 + 1 - y)
    for step in range(1, hops + 1):
        new = []
        for st in order:
            if step <= st[2]:
                new.append(arrive(st, step))
                if step < st[2]:
                    send(st, step + 1)
        for where in new:
            landed(where)
        between(step)
    swap.wait_send()
    for copy in sent:
        copy.wait_send()


def square_stage(chips, tasks, turns, delta_hbm, sketch_hbm, x_ref, out_ref, delta, sketch, term,
                 sib_buf, half, slots, load_s, core_s, core_r, a_s, a_r, b_s, b_r):
    chip, core, sib = place(chips)
    hello(chips, tasks)
    n = x_ref.shape[1]
    part = slots.shape[1]
    side = chips * part
    loads = []
    deep = delta.shape[1] // LOADS
    for i in range(LOADS):
        at = slice(i * deep, (i + 1) * deep)
        loads.append((
            pltpu.make_async_copy(delta_hbm.at[:, at], delta.at[:, at], load_s.at[2 * i]),
            pltpu.make_async_copy(sketch_hbm.at[:, at], sketch.at[:, at], load_s.at[2 * i + 1]),
        ))
        for copy in loads[-1]:
            copy.start()
    for i in range(LOADS):
        for copy in loads[i]:
            copy.wait()
        at = slice(i * deep, (i + 1) * deep)
        product = lax.dot_general(delta[:, at], sketch[:, at], (((1,), (1,)), ((), ())),
                                  preferred_element_type=f32)
        x_ref[...] = x_ref[...] + product if i else product
    across = x_ref[...].T
    top = 0
    for at in range(0, n, 128):
        wide = min(128, n - at)
        piece = dot_nn(across[at:], x_ref[:, at:at + wide])
        if wide < 128:
            piece = jnp.concatenate([piece, jnp.zeros((n - at, 128 - wide), f32)], axis=1)
        term[top:top + n - at] = piece
        top += n - at
    if top < 2 * side:
        term[top:] = jnp.zeros((2 * side - top, 128), f32)
    turns(3)
    barrier_wait(chips, tasks)

    def of_side(which):
        return pl.ds(pl.multiple_of(which * side, part), side)

    def of_chip(ref, at):
        return ref.at[pl.ds(pl.multiple_of(at * part, part), part)]

    swap = remote(term.at[of_side(1 - core)], sib_buf, core_s.at[0], core_r.at[0], {"row": sib})
    swap.start()
    turns(1)
    swap.wait()
    half[...] = term[of_side(core)] + sib_buf[...]
    src, dst = (lambda c: of_chip(half, c)), (lambda d: slots.at[d])
    to_chips(chips, src, dst, a_s, a_r)
    turns(4)
    wait_chips(chips, src, dst, a_s, a_r)
    own = pl.ds(pl.multiple_of(chip * part, part), part)
    total = lax.fori_loop(1, chips, lambda d, t: t + slots[d], half[own])
    out_ref[pl.ds(pl.multiple_of((core * chips + chip) * part, part), part)] = total
    src = lambda c: of_chip(out_ref, core * chips + chip)
    to_chips(chips, src, lambda d: src(0), b_s, b_r)
    turns(4)
    wait_chips(chips, src, lambda d: of_chip(out_ref, core * chips + around(chip, chips - d, chips)),
               b_s, b_r)
    mine, theirs = out_ref.at[of_side(core)], out_ref.at[of_side(1 - core)]
    swap = remote(mine, mine, core_s.at[1], core_r.at[1], {"row": sib})
    swap.start()
    turns(1)
    swap.wait_send()
    remote(mine, theirs, core_s.at[1], core_r.at[1], {"row": sib}).wait_recv()


def square_scratch(delta, sketch, chips):
    n = sketch.shape[0]
    packed = sum(n - at for at in range(0, n, 128))
    part = -(-packed // (16 * chips)) * 8
    return [pltpu.VMEM((delta.shape[0], n), f32), pltpu.VMEM((2 * chips * part, 128), f32),
            pltpu.VMEM(delta.shape, bf16), pltpu.VMEM(sketch.shape, bf16),
            pltpu.VMEM((2 * chips * part, 128), f32)] + [pltpu.VMEM((chips * part, 128), f32)] * 2 + [
            pltpu.VMEM((chips, part, 128), f32), DMA((2 * LOADS,)), DMA((2,)), DMA((2,))
    ] + [DMA((chips,))] * 4


def dot_nt(a, b):
    return lax.dot_general(a, b, (((1,), (1,)), ((), ())), precision=highest,
                           preferred_element_type=f32)


def dot_nn(a, b):
    return lax.dot_general(a, b, (((1,), (0,)), ((), ())), precision=highest,
                           preferred_element_type=f32)


def basis_stage(shrink, packed, x_ref, own_ref, cols, fac, inv):
    n = x_ref.shape[1]
    blocks = n // CB
    row_id = lax.broadcasted_iota(jnp.int32, (CB, 2 * CB), 0)
    lane_id = lax.broadcasted_iota(jnp.int32, (CB, 2 * CB), 1)
    eye = (lane_id == row_id + CB).astype(f32)
    inv[...] = jnp.zeros_like(inv)
    for k in range(blocks):
        wide, off = divmod(k * CB, 128)
        top = sum(n - 128 * w for w in range(wide))
        cols[k, k * CB:, :] = packed[top + off:top + n - 128 * wide, off:off + CB]
    for k in range(blocks):
        at = k * CB
        both = jnp.concatenate([cols[k, at:at + CB, :], jnp.zeros((CB, CB), f32)], axis=1) + eye
        for first in range(0, CB, PANEL):
            wide = [jnp.broadcast_to(both[:, first + m:first + m + 1], both.shape)
                    for m in range(PANEL)]
            for m in range(PANEL):
                j = first + m
                f = jnp.where(row_id > j, wide[m] * (1.0 / wide[m][j:j + 1, :]), 0.0)
                for q in range(m + 1, PANEL):
                    wide[q] = wide[q] - f * wide[q][j:j + 1, :]
                both = both - f * both[j:j + 1, :]
        diag = jnp.sum(jnp.where(lane_id == row_id, both, 0.0), axis=1, keepdims=True)
        zkk = both[:, CB:] * lax.rsqrt(diag)
        if k + 1 < blocks:
            panel = dot_nt(cols[k, at + CB:, :], zkk)
            fac[k, at + CB:, :] = panel
            for j in range(k + 1, blocks):
                off = (j - k - 1) * CB
                cols[j, j * CB:, :] = cols[j, j * CB:, :] - dot_nt(
                    panel[off:, :], panel[off:off + CB, :])
        for c in range(k):
            acc = dot_nn(fac[c, at:at + CB, :], inv[c, c * CB:(c + 1) * CB, :])
            for m in range(c + 1, k):
                acc = acc + dot_nn(fac[m, at:at + CB, :], inv[c, m * CB:(m + 1) * CB, :])
            inv[c, at:at + CB, :] = -dot_nn(zkk, acc)
        inv[k, at:at + CB, :] = zkk
    z = jnp.concatenate([inv[c] for c in range(blocks)], axis=1)
    own_ref[...] = dot_nt(x_ref[...], z) * shrink


def start_tasks(tasks, src, dst, ssem, rsem):
    me = lax.axis_index("task")

    def body(d):
        other = around(me, d, tasks)
        remote(src(other), dst(me), ssem.at[d], rsem.at[d], {"task": other}).start()

    loop(1, tasks, body)


def wait_tasks(tasks, src, dst, ssem, rsem):
    me = lax.axis_index("task")

    def body(d):
        other = around(me, d, tasks)
        back = around(me, tasks - d, tasks)
        remote(src(other), dst(back), ssem.at[d], rsem.at[d], {"task": other}).wait()

    loop(1, tasks, body)


def spread(tasks, at, ssem, rsem):
    me = lax.axis_index("task")
    xs = tasks // 2
    x, y = me % xs, me // xs
    sent = []

    def send(n, block, to):
        copy = remote(block, block, ssem.at[n], rsem.at[n], {"task": to})
        copy.start()
        sent.append(copy)

    def arrive(n, block):
        remote(block, block, ssem.at[n], rsem.at[n], {"task": me}).wait_recv()

    def name(xx, yy):
        return yy * xs + xx % xs

    own = at(me)
    halves = xs == 4
    across = [d for d in range(1, xs) if d == xs // 2]
    along = [d for d in range(1, xs) if d != xs // 2]
    send(0, own, name(x, 1 - y))
    for d in along if halves else along + across:
        send(d, own, name(x + d, y))
    yield
    twin = at(name(x, 1 - y))
    arrive(0, twin)
    for d in along:
        send(xs + d, twin, name(x + d, y))
    yield name(x, 1 - y)

    def half(block, which):
        size = block.shape[0] // 2
        return block.at[pl.ds(which * size, size)]

    if halves:
        for d, n, which in ((1, 2, 0), (3, xs, 1)):
            source = name(x + xs - d, y)
            arrive(d, at(source))
            send(n, half(at(source), which), name(x + d, y))
            yield source
    for d in across:
        block = at(name(x + xs - d, y))
        if halves:
            arrive(2, half(block, 0))
            arrive(xs, half(block, 1))
        else:
            arrive(d, block)
        send(xs + d, block, name(x, 1 - y))
        yield name(x + xs - d, y)
    for d in [] if halves else along:
        block = name(x + xs - d, y)
        arrive(d, at(block))
        yield block
    for d in along + across:
        block = name(x + xs - d, 1 - y)
        arrive(xs + d, at(block))
        yield block
    for copy in sent:
        copy.wait_send()


def pair_tiles(width):
    return 16 * (2 * (width // 128) + (1 if width % 128 else 0))


def pack_pair(one, two):
    width = one.shape[1]
    full = width // 128
    parts = [v[:, i * 128:(i + 1) * 128] for v in (one, two) for i in range(full)]
    if width % 128:
        parts.append(jnp.concatenate([one[:, full * 128:], two[:, full * 128:]], axis=1))
    return jnp.concatenate(parts, axis=0)


def unpack_pair(packed, width):
    full = width // 128
    out = []
    for v in range(2):
        parts = [packed[(v * full + i) * 16:(v * full + i + 1) * 16] for i in range(full)]
        if width % 128:
            parts.append(packed[2 * full * 16:, v * 64:v * 64 + 64])
        out.append(jnp.concatenate(parts, axis=1) if len(parts) > 1 else parts[0])
    return out


def joint_kernel(
    chips, tasks, delta_hbm, sketch_hbm, out_ref, wall_ref, square_refs, basis_refs,
    turned, stack, packed, terms, sib_buf, half, slots, column, matrix, final,
    slab, slab2, slab3, parts, sib_parts, half2, slots2, other, other_in, mine, block, gathered,
    g_s, g_r, sw_s, sw_r, a_s, a_r, b_s, b_r, c_s, c_r, power, total_w, gram_other, gram_in, y0_s, y1_s, y2_s,
    p_s, p_r, q_s, q_r,
    t1_s, t1_r, t2_s, t2_r, t3_s, t3_r, w_s, w_r, sp_s, sp_r, d_s, d_r, e_s, e_r, y_sem, t4_s, t4_r, f_s, f_r,
):
    chip, core, sib = place(chips)
    me = lax.axis_index("task")
    x_ref, gram_ref, delta = square_refs[:3]
    own_ref = basis_refs[0]
    rows, width = own_ref.shape
    depth = terms.shape[2]
    per = width // depth
    pairs = tasks // 2
    span = turned.shape[0] // (2 * chips)
    turned_count = [0]

    def turns(n):
        for _ in range(n):
            i = turned_count[0]
            if i < 2 * chips:
                turned[i * span:(i + 1) * span] = delta[:, i * span:(i + 1) * span].T
                turned_count[0] += 1

    square_stage(chips, tasks, turns, delta_hbm, sketch_hbm, *square_refs)
    basis_stage(1.0 / math.sqrt(tasks), gram_ref, x_ref, *basis_refs)
    own = own_ref[...].astype(bf16)
    stack[me] = own
    packed[me] = pack_rows(own)

    def swap_term(s, i):
        at = pl.ds(s * (per // 2), per // 2)
        return remote(terms.at[at, 1 - core], sib_buf.at[at], sw_s.at[i], sw_r.at[i], {"row": sib})

    def gram_term(s, i):
        term = lax.dot_general(stack[s], stack[me], (((0,), (0,)), ((), ())),
                               preferred_element_type=f32).astype(bf16)
        terms[pl.ds(s * (per // 2), per // 2)] = term.reshape(per // 2, 2, depth, width)
        swap_term(s, i).start()

    def both_cores(s, i):
        swap_term(s, i).wait()
        for e in range(per // 2):
            c = s * (per // 2) + e
            both = terms[c, core].astype(f32) + sib_buf[c].astype(f32)
            half[c] = pack_rows(both).astype(bf16)

    steps = spread(tasks, lambda c: packed.at[c], g_s, g_r)
    next(steps)
    gram_term(me, 0)
    ready = [me]
    for got in steps:
        unpack_to(stack.at[got], packed[got], rows, width)
        ready.append(got)
        gram_term(got, len(ready) - 1)
        turns(1)
        both_cores(ready[-2], len(ready) - 2)
    both_cores(ready[-1], len(ready) - 1)
    gram = ring_reduce(chips, half, slots, gram_other, gram_in, a_s, a_r, y0_s, lambda: None)
    first = gram.astype(bf16)
    slab[me] = first

    tsrc = lambda c: slab.at[me]
    start_tasks(tasks, tsrc, lambda c: slab.at[c], t1_s, t1_r)

    def gather(buf, sems, recvs, ys, ps, pr, prepare, use):
        seen, used = [], []

        def pass_on(c):
            return remote(buf.at[c, core], buf.at[c, core], ps.at[c], pr.at[c], {"row": sib})

        def landed(c):
            pass_on(c).start()
            seen.append(c)
            unpack_to(matrix.at[c * 2 + core], buf[c, core], depth, width)

        def finish(upto):
            for c in seen[len(used):upto]:
                remote(buf.at[c, core], buf.at[c, 1 - core], ps.at[c], pr.at[c], {"row": sib}).wait_recv()
                unpack_to(matrix.at[c * 2 + 1 - core], buf[c, 1 - core], depth, width)
                used.append(c)

        def between(step):
            if step == 1:
                prepare()
            finish(2 + 4 * (step - 1))
            whole()

        tasks_used = []

        def whole():
            if per != 4:
                return
            zs, z = chips // 2, chip // 2
            order = [0]
            for step in range(1, zs // 2):
                order += [-step, step]
            order += [zs // 2]
            for n, off in enumerate(order):
                needs = 2 if n == 0 else 2 + 4 * ((n + 1) // 2)
                if n == len(order) - 1:
                    needs = chips
                if n not in tasks_used and len(used) >= needs:
                    tasks_used.append(n)
                    use((z + off + zs) % zs)

        ring_gather(chips, lambda c: buf.at[c, core], sems, recvs, ys, landed, between)
        finish(chips)
        whole()
        if per != 4:
            loop(0, tasks, use)
        loop(0, chips, lambda c: pass_on(c).wait_send())

    def times_one(left, s):
        right = matrix[pl.ds(s * per, per)].reshape(width, width)
        return jnp.dot(unpack_rows(left[s], depth, width), right, preferred_element_type=f32)

    def square_one(s):
        power[...] += times_one(slab, s)

    def times(left):
        return lax.fori_loop(
            0, tasks, lambda s, total: total + times_one(left, s), jnp.zeros((depth, width), f32))

    power[...] = jnp.zeros_like(power)
    column[chip, core] = first
    gather(column, b_s, b_r, y1_s, p_s, p_r,
           lambda: wait_tasks(tasks, tsrc, lambda c: slab.at[c], t1_s, t1_r), square_one)
    two = pack_rows(power[...])
    slab2[me] = two.astype(bf16)
    src2 = lambda c: slab2.at[me]
    start_tasks(tasks, src2, lambda c: slab2.at[c], t2_s, t2_r)
    turns(6)
    wait_tasks(tasks, src2, lambda c: slab2.at[c], t2_s, t2_r)
    three = pack_rows(times(slab2))
    slab3[me] = three.astype(bf16)
    src3 = lambda c: slab3.at[me]
    start_tasks(tasks, src3, lambda c: slab3.at[c], t3_s, t3_r)
    part = -2.4375 * gram + 1.6875 * two - 0.5625 * three
    turns(6)
    wait_tasks(tasks, src3, lambda c: slab3.at[c], t3_s, t3_r)
    final[chip, core] = (part + 0.0625 * pack_rows(times(slab3))).astype(bf16)

    def apply(s):
        right = matrix[pl.ds(s * per, per)].reshape(width, width)
        total_w[...] += jnp.dot(stack[s], right, preferred_element_type=f32)

    total_w[...] = 2.25 * own_ref[...]
    gather(final, c_s, c_r, y2_s, q_s, q_r, lambda: None, apply)
    weights = total_w[...].astype(bf16)
    wall_ref[me] = weights
    packed[me] = pack_rows(weights)
    wsteps = spread(tasks, lambda c: packed.at[c], w_s, w_r)
    next(wsteps)

    def swap_part(u):
        return remote(parts.at[u, :, 1 - core], sib_parts.at[u], sp_s.at[u], sp_r.at[u], {"row": sib})

    def coef_term(u):
        tall = turned.shape[0] // tasks
        rows_u = turned[pl.ds(pl.multiple_of(u * tall, tall), tall)]
        term = jnp.dot(rows_u, wall_ref[me], preferred_element_type=f32).astype(bf16)
        parts[u] = term.reshape(parts.shape[1:])
        swap_part(u).start()

    turns(2 * chips)
    loop(0, tasks, coef_term)
    twin = next(wsteps)
    unpack_to(wall_ref.at[twin], packed[twin], rows, width)
    loop(0, tasks, lambda u: swap_part(u).wait())

    def add(c):
        for p in range(pairs):
            one, two = (
                parts[u, c, core].astype(f32) + sib_parts[u, c].astype(f32)
                for u in (2 * p, 2 * p + 1)
            )
            half2[c, p] = pack_pair(one, two).astype(bf16)

    loop(0, chips, add)

    def advance():
        for got in wsteps:
            unpack_to(wall_ref.at[got], packed[got], rows, width)
            break

    total = ring_reduce(chips, half2, slots2, other, other_in, d_s, d_r, y_sem, advance)
    for p in range(pairs):
        for v, piece in enumerate(unpack_pair(total[p], width)):
            mine[2 * p + v] = piece.astype(bf16)
    block[me] = mine[me]
    tsrc4, tdst4 = (lambda c: mine.at[c]), (lambda c: block.at[c])
    start_tasks(tasks, tsrc4, tdst4, t4_s, t4_r)
    for got in wsteps:
        unpack_to(wall_ref.at[got], packed[got], rows, width)
    wait_tasks(tasks, tsrc4, tdst4, t4_s, t4_r)
    for p in range(pairs):
        gathered[core, chip, p] = pack_pair(block[2 * p], block[2 * p + 1])
    seen = []

    def spill(c, which):
        for p in range(pairs):
            for v, piece in enumerate(unpack_pair(gathered[which, c, p], width)):
                out_ref[2 * p + v, c, which] = piece

    def pass_on(c):
        spot = gathered.at[core, c]
        return remote(spot, spot, f_s.at[c], f_r.at[c], {"row": sib})

    def landed(c):
        pass_on(c).start()
        seen.append(c)
        spill(c, core)

    ring_gather(chips, lambda c: gathered.at[core, c], e_s, e_r, y_sem, landed)
    for c in seen:
        remote(gathered.at[core, c], gathered.at[1 - core, c], f_s.at[c], f_r.at[c],
               {"row": sib}).wait_recv()
        spill(c, 1 - core)
    loop(0, chips, lambda c: pass_on(c).wait_send())


def joint(delta, sketch, chips, tasks):
    rows, features = delta.shape
    width = sketch.shape[0]
    depth = tasks * width // (2 * chips)
    piece = features // (tasks * chips * 2)
    chunk = (tasks // 2, pair_tiles(width), 128)
    high = tiles(depth, width)[2]
    tall = tiles(rows, width)[2]
    buf = lambda *shape: pltpu.VMEM(shape, bf16)
    pair = lambda n: [DMA((n,)), DMA((n,))]
    return pl.pallas_call(
        functools.partial(joint_kernel, chips, tasks),
        out_shape=(jax.ShapeDtypeStruct((tasks, chips, 2, piece, width), bf16),
                   jax.ShapeDtypeStruct((tasks, rows, width), bf16)),
        in_specs=[pl.BlockSpec(memory_space=pl.ANY)] * 2,
        out_specs=(VMEM, VMEM),
        scratch_shapes=[
            tuple(square_scratch(delta, sketch, chips)),
            (pltpu.VMEM((rows, width), f32),) + (pltpu.VMEM((width // CB, width, CB), f32),) * 3,
            buf(features, rows), buf(tasks, rows, width), buf(tasks, tall, 128),
            buf(chips, 2, depth, width), buf(chips, depth, width), buf(chips, high, 128),
            buf(chips, high, 128), buf(chips, 2, high, 128), buf(chips * 2, depth, width),
            buf(chips, 2, high, 128),
            buf(tasks, high, 128), buf(tasks, high, 128), buf(tasks, high, 128),
            buf(tasks, chips, 2, piece, width), buf(tasks, chips, piece, width),
            buf(chips, *chunk), buf(chips, *chunk), buf(*chunk), buf(*chunk),
            buf(tasks, piece, width), buf(tasks, piece, width), buf(2, chips, *chunk),
        ] + pair(tasks) + pair(tasks) + pair(chips) * 3
        + [pltpu.VMEM((depth, width), f32), pltpu.VMEM((rows, width), f32),
           buf(high, 128), buf(high, 128), DMA((4,)), DMA((4,)), DMA((4,))]
        + pair(chips) * 2
        + pair(tasks) * 5 + pair(chips) * 2 + [DMA((4,))] + pair(tasks) + pair(chips),
        compiler_params=params(2),
        name="joint",
    )(delta, sketch)


def local(delta, sketch, base):
    tasks = lax.axis_size("task")
    chips = lax.axis_size("row") // 2
    delta_rows, task_sketch = delta[0], sketch[0]
    width = task_sketch.shape[1]
    coefs, stack = joint(delta_rows, task_sketch.T, chips, tasks)
    coefs = coefs.reshape(tasks, -1, width)
    update = lax.dot_general(
        stack, coefs, (((0, 2), (0, 2)), ((), ())), preferred_element_type=f32
    )
    return (base.astype(f32) + update).astype(bf16)


def solution(mesh):
    return jax.shard_map(
        local,
        mesh=mesh,
        in_specs=(P("task", "row", None), P("task", None, None), P("row", "task")),
        out_specs=P("row", "task"),
        check_vma=False,
    )
```
